256 devices in a mesh: frames: 32 (over z_lo, y, core), feat: 8 (over z_hi, x).
Axes of the slice: x: 4, y: 4, z: 8 (z_hi: 2, z_lo: 4; z = z_hi * 4 + z_lo), core: 2. Of those that a mesh axis runs over, the one named last changes fastest.
Arguments:
- frames_data: bfloat16 [32768, 8192], P('frames', 'feat')
- starts: int32 [64], replicated, may hold values from 0 to 32511, as said below
- lags: int32 [64], replicated, may hold values from 1 to 10, as said below
Outputs:
- panel_rows: float32 [8, 1024, 512], P('feat', 'frames')
- whitened_cross: float32 [8, 1024, 512], P('feat', 'frames')
- whitened_tau: float32 [512, 512], P('frames')
The draws below stay inside these ranges and needn't reach their ends.
Inputs may be any that keep to these rules, and one draw needn't show every extreme that they name: starts rise strictly, starts[0] = 0; trajectory k holds frames starts[k] to starts[k+1] - 1, the last one runs to the end. `lags`: some trajectory has lag 10.
All inputs are finite; a program needn't handle non-finite values.
Results may differ from the reference program's by a relative error of at most 0.0003.
Values may be sent and summed in bfloat16 or wider, within the bound.
No kernel may reach another device: no remote copies, remote signals or barrier semaphores. Data moves between devices by JAX's collectives and lax.ppermute only.
A program may use at most 64 MiB of HBM per device.

```python
import jax
import jax.numpy as jnp
from jax import lax

F = 8192
P_SIZE = 512
LAGMAX = 10
FRAMES = 32768
FBLK = 1024
NTRAJ = 64


def draw_frames_data(key, part):
    key = jax.random.fold_in(key, 11)
    k_noise, k_slow, k_amp = jax.random.split(key, 3)
    noise = jax.random.normal(k_noise, (FRAMES, F), jnp.float32)
    slow = jax.random.normal(k_slow, (FRAMES // 16, F), jnp.float32)
    amplitude = jnp.exp(jax.random.uniform(k_amp, (1, F), jnp.float32, -1.2, 1.1))
    values = noise + jnp.repeat(slow, 16, axis=0) * amplitude
    return values.astype(jnp.bfloat16)


def draw_starts(key, part):
    key = jax.random.fold_in(key, 12)
    spacing = FRAMES // NTRAJ
    jitter = jax.random.randint(key, (NTRAJ,), 0, spacing // 2)
    jitter = jitter.at[NTRAJ - 1].set(spacing // 2 - 1)
    base = jnp.arange(NTRAJ, dtype=jnp.int32) * spacing + jitter
    return base.at[0].set(0).astype(jnp.int32)


def draw_lags(key, part):
    key = jax.random.fold_in(key, 13)
    k_val, k_pos = jax.random.split(key)
    values = jax.random.randint(k_val, (NTRAJ,), 1, LAGMAX + 1)
    where = jax.random.randint(k_pos, (), 0, NTRAJ)
    return values.at[where].set(LAGMAX).astype(jnp.int32)


def setup_inputs(seed: int = 0) -> dict:
    arg_keys = jax.random.split(jax.random.key(seed), 4)
    frames_data = draw_frames_data(jax.random.fold_in(arg_keys[3], 71), 0)
    starts = draw_starts(jax.random.fold_in(arg_keys[3], 71), 0)
    lags = draw_lags(jax.random.fold_in(arg_keys[3], 71), 0)
    return dict(frames_data=frames_data, starts=starts, lags=lags)


def trajectory_of(times, starts):
    return jnp.sum((times[:, None] >= starts[None, :]).astype(jnp.int32), axis=1) - 1

def reference(frames_data, starts, lags):
    total = frames_data.shape[0]
    times = jnp.arange(total, dtype=jnp.int32)
    owner = trajectory_of(times, starts)
    lag_of = jnp.take(lags, owner)
    nxt = times + lag_of
    inside = jnp.minimum(nxt, total - 1).astype(jnp.int32)
    valid = (nxt < total) & (trajectory_of(inside, starts) == owner)
    ends = jnp.concatenate([starts[1:], jnp.array([total], dtype=jnp.int32)])
    count = jnp.sum(jnp.maximum(ends - starts - lags, 0)).astype(jnp.float32)
    weight = valid.astype(jnp.bfloat16)[:, None]
    lagged = jnp.take(frames_data, inside, axis=0)
    left = jnp.concatenate([frames_data * weight, lagged * weight], axis=0)
    right_zero = jnp.concatenate([frames_data[:, :P_SIZE], lagged[:, :P_SIZE]], axis=0)
    right_tau = jnp.concatenate([lagged[:, :P_SIZE], frames_data[:, :P_SIZE]], axis=0)
    dims = (((0,), (0,)), ((), ()))
    c_zero = lax.dot_general(left.astype(jnp.float32), right_zero.astype(jnp.float32), dims, preferred_element_type=jnp.float32) * (0.5 / count)
    c_tau = lax.dot_general(left.astype(jnp.float32), right_tau.astype(jnp.float32), dims, preferred_element_type=jnp.float32) * (0.5 / count)
    lower = jnp.linalg.cholesky(c_zero[:P_SIZE])
    panel = jax.scipy.linalg.solve_triangular(lower, c_zero.T, lower=True).T
    cross = jax.scipy.linalg.solve_triangular(lower, c_tau.T, lower=True).T
    tau_white = jax.scipy.linalg.solve_triangular(lower, cross[:P_SIZE], lower=True)
    return (panel.reshape(-1, FBLK, P_SIZE), cross.reshape(-1, FBLK, P_SIZE), tau_white)
```

```python
import jax
import jax.numpy as jnp
from jax import lax
from jax.experimental import pallas as pl
from jax.experimental.pallas import tpu as pltpu
from jax.sharding import Mesh
from jax.sharding import PartitionSpec as P

P_SIZE = 512
RIM = 16
NB = 128
HI = lax.Precision.HIGHEST
F32 = jnp.float32
BF16 = jnp.bfloat16
AXES = ("z", "y", "c", "w", "x")
SIZES = (4, 4, 2, 2, 4)
CHUNK = 272
FIRST = CHUNK - 2 * RIM
STEP0 = 1024 - 3 * CHUNK


def coords():
    for z in range(4):
        for y in range(4):
            for c in range(2):
                for w in range(2):
                    for x in range(4):
                        yield (z, y, c, w, x)


def flat(p):
    i = 0
    for v, n in zip(p, SIZES):
        i = i * n + v
    return i


def move(value, target):
    pairs = []
    for p in coords():
        q = target(*p)
        if q is not None:
            pairs.append((flat(p), flat(q)))
    return lax.ppermute(value, AXES, pairs)


def call(kernel, outs, args, name, smem=True, scratch=(), flops=0):
    specs = [pl.BlockSpec(memory_space=pltpu.VMEM)] * len(args)
    if smem:
        specs[0] = pl.BlockSpec(memory_space=pltpu.SMEM)
    return pl.pallas_call(
        kernel,
        out_shape=outs,
        in_specs=specs,
        out_specs=[pl.BlockSpec(memory_space=pltpu.VMEM)] * len(outs),
        scratch_shapes=list(scratch),
        compiler_params=pltpu.CompilerParams(vmem_limit_bytes=48 * 2**20),
        cost_estimate=pl.CostEstimate(flops=flops, bytes_accessed=2**20, transcendentals=0),
        name=name,
    )(*args)


def mm(a, b, precision=None):
    return lax.dot_general(
        a, b, (((0,), (0,)), ((), ())), precision=precision, preferred_element_type=F32
    )


def mn(a, b):
    return lax.dot_general(
        a, b, (((1,), (0,)), ((), ())), precision=HI, preferred_element_type=F32
    )


def mt(a, b):
    return lax.dot_general(
        a, b, (((1,), (1,)), ((), ())), precision=HI, preferred_element_type=F32
    )


def frame_info(first, rows, table):
    starts, ends, lags = (table[i : i + 1, :].astype(F32) for i in range(3))
    t = (first + lax.broadcasted_iota(jnp.int32, (rows, 1), 0)).astype(F32)
    here = (starts <= t) & (t < ends)
    pick = lambda v: jnp.sum(jnp.where(here, v, 0.0), axis=1, keepdims=True)
    lag = pick(lags)
    ahead = jnp.where(t + lag < pick(ends), 1.0, 0.0)
    behind = jnp.where(t - lag >= pick(starts), 1.0, 0.0)
    return lag, ahead, behind


def pair_count(table):
    starts, ends, lags = (table[i : i + 1, :].astype(F32) for i in range(3))
    return jnp.sum(jnp.maximum(ends - starts - lags, 0.0), axis=1, keepdims=True)


def shifted(window, lag, ahead, behind):
    rows, width = lag.shape[0], window.shape[0]
    off = (
        lax.broadcasted_iota(jnp.int32, (rows, width), 1)
        - lax.broadcasted_iota(jnp.int32, (rows, width), 0)
        - RIM
    ).astype(F32)
    later = jnp.where((off == lag) & (ahead > 0.0), 1.0, 0.0).astype(BF16)
    earlier = jnp.where((off == -lag) & (behind > 0.0), 1.0, 0.0).astype(BF16)
    dims = (((1,), (0,)), ((), ()))
    zp = lax.dot_general(later, window, dims, preferred_element_type=F32)
    zm = lax.dot_general(earlier, window, dims, preferred_element_type=F32)
    return zp.astype(BF16), zm.astype(BF16)


def store_diag(d, pos, mine, theirs):
    z, y, c = pos[1], pos[2], pos[3]
    for yy in range(4):
        for zz in range(4):
            at = lax.rem(yy - y + 4, 4) * 64 + lax.rem(zz - z + 4, 4) * 16
            at = pl.multiple_of(at, 16)
            o = yy * 64 + zz * 16
            a, b = d[o : o + 16, :], d[256 + o : 256 + o + 16, :]
            mine[pl.ds(at, 16), :] = jnp.where(c == 0, a, b)
            theirs[pl.ds(at, 16), :] = jnp.where(c == 0, b, a)


def diag_zero_kernel(pos, table, xp, mine, theirs):
    lag, ahead, behind = frame_info(pos[0], xp.shape[0], table)
    v = xp[...]
    weighted = v * (0.5 * (ahead + behind)).astype(BF16)
    store_diag(mm(v, weighted) / pair_count(table), pos, mine, theirs)


def diag_tau_kernel(pos, table, xp, before, after, mine, theirs, ext, right):
    rows = xp.shape[0]
    ext[0:RIM, :] = before[...]
    ext[RIM : RIM + rows, :] = xp[...]
    ext[RIM + rows :, :] = after[...]
    for b in range(0, rows, 256):
        lag, ahead, behind = frame_info(pos[0] + b, 256, table)
        zp, zm = shifted(ext[b : b + 256 + 2 * RIM, :], lag, ahead, behind)
        right[b : b + 256, :P_SIZE] = zp
        right[b : b + 256, P_SIZE:] = zm
    v = xp[...]
    d = mm(v, right[:, :P_SIZE]) + mm(v, right[:, P_SIZE:])
    store_diag(d * (0.5 / pair_count(table)), pos, mine, theirs)


def cov_kernel(pos, table, x, g0, g1, g2, g3, m0, t0, m1, t1, ext, right):
    rows = x.shape[0]
    z, y, c, col = pos[1], pos[2], pos[3], pos[4]
    for k, g in enumerate((g0, g1, g2, g3)):
        q = lax.rem(col - k + 4, 4)

        @pl.when(q == 0)
        def _():
            ext[0:RIM, :] = g[0:RIM, :]
            ext[RIM + rows :, :] = g[RIM : 2 * RIM, :]
            ext[RIM : RIM + FIRST, :] = g[2 * RIM :, :]

        @pl.when(q != 0)
        def _():
            at = pl.multiple_of(RIM + STEP0 + CHUNK * (q - 1), 16)
            ext[pl.ds(at, CHUNK), :] = g[...]

    for b in range(0, rows, 256):
        lag, ahead, behind = frame_info(pos[0] + b, 256, table)
        zp, zm = shifted(ext[b : b + 256 + 2 * RIM, :], lag, ahead, behind)
        own = ext[b + RIM : b + RIM + 256, :]
        right[b : b + 256, :P_SIZE] = own * (0.5 * (ahead + behind)).astype(BF16)
        right[b : b + 256, P_SIZE : 2 * P_SIZE] = zp
        right[b : b + 256, 2 * P_SIZE :] = zm
    scale = 1.0 / pair_count(table)
    for zz in range(4):
        left = x[:, 256 * zz : 256 * zz + 256]
        d0 = mm(left, right[:, :P_SIZE]) * scale
        d1 = mm(left, right[:, P_SIZE : 2 * P_SIZE]) + mm(left, right[:, 2 * P_SIZE :])
        d1 = d1 * (0.5 * scale)
        at = pl.multiple_of(lax.rem(zz - z + 4, 4) * 32, 32)
        for yy in range(4):
            ky = lax.rem(yy - y + 4, 4)
            for d, mine, theirs in ((d0, m0, t0), (d1, m1, t1)):
                a, b = d[64 * yy : 64 * yy + 32, :], d[64 * yy + 32 : 64 * yy + 64, :]
                mine[ky, pl.ds(at, 32), :] = jnp.where(c == 0, a, b)
                theirs[ky, pl.ds(at, 32), :] = jnp.where(c == 0, b, a)


def factor(s):
    n = NB
    groups = [s[8 * i : 8 * i + 8, :] for i in range(n // 8)]
    sub = lax.broadcasted_iota(jnp.int32, (8, n), 0)
    lane = lax.broadcasted_iota(jnp.int32, (8, n), 1)
    for j in range(n // 8):
        r0 = 8 * j
        look = j + 1 < n // 8
        block = (lane >= r0) & (lane < r0 + 8)
        rows = groups[j]
        cols = [jnp.broadcast_to(rows[:, r0 + r : r0 + r + 1], (8, n)) for r in range(8)]
        rows = jnp.where(block, jnp.where(lane - r0 == sub, 1.0, 0.0), rows)
        if look:
            more = groups[j + 1]
            below = [jnp.broadcast_to(more[:, r0 + r : r0 + r + 1], (8, n)) for r in range(8)]
            more = jnp.where(block, 0.0, more)
        for r in range(8):
            rs = lax.rsqrt(cols[r][r : r + 1, :])
            l = cols[r] * rs
            lm = jnp.where(sub > r, l, 0.0)
            row = rows[r : r + 1, :] * rs
            rows = jnp.where(sub == r, row, rows - lm * row)
            if look:
                lq = below[r] * rs
                more = more - lq * row
            for s_ in range(r + 1, 8):
                at = l[s_ : s_ + 1, :]
                cols[s_] = cols[s_] - lm * at
                if look:
                    below[s_] = below[s_] - lq * at
        groups[j] = rows
        if look:
            groups[j + 1] = more
        if j + 2 < n // 8:
            m = n - r0 - 16
            rest = jnp.concatenate(groups[j + 2 :], axis=0)
            lanes = lax.broadcasted_iota(jnp.int32, (m, n), 1)
            rest = jnp.where((lanes >= r0) & (lanes < r0 + 8), 0.0, rest)
            rest = rest - mm(rows, rows, HI)[r0 + 16 :, :]
            for i in range(j + 2, n // 8):
                groups[i] = rest[8 * (i - j - 2) : 8 * (i - j - 1), :]
    return lower_part(jnp.concatenate(groups, axis=0))


def lower_part(v):
    r = lax.broadcasted_iota(jnp.int32, v.shape, 0)
    c = lax.broadcasted_iota(jnp.int32, v.shape, 1)
    return jnp.where(r >= c, v, 0.0)


def place(pos, pieces, out):
    z, y, c = pos[1], pos[2], pos[3]
    for kc in range(2):
        cc = lax.rem(c + kc, 2)
        for ky in range(4):
            yy = lax.rem(y - ky + 4, 4)
            for kz in range(4):
                zz = lax.rem(z - kz + 4, 4)
                at = pl.multiple_of(cc * 256 + yy * 64 + zz * 16, 16)
                out[pl.ds(at, 16), :] = pieces[kc][ky][16 * kz : 16 * kz + 16, :]


def inverse_kernel(pos, a0, a1, a2, a3, b0, b1, b2, b3, out, w):
    place(pos, ((a0, a1, a2, a3), (b0, b1, b2, b3)), w)
    size = P_SIZE
    r = lax.broadcasted_iota(jnp.int32, (NB, NB), 0)
    c = lax.broadcasted_iota(jnp.int32, (NB, NB), 1)
    for o in range(0, size, NB):
        t = factor(w[o : o + NB, o : o + NB])
        w[o : o + NB, o : o + NB] = jnp.where(r == c, 1.0, 0.0)
        new = mn(t, w[o : o + NB, :])
        w[o : o + NB, :] = new
        if o + NB < size:
            w[o + NB :, o : o + NB] = jnp.zeros((size - o - NB, NB), F32)
            w[o + NB :, :] = w[o + NB :, :] - mm(new[:, o + NB :], new, HI)
    out[...] = lower_part(w[...])


def whiten_kernel(pos, inv, p0, p1, p2, p3, q0, q1, q2, q3, a0, a1, a2, a3, b0, b1, b2, b3,
                  panel, cross, tau, ct, left):
    place(pos, ((a0, a1, a2, a3), (b0, b1, b2, b3)), ct)
    m = inv[...]
    left[0:32, :] = (p0[...] + p1[...]) + (p2[...] + p3[...])
    left[32:64, :] = (q0[...] + q1[...]) + (q2[...] + q3[...])
    at = pl.multiple_of(16 * (pos[1] * 8 + pos[2] * 2 + pos[3]), 16)
    left[64:80, :] = mn(inv[pl.ds(at, 16), :], ct[...])
    res = mt(left[...], m)
    panel[0] = res[0:32, :]
    cross[0] = res[32:64, :]
    tau[...] = res[64:80, :]


def swap_core(v, only=None):
    return move(v, lambda z, y, c, w, x: (z, y, 1 - c, w, x) if only is None or (w, x) == only else None)


def along_y(v, k, only=None):
    return move(v, lambda z, y, c, w, x: (z, (y + k) % 4, c, w, x) if only is None or (w, x) == only else None)


def along_z(v, k, only=None):
    return move(v, lambda z, y, c, w, x: ((z + k) % 4, y, c, w, x) if only is None or (w, x) == only else None)


def diag_sum(mine, theirs):
    src = (0, 0)
    s = [mine[64 * k : 64 * k + 64] for k in range(4)]
    got = swap_core(theirs, src)
    s = [s[k] + got[64 * k : 64 * k + 64] for k in range(4)]
    y = [along_y(s[k], k, src) for k in (1, 2, 3)]
    t = s[0] + y[0] + y[1] + y[2]
    zs = [along_z(t[16 * k : 16 * k + 16], k, src) for k in (1, 2, 3)]
    own = t[0:16] + zs[0] + zs[1] + zs[2]
    w_at, x_at = lax.axis_index("w"), lax.axis_index("x")
    over = move(own, lambda z, y, c, w, x: (z, y, c, 1, 0) if (w, x) == (0, 0) else None)
    own = jnp.where(w_at == 0, own, over)
    far = [
        move(own, lambda z, y, c, w, x: (z, y, c, w, k) if x == 0 else None) for k in (1, 2, 3)
    ]
    own = jnp.where(x_at == 0, own, far[0] + far[1] + far[2])
    g = jnp.concatenate([own] + [along_z(own, k) for k in (1, 2, 3)], axis=0)
    a = [g] + [along_y(g, k) for k in (1, 2, 3)]
    b = [swap_core(v) for v in a]
    return a + b


def body(frames_data, starts, lags):
    tok, width = frames_data.shape
    z, y, c, w, x = (lax.axis_index(a) for a in AXES)
    slab = z * 8 + y * 2 + c
    total = tok * 32
    ends = jnp.concatenate([starts[1:], jnp.array([total], dtype=jnp.int32)])
    table = jnp.stack([starts, ends, lags])
    pos = jnp.stack([slab * tok, z, y, c, x]).astype(jnp.int32)
    panel = frames_data[:, :P_SIZE]

    half = jax.ShapeDtypeStruct((256, P_SIZE), F32)
    dz = call(diag_zero_kernel, [half, half], (pos, table, panel), "diag_zero", flops=10**9)
    zero_pieces = diag_sum(*dz)

    def step(by):
        def target(z, y, c, w, x):
            i = z * 8 + y * 2 + c + by
            return (i // 8, i // 2 % 4, i % 2, 0, 0) if (w, x) == (0, 0) and 0 <= i < 32 else None
        return target

    after = move(panel[:RIM], step(-1))
    before = move(panel[tok - RIM :], step(1))

    chunks = [panel[STEP0 + CHUNK * (k - 1) : STEP0 + CHUNK * k] for k in (1, 2, 3)]
    sent = [
        move(chunks[k - 1], lambda z, y, c, w, x: (z, y, c, w, k) if (w, x) == (0, 0) else None)
        for k in (1, 2, 3)
    ]
    first = jnp.concatenate([before, after, panel[:FIRST]], axis=0)
    hold = jnp.where(x == 0, first, sent[0] + sent[1] + sent[2])
    over = move(hold, lambda z, y, c, w, x: (z, y, c, 1, x) if w == 0 else None)
    hold = jnp.where(w == 0, hold, over)
    gathered = [hold] + [
        move(hold, lambda z, y, c, w, x: (z, y, c, w, (x + k) % 4)) for k in (1, 2, 3)
    ]

    dt = call(
        diag_tau_kernel, [half, half], (pos, table, panel, before, after), "diag_tau",
        scratch=[pltpu.VMEM((tok + 2 * RIM, P_SIZE), BF16), pltpu.VMEM((tok, 2 * P_SIZE), BF16)],
        flops=2 * 10**9,
    )
    tau_pieces = diag_sum(*dt)

    quarter = jax.ShapeDtypeStruct((4, 128, P_SIZE), F32)
    m0, t0, m1, t1 = call(
        cov_kernel, [quarter] * 4, (pos, table, frames_data, *gathered), "covariance",
        scratch=[pltpu.VMEM((tok + 2 * RIM, P_SIZE), BF16), pltpu.VMEM((tok, 3 * P_SIZE), BF16)],
        flops=5 * 10**9,
    )
    rows = []
    for mine, theirs in ((m0, t0), (m1, t1)):
        got = swap_core(theirs)
        s = [mine[k] + got[k] for k in range(4)]
        ys = [along_y(s[k], k) for k in (1, 2, 3)]
        t = s[0] + ys[0] + ys[1] + ys[2]
        rows += [t[0:32]] + [along_z(t[32 * k : 32 * k + 32], k) for k in (1, 2, 3)]

    (inv,) = call(
        inverse_kernel, [jax.ShapeDtypeStruct((P_SIZE, P_SIZE), F32)], (pos, *zero_pieces), "inverse",
        scratch=[pltpu.VMEM((P_SIZE, P_SIZE), F32)], flops=20 * 10**9,
    )
    own = jax.ShapeDtypeStruct((1, 32, P_SIZE), F32)
    return tuple(
        call(
            whiten_kernel, [own, own, jax.ShapeDtypeStruct((16, P_SIZE), F32)],
            (pos, inv, *rows, *tau_pieces), "whiten",
            scratch=[pltpu.VMEM((P_SIZE, P_SIZE), F32), pltpu.VMEM((80, P_SIZE), F32)], flops=2 * 10**9,
        )
    )


def solution(mesh):
    split = Mesh(mesh.devices.reshape(SIZES), AXES)
    frames, feat = ("z", "y", "c"), ("w", "x")
    return jax.shard_map(
        body,
        mesh=split,
        in_specs=(P(frames, feat), P(), P()),
        out_specs=(P(feat, frames, None), P(feat, frames, None), P(frames, None)),
        check_vma=False,
    )
```

```python
import jax
import jax.numpy as jnp
from jax import lax
from jax.experimental import pallas as pl
from jax.experimental.pallas import tpu as pltpu
from jax.sharding import Mesh
from jax.sharding import PartitionSpec as P

P_SIZE = 512
RIM = 16
NB = 128
HI = lax.Precision.HIGHEST
F32 = jnp.float32
BF16 = jnp.bfloat16
AXES = ("z", "y", "c", "w", "x")
SIZES = (4, 4, 2, 2, 4)
CHUNK = 272
FIRST = CHUNK - 2 * RIM
STEP0 = 1024 - 3 * CHUNK


def coords():
    for z in range(4):
        for y in range(4):
            for c in range(2):
                for w in range(2):
                    for x in range(4):
                        yield (z, y, c, w, x)


def flat(p):
    i = 0
    for v, n in zip(p, SIZES):
        i = i * n + v
    return i


def move(value, target):
    pairs = []
    for p in coords():
        q = target(*p)
        if q is not None:
            pairs.append((flat(p), flat(q)))
    return lax.ppermute(value, AXES, pairs)


def call(kernel, outs, args, name, smem=True, scratch=(), flops=0):
    specs = [pl.BlockSpec(memory_space=pltpu.VMEM)] * len(args)
    if smem:
        specs[0] = pl.BlockSpec(memory_space=pltpu.SMEM)
    return pl.pallas_call(
        kernel,
        out_shape=outs,
        in_specs=specs,
        out_specs=[pl.BlockSpec(memory_space=pltpu.VMEM)] * len(outs),
        scratch_shapes=list(scratch),
        compiler_params=pltpu.CompilerParams(vmem_limit_bytes=48 * 2**20),
        cost_estimate=pl.CostEstimate(flops=flops, bytes_accessed=2**20, transcendentals=0),
        name=name,
    )(*args)


def mm(a, b, precision=None):
    return lax.dot_general(
        a, b, (((0,), (0,)), ((), ())), precision=precision, preferred_element_type=F32
    )


def mn(a, b):
    return lax.dot_general(
        a, b, (((1,), (0,)), ((), ())), precision=HI, preferred_element_type=F32
    )


def mt(a, b):
    return lax.dot_general(
        a, b, (((1,), (1,)), ((), ())), precision=HI, preferred_element_type=F32
    )


def frame_info(first, rows, table):
    starts, ends, lags = (table[i : i + 1, :].astype(F32) for i in range(3))
    t = (first + lax.broadcasted_iota(jnp.int32, (rows, 1), 0)).astype(F32)
    here = (starts <= t) & (t < ends)
    pick = lambda v: jnp.sum(jnp.where(here, v, 0.0), axis=1, keepdims=True)
    lag = pick(lags)
    ahead = jnp.where(t + lag < pick(ends), 1.0, 0.0)
    behind = jnp.where(t - lag >= pick(starts), 1.0, 0.0)
    return lag, ahead, behind


def pair_count(table):
    starts, ends, lags = (table[i : i + 1, :].astype(F32) for i in range(3))
    return jnp.sum(jnp.maximum(ends - starts - lags, 0.0), axis=1, keepdims=True)


def shifted(window, lag, ahead, behind):
    rows, width = lag.shape[0], window.shape[0]
    off = (
        lax.broadcasted_iota(jnp.int32, (rows, width), 1)
        - lax.broadcasted_iota(jnp.int32, (rows, width), 0)
        - RIM
    ).astype(F32)
    later = jnp.where((off == lag) & (ahead > 0.0), 1.0, 0.0).astype(BF16)
    earlier = jnp.where((off == -lag) & (behind > 0.0), 1.0, 0.0).astype(BF16)
    dims = (((1,), (0,)), ((), ()))
    zp = lax.dot_general(later, window, dims, preferred_element_type=F32)
    zm = lax.dot_general(earlier, window, dims, preferred_element_type=F32)
    return zp.astype(BF16), zm.astype(BF16)


def diag_kernel(pos, table, xp, before, after, mine, theirs, ext, right):
    rows = xp.shape[0]
    ext[0:RIM, :] = before[...]
    ext[RIM : RIM + rows, :] = xp[...]
    ext[RIM + rows :, :] = after[...]
    fill_right(pos, table, ext, right, rows, P_SIZE)
    scale = 1.0 / pair_count(table)
    c = pos[1]
    v = xp[...]
    for half in range(2):
        cols = slice(256 * half, 256 * half + 256)
        d0 = mm(v[:, cols], right[:, :P_SIZE]) * scale
        d1 = mm(v[:, cols], right[:, P_SIZE : 2 * P_SIZE]) + mm(v[:, cols], right[:, 2 * P_SIZE :])
        d1 = d1 * (0.5 * scale)
        r = lax.broadcasted_iota(jnp.int32, d0.shape, 0) + 256 * half
        l = lax.broadcasted_iota(jnp.int32, d0.shape, 1)
        packed = jnp.where(r >= l, d0, d1)
        diag = jnp.sum(jnp.where(r == l, d1, 0.0), axis=1, keepdims=True)
        diag = jnp.broadcast_to(diag, (256, NB))

        @pl.when(c == half)
        def _():
            mine[:, :P_SIZE] = packed
            mine[:, P_SIZE:] = diag

        @pl.when(c != half)
        def _():
            theirs[:, :P_SIZE] = packed
            theirs[:, P_SIZE:] = diag


def fill_right(pos, table, ext, right, rows, n):
    for b in range(0, rows, 256):
        lag, ahead, behind = frame_info(pos[0] + b, 256, table)
        zp, zm = shifted(ext[b : b + 256 + 2 * RIM, :], lag, ahead, behind)
        own = ext[b + RIM : b + RIM + 256, :]
        right[b : b + 256, :n] = own * (0.5 * (ahead + behind)).astype(BF16)
        right[b : b + 256, n : 2 * n] = zp
        right[b : b + 256, 2 * n :] = zm


def cov_kernel(pos, table, x, g, mine, theirs, ext, right):
    rows, n = x.shape[0], g.shape[2]
    c = pos[1]
    ext[0:RIM, :] = g[0, 0:RIM, :]
    ext[RIM + rows :, :] = g[0, RIM : 2 * RIM, :]
    ext[RIM : RIM + FIRST, :] = g[0, 2 * RIM :, :]
    for q in range(1, 4):
        at = RIM + STEP0 + CHUNK * (q - 1)
        ext[at : at + CHUNK, :] = g[q]
    fill_right(pos, table, ext, right, rows, n)
    scale = 1.0 / pair_count(table)
    for zz in range(4):
        left = x[:, 256 * zz : 256 * zz + 256]
        d0 = mm(left, right[:, :n]) * scale
        d1 = mm(left, right[:, n : 2 * n]) + mm(left, right[:, 2 * n :])
        d1 = d1 * (0.5 * scale)
        for yy in range(4):
            for d, o in ((d0, 0), (d1, n)):
                a, b = d[64 * yy : 64 * yy + 32, :], d[64 * yy + 32 : 64 * yy + 64, :]
                mine[yy, 32 * zz : 32 * zz + 32, o : o + n] = jnp.where(c == 0, a, b)
                theirs[yy, 32 * zz : 32 * zz + 32, o : o + n] = jnp.where(c == 0, b, a)


def factor(s):
    n = NB
    groups = [s[8 * i : 8 * i + 8, :] for i in range(n // 8)]
    sub = lax.broadcasted_iota(jnp.int32, (8, n), 0)
    lane = lax.broadcasted_iota(jnp.int32, (8, n), 1)
    for j in range(n // 8):
        r0 = 8 * j
        look = j + 1 < n // 8
        block = (lane >= r0) & (lane < r0 + 8)
        rows = groups[j]
        cols = [jnp.broadcast_to(rows[:, r0 + r : r0 + r + 1], (8, n)) for r in range(8)]
        rows = jnp.where(block, jnp.where(lane - r0 == sub, 1.0, 0.0), rows)
        if look:
            more = groups[j + 1]
            below = [jnp.broadcast_to(more[:, r0 + r : r0 + r + 1], (8, n)) for r in range(8)]
            more = jnp.where(block, 0.0, more)
        for r in range(8):
            rs = lax.rsqrt(cols[r][r : r + 1, :])
            l = cols[r] * rs
            lm = jnp.where(sub > r, l, 0.0)
            row = rows[r : r + 1, :] * rs
            rows = jnp.where(sub == r, row, rows - lm * row)
            if look:
                lq = below[r] * rs
                more = more - lq * row
            for s_ in range(r + 1, 8):
                at = l[s_ : s_ + 1, :]
                cols[s_] = cols[s_] - lm * at
                if look:
                    below[s_] = below[s_] - lq * at
        groups[j] = rows
        if look:
            groups[j + 1] = more
        if j + 2 < n // 8:
            m = n - r0 - 16
            rest = jnp.concatenate(groups[j + 2 :], axis=0)
            lanes = lax.broadcasted_iota(jnp.int32, (m, n), 1)
            rest = jnp.where((lanes >= r0) & (lanes < r0 + 8), 0.0, rest)
            rest = rest - mm(rows, rows, HI)[r0 + 16 :, :]
            for i in range(j + 2, n // 8):
                groups[i] = rest[8 * (i - j - 2) : 8 * (i - j - 1), :]
    return lower_part(jnp.concatenate(groups, axis=0))


def lower_part(v):
    r = lax.broadcasted_iota(jnp.int32, v.shape, 0)
    c = lax.broadcasted_iota(jnp.int32, v.shape, 1)
    return jnp.where(r >= c, v, 0.0)


def inverse_kernel(pos, own, other, out, up, w):
    c = pos[1]
    r = lax.broadcasted_iota(jnp.int32, (P_SIZE // 2, P_SIZE), 0)
    l = lax.broadcasted_iota(jnp.int32, (P_SIZE // 2, P_SIZE), 1)
    for half in range(2):
        at = slice(256 * half, 256 * half + 256)
        v = jnp.where(c == half, own[:, :P_SIZE], other[:, :P_SIZE])
        d = jnp.where(c == half, own[:, P_SIZE : P_SIZE + 1], other[:, P_SIZE : P_SIZE + 1])
        w[at, :] = v
        up[at, :] = jnp.where(l > r + 256 * half, v, jnp.where(l == r + 256 * half, d, 0.0))
    size = P_SIZE
    r = lax.broadcasted_iota(jnp.int32, (NB, NB), 0)
    l = lax.broadcasted_iota(jnp.int32, (NB, NB), 1)
    for o in range(0, size, NB):
        s = jnp.where(r >= l, w[o : o + NB, o : o + NB], 0.0)
        w[o : o + NB, o : o + NB] = s + jnp.where(r < l, s.T, 0.0)
    for o in range(0, size, NB):
        e = o + NB
        t = factor(w[o:e, o:e])
        w[o:e, o:e] = t
        if o:
            w[o:e, :o] = mn(t, w[o:e, :o])
        if e < size:
            low = mt(w[e:, o:e], t)
            w[e:, o:e] = -mn(low, t)
            if o:
                w[e:, :o] = w[e:, :o] - mn(low, w[o:e, :o])
            w[e:, e:] = w[e:, e:] - mt(low, low)
    out[...] = lower_part(w[...])


def whiten_kernel(pos, inv, up, h0, h1, panel, cross, tau, left):
    m = inv[...]
    n = P_SIZE // 2
    for i, h in enumerate((h0, h1)):
        s = (h[0] + h[1]) + (h[2] + h[3])
        left[0:32, i * n : (i + 1) * n] = s[:, :n]
        left[32:64, i * n : (i + 1) * n] = s[:, n:]
    rows = inv[pl.ds(pl.multiple_of(pos[2], 16), 16), :]
    u = up[...]
    r = lax.broadcasted_iota(jnp.int32, u.shape, 0)
    l = lax.broadcasted_iota(jnp.int32, u.shape, 1)
    left[64:80, :] = mn(rows, u) + mt(rows, jnp.where(l > r, u, 0.0))
    res = mt(left[...], m)
    panel[0] = res[0:32, :]
    cross[0] = res[32:64, :]
    tau[...] = res[64:80, :]


def swap_core(v, only=None):
    return move(v, lambda z, y, c, w, x: (z, y, 1 - c, w, x) if only is None or (w, x) == only else None)


def exchange(v, axes):
    return lax.all_to_all(v, axes, 0, 0, tiled=True)


def spread(v, axes, n):
    return exchange(jnp.broadcast_to(v[None], (n, *v.shape)), axes)


def diag_sum(mine, theirs, w):
    half = (mine + swap_core(theirs, (0, 0))).reshape(16, 16, mine.shape[1])
    own = jnp.sum(exchange(half, ("z", "y")), axis=0)
    over = move(own, lambda z, y, c, w, x: (z, y, c, 1, 0) if (w, x) == (0, 0) else None)
    own = spread(jnp.where(w == 0, own, over), "x", 4)[0]
    half = spread(own, ("z", "y"), 16).reshape(mine.shape)
    return half, swap_core(half)


def body(frames_data, starts, lags):
    tok, width = frames_data.shape
    z, y, c, w, x = (lax.axis_index(a) for a in AXES)
    slab = z * 8 + y * 2 + c
    total = tok * 32
    ends = jnp.concatenate([starts[1:], jnp.array([total], dtype=jnp.int32)])
    table = jnp.stack([starts, ends, lags])
    pos = jnp.stack([slab * tok, c, slab * 16]).astype(jnp.int32)
    panel = frames_data[:, :P_SIZE]

    def step(by):
        def target(z, y, c, w, x):
            i = z * 8 + y * 2 + c + by
            return (i // 8, i // 2 % 4, i % 2, 0, 0) if (w, x) == (0, 0) and 0 <= i < 32 else None
        return target

    after = move(panel[:RIM], step(-1))
    before = move(panel[tok - RIM :], step(1))

    packed = jax.ShapeDtypeStruct((256, P_SIZE + NB), F32)
    dz = call(
        diag_kernel, [packed, packed], (pos, table, panel, before, after), "diagonal",
        scratch=[pltpu.VMEM((tok + 2 * RIM, P_SIZE), BF16), pltpu.VMEM((tok, 3 * P_SIZE), BF16)],
        flops=3 * 10**9,
    )
    n = P_SIZE // 2
    rows = []
    for h in range(2):
        cols = slice(h * n, h * n + n)
        chunks = [frames_data[STEP0 + CHUNK * (k - 1) : STEP0 + CHUNK * k, cols] for k in (1, 2, 3)]
        sent = [
            move(chunks[k - 1], lambda z, y, c, w, x: (z, y, c, w, k) if (w, x) == (0, 0) else None)
            for k in (2, 1, 3)
        ]
        first = jnp.concatenate([before[:, cols], after[:, cols], frames_data[:FIRST, cols]], axis=0)
        hold = jnp.where(x == 0, first, sent[0] + sent[1] + sent[2])
        over = move(hold, lambda z, y, c, w, x: (z, y, c, 1, x) if w == 0 else None)
        gathered = spread(jnp.where(w == 0, hold, over), "x", 4)
        part = jax.ShapeDtypeStruct((4, 128, P_SIZE), F32)
        mine, theirs = call(
            cov_kernel, [part] * 2, (pos, table, frames_data, gathered), "covariance",
            scratch=[pltpu.VMEM((tok + 2 * RIM, n), BF16), pltpu.VMEM((tok, 3 * n), BF16)],
            flops=3 * 10**9,
        )
        s = jnp.sum(exchange(mine + swap_core(theirs), "y"), axis=0)
        rows.append(exchange(s.reshape(4, 32, P_SIZE), "z"))

    full = jax.ShapeDtypeStruct((P_SIZE, P_SIZE), F32)
    inv, up = call(
        inverse_kernel, [full, full], (pos, *diag_sum(*dz, w)), "inverse",
        scratch=[pltpu.VMEM((P_SIZE, P_SIZE), F32)], flops=20 * 10**9,
    )
    own = jax.ShapeDtypeStruct((1, 32, P_SIZE), F32)
    return tuple(
        call(
            whiten_kernel, [own, own, jax.ShapeDtypeStruct((16, P_SIZE), F32)],
            (pos, inv, up, *rows), "whiten", scratch=[pltpu.VMEM((80, P_SIZE), F32)], flops=2 * 10**9,
        )
    )


def solution(mesh):
    split = Mesh(mesh.devices.reshape(SIZES), AXES)
    frames, feat = ("z", "y", "c"), ("w", "x")
    return jax.shard_map(
        body,
        mesh=split,
        in_specs=(P(frames, feat), P(), P()),
        out_specs=(P(feat, frames, None), P(feat, frames, None), P(frames, None)),
        check_vma=False,
    )
```

```python
import functools

import jax
import jax.numpy as jnp
from jax import lax
from jax.experimental import pallas as pl
from jax.experimental.pallas import tpu as pltpu
from jax.sharding import Mesh
from jax.sharding import PartitionSpec as P

P_SIZE = 512
RIM = 16
NB = 128
HI = lax.Precision.HIGHEST
F32 = jnp.float32
BF16 = jnp.bfloat16
AXES = ("z", "y", "c", "w", "x")
SIZES = (4, 4, 2, 2, 4)
CHUNK = 272
FIRST = CHUNK - 2 * RIM
STEP0 = 1024 - 3 * CHUNK


def coords():
    for z in range(4):
        for y in range(4):
            for c in range(2):
                for w in range(2):
                    for x in range(4):
                        yield (z, y, c, w, x)


def flat(p):
    i = 0
    for v, n in zip(p, SIZES):
        i = i * n + v
    return i


def move(value, target):
    pairs = []
    for p in coords():
        q = target(*p)
        if q is not None:
            pairs.append((flat(p), flat(q)))
    return lax.ppermute(value, AXES, pairs)


def call(kernel, outs, args, name, scratch=(), flops=0, vmem=16):
    specs = [pl.BlockSpec(memory_space=pltpu.VMEM)] * len(args)
    specs[0] = pl.BlockSpec(memory_space=pltpu.SMEM)
    return pl.pallas_call(
        kernel,
        out_shape=outs,
        in_specs=specs,
        out_specs=[pl.BlockSpec(memory_space=pltpu.VMEM)] * len(outs),
        scratch_shapes=list(scratch),
        compiler_params=pltpu.CompilerParams(vmem_limit_bytes=vmem * 2**20),
        cost_estimate=pl.CostEstimate(flops=flops, bytes_accessed=2**20, transcendentals=0),
        name=name,
    )(*args)


def mm(a, b, precision=None):
    return lax.dot_general(
        a, b, (((0,), (0,)), ((), ())), precision=precision, preferred_element_type=F32
    )


def mn(a, b):
    return lax.dot_general(
        a, b, (((1,), (0,)), ((), ())), precision=HI, preferred_element_type=F32
    )


def mt(a, b):
    return lax.dot_general(
        a, b, (((1,), (1,)), ((), ())), precision=HI, preferred_element_type=F32
    )


def frame_info(first, rows, table):
    starts, ends, lags = (table[i : i + 1, :].astype(F32) for i in range(3))
    t = (first + lax.broadcasted_iota(jnp.int32, (rows, 1), 0)).astype(F32)
    here = (starts <= t) & (t < ends)
    pick = lambda v: jnp.sum(jnp.where(here, v, 0.0), axis=1, keepdims=True)
    lag = pick(lags)
    ahead = jnp.where(t + lag < pick(ends), 1.0, 0.0)
    behind = jnp.where(t - lag >= pick(starts), 1.0, 0.0)
    return lag, ahead, behind


def pair_count(table):
    starts, ends, lags = (table[i : i + 1, :].astype(F32) for i in range(3))
    return jnp.sum(jnp.maximum(ends - starts - lags, 0.0), axis=1, keepdims=True)


def shifted(window, lag, ahead, behind):
    rows, width = lag.shape[0], window.shape[0]
    off = (
        lax.broadcasted_iota(jnp.int32, (rows, width), 1)
        - lax.broadcasted_iota(jnp.int32, (rows, width), 0)
        - RIM
    ).astype(F32)
    later = jnp.where((off == lag) & (ahead > 0.0), 1.0, 0.0).astype(BF16)
    earlier = jnp.where((off == -lag) & (behind > 0.0), 1.0, 0.0).astype(BF16)
    dims = (((1,), (0,)), ((), ()))
    zp = lax.dot_general(later, window, dims, preferred_element_type=F32)
    zm = lax.dot_general(earlier, window, dims, preferred_element_type=F32)
    return zp.astype(BF16), zm.astype(BF16)


def diag_kernel(pos, table, xp, before, after, mine, theirs, ext, right):
    rows = xp.shape[0]
    ext[0:RIM, :] = before[...]
    ext[RIM : RIM + rows, :] = xp[...]
    ext[RIM + rows :, :] = after[...]
    fill_right(pos, table, ext, right, rows, P_SIZE)
    scale = 1.0 / pair_count(table)
    c = pos[1]
    v = xp[...]
    for half in range(2):
        cols = slice(256 * half, 256 * half + 256)
        d0 = mm(v[:, cols], right[:, :P_SIZE]) * scale
        d1 = mm(v[:, cols], right[:, P_SIZE : 2 * P_SIZE]) + mm(v[:, cols], right[:, 2 * P_SIZE :])
        d1 = d1 * (0.5 * scale)
        r = lax.broadcasted_iota(jnp.int32, d0.shape, 0) + 256 * half
        l = lax.broadcasted_iota(jnp.int32, d0.shape, 1)
        packed = jnp.where(r >= l, d0, d1)
        diag = jnp.sum(jnp.where(r == l, d1, 0.0), axis=1, keepdims=True)
        diag = jnp.broadcast_to(diag, (256, NB))

        @pl.when(c == half)
        def _():
            mine[:, :P_SIZE] = packed
            mine[:, P_SIZE:] = diag

        @pl.when(c != half)
        def _():
            theirs[:, :P_SIZE] = packed
            theirs[:, P_SIZE:] = diag


def fill_right(pos, table, ext, right, rows, n):
    for b in range(0, rows, 256):
        lag, ahead, behind = frame_info(pos[0] + b, 256, table)
        zp, zm = shifted(ext[b : b + 256 + 2 * RIM, :], lag, ahead, behind)
        own = ext[b + RIM : b + RIM + 256, :]
        right[b : b + 256, :n] = own * (0.5 * (ahead + behind)).astype(BF16)
        right[b : b + 256, n : 2 * n] = zp
        right[b : b + 256, 2 * n :] = zm


def cov_kernel(pos, table, x, g0, g1, g2, g3, m0, t0, m1, t1, ext, right):
    rows, n = x.shape[0], P_SIZE
    c, z, y, col = pos[1], pos[3], pos[4], pos[5]
    for k, g in enumerate((g0, g1, g2, g3)):
        q = lax.rem(col - k + 4, 4)

        @pl.when(q == 0)
        def _():
            ext[0:RIM, :] = g[0:RIM, :]
            ext[RIM + rows :, :] = g[RIM : 2 * RIM, :]
            ext[RIM : RIM + FIRST, :] = g[2 * RIM :, :]

        @pl.when(q != 0)
        def _():
            at = pl.multiple_of(RIM + STEP0 + CHUNK * (q - 1), 16)
            ext[pl.ds(at, CHUNK), :] = g[...]

    fill_right(pos, table, ext, right, rows, n)
    scale = 1.0 / pair_count(table)
    for zz in range(4):
        left = x[:, 256 * zz : 256 * zz + 256]
        d0 = mm(left, right[:, :n]) * scale
        d1 = mm(left, right[:, n : 2 * n]) + mm(left, right[:, 2 * n :])
        d1 = d1 * (0.5 * scale)
        at = pl.multiple_of(lax.rem(zz - z + 4, 4) * 32, 32)
        for yy in range(4):
            ky = lax.rem(yy - y + 4, 4)
            for d, mine, theirs in ((d0, m0, t0), (d1, m1, t1)):
                a, b = d[64 * yy : 64 * yy + 32, :], d[64 * yy + 32 : 64 * yy + 64, :]
                mine[ky, pl.ds(at, 32), :] = jnp.where(c == 0, a, b)
                theirs[ky, pl.ds(at, 32), :] = jnp.where(c == 0, b, a)


def factor(s):
    n = NB
    groups = [s[8 * i : 8 * i + 8, :] for i in range(n // 8)]
    sub = lax.broadcasted_iota(jnp.int32, (8, n), 0)
    lane = lax.broadcasted_iota(jnp.int32, (8, n), 1)
    for j in range(n // 8):
        r0 = 8 * j
        look = j + 1 < n // 8
        block = (lane >= r0) & (lane < r0 + 8)
        rows = groups[j]
        cols = [jnp.broadcast_to(rows[:, r0 + r : r0 + r + 1], (8, n)) for r in range(8)]
        rows = jnp.where(block, jnp.where(lane - r0 == sub, 1.0, 0.0), rows)
        if look:
            more = groups[j + 1]
            below = [jnp.broadcast_to(more[:, r0 + r : r0 + r + 1], (8, n)) for r in range(8)]
            more = jnp.where(block, 0.0, more)
        for r in range(8):
            rs = lax.rsqrt(cols[r][r : r + 1, :])
            l = cols[r] * rs
            lm = jnp.where(sub > r, l, 0.0)
            row = rows[r : r + 1, :] * rs
            rows = jnp.where(sub == r, row, rows - lm * row)
            if look:
                lq = below[r] * rs
                more = more - lq * row
            for s_ in range(r + 1, 8):
                at = l[s_ : s_ + 1, :]
                cols[s_] = cols[s_] - lm * at
                if look:
                    below[s_] = below[s_] - lq * at
        groups[j] = rows
        if look:
            groups[j + 1] = more
        if j + 2 < n // 8:
            m = n - r0 - 16
            rest = jnp.concatenate(groups[j + 2 :], axis=0)
            lanes = lax.broadcasted_iota(jnp.int32, (m, n), 1)
            rest = jnp.where((lanes >= r0) & (lanes < r0 + 8), 0.0, rest)
            rest = rest - mm(rows, rows, HI)[r0 + 16 :, :]
            for i in range(j + 2, n // 8):
                groups[i] = rest[8 * (i - j - 2) : 8 * (i - j - 1), :]
    return lower_part(jnp.concatenate(groups, axis=0))


def lower_part(v):
    r = lax.broadcasted_iota(jnp.int32, v.shape, 0)
    c = lax.broadcasted_iota(jnp.int32, v.shape, 1)
    return jnp.where(r >= c, v, 0.0)


def unpack_kernel(pos, own, other, w, up):
    c = pos[1]
    r = lax.broadcasted_iota(jnp.int32, (P_SIZE // 2, P_SIZE), 0)
    l = lax.broadcasted_iota(jnp.int32, (P_SIZE // 2, P_SIZE), 1)
    for half in range(2):
        at = slice(256 * half, 256 * half + 256)
        v = jnp.where(c == half, own[:, :P_SIZE], other[:, :P_SIZE])
        d = jnp.where(c == half, own[:, P_SIZE : P_SIZE + 1], other[:, P_SIZE : P_SIZE + 1])
        w[at, :] = v
        up[at, :] = jnp.where(l > r + 256 * half, v, jnp.where(l == r + 256 * half, d, 0.0))
    r = lax.broadcasted_iota(jnp.int32, (NB, NB), 0)
    l = lax.broadcasted_iota(jnp.int32, (NB, NB), 1)
    for o in range(0, P_SIZE, NB):
        s = jnp.where(r >= l, w[o : o + NB, o : o + NB], 0.0)
        w[o : o + NB, o : o + NB] = s + jnp.where(r < l, s.T, 0.0)
    inverse_step(0, w)


def inverse_step(o, w):
    e = o + NB
    t = factor(w[o:e, o:e])
    w[o:e, o:e] = t
    if o:
        w[o:e, :o] = mn(t, w[o:e, :o])
    if e < P_SIZE:
        low = mt(w[e:, o:e], t)
        w[e:, o:e] = -mn(low, t)
        if o:
            w[e:, :o] = w[e:, :o] - mn(low, w[o:e, :o])
        w[e:, e:] = w[e:, e:] - mt(low, low)
    else:
        w[...] = lower_part(w[...])


def inverse_kernel(o, pos, v, w):
    w[...] = v[...]
    inverse_step(o, w)


def whiten_kernel(pos, inv, up, p0, p1, p2, p3, q0, q1, q2, q3, panel, cross, tau, left):
    m = inv[...]
    left[0:32, :] = (p0[...] + p1[...]) + (p2[...] + p3[...])
    left[32:64, :] = (q0[...] + q1[...]) + (q2[...] + q3[...])
    rows = inv[pl.ds(pl.multiple_of(pos[2], 16), 16), :]
    u = up[...]
    r = lax.broadcasted_iota(jnp.int32, u.shape, 0)
    l = lax.broadcasted_iota(jnp.int32, u.shape, 1)
    left[64:80, :] = mn(rows, u) + mt(rows, jnp.where(l > r, u, 0.0))
    res = mt(left[...], m)
    panel[0] = res[0:32, :]
    cross[0] = res[32:64, :]
    tau[...] = res[64:80, :]


def swap_core(v, only=None):
    return move(v, lambda z, y, c, w, x: (z, y, 1 - c, w, x) if only is None or (w, x) == only else None)


def exchange(v, axes):
    return lax.all_to_all(v, axes, 0, 0, tiled=True)


def spread(v, axes, n):
    return exchange(jnp.broadcast_to(v[None], (n, *v.shape)), axes)


def diag_sum(mine, theirs, w, first):
    theirs, first = lax.optimization_barrier((theirs, first))
    half = (mine + swap_core(theirs, (0, 0))).reshape(16, 16, mine.shape[1])
    own = jnp.sum(exchange(half, ("z", "y")), axis=0)
    over = move(own, lambda z, y, c, w, x: (z, y, c, 1, 0) if (w, x) == (0, 0) else None)
    own = spread(jnp.where(w == 0, own, over), "x", 4)[0]
    half = spread(own, ("z", "y"), 16).reshape(mine.shape)
    return half, swap_core(half), first


def body(frames_data, starts, lags):
    tok, width = frames_data.shape
    z, y, c, w, x = (lax.axis_index(a) for a in AXES)
    slab = z * 8 + y * 2 + c
    total = tok * 32
    ends = jnp.concatenate([starts[1:], jnp.array([total], dtype=jnp.int32)])
    table = jnp.stack([starts, ends, lags])
    pos = jnp.stack([slab * tok, c, slab * 16, z, y, x]).astype(jnp.int32)
    panel = frames_data[:, :P_SIZE]

    def step(by):
        def target(z, y, c, w, x):
            i = z * 8 + y * 2 + c + by
            return (i // 8, i // 2 % 4, i % 2, 0, 0) if (w, x) == (0, 0) and 0 <= i < 32 else None
        return target

    after = move(panel[:RIM], step(-1))
    before = move(panel[tok - RIM :], step(1))

    packed = jax.ShapeDtypeStruct((256, P_SIZE + NB), F32)
    dz = call(
        diag_kernel, [packed, packed], (pos, table, panel, before, after), "diagonal",
        scratch=[pltpu.VMEM((tok + 2 * RIM, P_SIZE), BF16), pltpu.VMEM((tok, 3 * P_SIZE), BF16)],
        flops=3 * 10**9,
    )
    sent = [
        move(panel[STEP0 + CHUNK * (k - 1) : STEP0 + CHUNK * k],
             lambda z, y, c, w, x: (z, y, c, w, k) if (w, x) == (0, 0) else None)
        for k in (2, 1, 3)
    ]
    own, other, sent = diag_sum(*dz, w, sent)
    first = jnp.concatenate([before, after, panel[:FIRST]], axis=0)
    hold = jnp.where(x == 0, first, sent[0] + sent[1] + sent[2])
    over = move(hold, lambda z, y, c, w, x: (z, y, c, 1, x) if w == 0 else None)
    hold = jnp.where(w == 0, hold, over)
    gathered = [hold] + [
        move(hold, lambda z, y, c, w, x: (z, y, c, w, (x + k) % 4)) for k in (1, 2, 3)
    ]
    part = jax.ShapeDtypeStruct((4, 128, P_SIZE), F32)
    m0, t0, m1, t1 = call(
        cov_kernel, [part] * 4, (pos, table, frames_data, *gathered), "covariance",
        scratch=[pltpu.VMEM((tok + 2 * RIM, P_SIZE), BF16), pltpu.VMEM((tok, 3 * P_SIZE), BF16)],
        flops=5 * 10**9, vmem=20,
    )
    rows = []
    for mine, theirs in ((m0, t0), (m1, t1)):
        got = swap_core(theirs)
        s = [mine[k] + got[k] for k in range(4)]
        ys = [move(s[k], lambda z, y, c, w, x: (z, (y + k) % 4, c, w, x)) for k in (2, 1, 3)]
        t = s[0] + ys[0] + ys[1] + ys[2]
        rows += [t[:32]] + [
            move(t[32 * k : 32 * k + 32], lambda z, y, c, w, x: ((z + k) % 4, y, c, w, x)) for k in (2, 1, 3)
        ]

    full = jax.ShapeDtypeStruct((P_SIZE, P_SIZE), F32)
    inv, up = call(unpack_kernel, [full, full], (pos, own, other), "factor0", flops=5 * 10**9, vmem=8)
    for o in range(NB, P_SIZE, NB):
        (inv,) = call(functools.partial(inverse_kernel, o), [full], (pos, inv), "factor%d" % o, flops=5 * 10**9, vmem=8)
    own = jax.ShapeDtypeStruct((1, 32, P_SIZE), F32)
    return tuple(
        call(
            whiten_kernel, [own, own, jax.ShapeDtypeStruct((16, P_SIZE), F32)],
            (pos, inv, up, *rows), "whiten", scratch=[pltpu.VMEM((80, P_SIZE), F32)], flops=2 * 10**9,
        )
    )


def solution(mesh):
    split = Mesh(mesh.devices.reshape(SIZES), AXES)
    frames, feat = ("z", "y", "c"), ("w", "x")
    return jax.shard_map(
        body,
        mesh=split,
        in_specs=(P(frames, feat), P(), P()),
        out_specs=(P(feat, frames, None), P(feat, frames, None), P(frames, None)),
        check_vma=False,
    )
```

```python
import functools

import jax
import jax.numpy as jnp
from jax import lax
from jax.experimental import pallas as pl
from jax.experimental.pallas import tpu as pltpu
from jax.sharding import Mesh
from jax.sharding import PartitionSpec as P

P_SIZE = 512
RIM = 16
NB = 128
HI = lax.Precision.HIGHEST
F32 = jnp.float32
BF16 = jnp.bfloat16
AXES = ("z", "y", "c", "w", "x")
SIZES = (4, 4, 2, 2, 4)
CHUNK = 272
FIRST = CHUNK - 2 * RIM
STEP0 = 1024 - 3 * CHUNK


def coords():
    for z in range(4):
        for y in range(4):
            for c in range(2):
                for w in range(2):
                    for x in range(4):
                        yield (z, y, c, w, x)


def flat(p):
    i = 0
    for v, n in zip(p, SIZES):
        i = i * n + v
    return i


def move(value, target):
    pairs = []
    for p in coords():
        q = target(*p)
        if q is not None:
            pairs.append((flat(p), flat(q)))
    return lax.ppermute(value, AXES, pairs)


def call(kernel, outs, args, name, scratch=(), flops=0, vmem=16, hbm=()):
    specs = [pl.BlockSpec(memory_space=pltpu.VMEM)] * len(args)
    specs[0] = pl.BlockSpec(memory_space=pltpu.SMEM)
    for i in hbm:
        specs[i] = pl.BlockSpec(memory_space=pltpu.HBM)
    return pl.pallas_call(
        kernel,
        out_shape=outs,
        in_specs=specs,
        out_specs=[pl.BlockSpec(memory_space=pltpu.VMEM)] * len(outs),
        scratch_shapes=list(scratch),
        compiler_params=pltpu.CompilerParams(vmem_limit_bytes=vmem * 2**20),
        cost_estimate=pl.CostEstimate(flops=flops, bytes_accessed=2**20, transcendentals=0),
        name=name,
    )(*args)


def mm(a, b, precision=None):
    return lax.dot_general(
        a, b, (((0,), (0,)), ((), ())), precision=precision, preferred_element_type=F32
    )


def mn(a, b):
    return lax.dot_general(
        a, b, (((1,), (0,)), ((), ())), precision=HI, preferred_element_type=F32
    )


def mt(a, b):
    return lax.dot_general(
        a, b, (((1,), (1,)), ((), ())), precision=HI, preferred_element_type=F32
    )


def frame_info(first, rows, table):
    starts, ends, lags = (table[i : i + 1, :].astype(F32) for i in range(3))
    t = (first + lax.broadcasted_iota(jnp.int32, (rows, 1), 0)).astype(F32)
    here = (starts <= t) & (t < ends)
    pick = lambda v: jnp.sum(jnp.where(here, v, 0.0), axis=1, keepdims=True)
    lag = pick(lags)
    ahead = jnp.where(t + lag < pick(ends), 1.0, 0.0)
    behind = jnp.where(t - lag >= pick(starts), 1.0, 0.0)
    return lag, ahead, behind


def pair_count(table):
    starts, ends, lags = (table[i : i + 1, :].astype(F32) for i in range(3))
    return jnp.sum(jnp.maximum(ends - starts - lags, 0.0), axis=1, keepdims=True)


def shifted(window, lag, ahead, behind):
    rows, width = lag.shape[0], window.shape[0]
    off = (
        lax.broadcasted_iota(jnp.int32, (rows, width), 1)
        - lax.broadcasted_iota(jnp.int32, (rows, width), 0)
        - RIM
    ).astype(F32)
    later = jnp.where((off == lag) & (ahead > 0.0), 1.0, 0.0).astype(BF16)
    earlier = jnp.where((off == -lag) & (behind > 0.0), 1.0, 0.0).astype(BF16)
    dims = (((1,), (0,)), ((), ()))
    zp = lax.dot_general(later, window, dims, preferred_element_type=F32)
    zm = lax.dot_general(earlier, window, dims, preferred_element_type=F32)
    return zp.astype(BF16), zm.astype(BF16)


def diag_kernel(pos, table, xp, before, after, mine, theirs, ext, right):
    rows = xp.shape[0]
    ext[0:RIM, :] = before[...]
    ext[RIM : RIM + rows, :] = xp[...]
    ext[RIM + rows :, :] = after[...]
    fill_right(pos, table, ext, right, rows, P_SIZE)
    scale = 1.0 / pair_count(table)
    c = pos[1]
    v = xp[...]
    for half in range(2):
        cols = slice(256 * half, 256 * half + 256)
        d0 = mm(v[:, cols], right[:, :P_SIZE]) * scale
        d1 = mm(v[:, cols], right[:, P_SIZE : 2 * P_SIZE]) + mm(v[:, cols], right[:, 2 * P_SIZE :])
        d1 = d1 * (0.5 * scale)
        r = lax.broadcasted_iota(jnp.int32, d0.shape, 0) + 256 * half
        l = lax.broadcasted_iota(jnp.int32, d0.shape, 1)
        packed = jnp.where(r >= l, d0, d1)
        diag = jnp.sum(jnp.where(r == l, d1, 0.0), axis=1, keepdims=True)
        diag = jnp.broadcast_to(diag, (256, NB))

        @pl.when(c == half)
        def _():
            mine[:, :P_SIZE] = packed
            mine[:, P_SIZE:] = diag

        @pl.when(c != half)
        def _():
            theirs[:, :P_SIZE] = packed
            theirs[:, P_SIZE:] = diag


def fill_right(pos, table, ext, right, rows, n):
    for b in range(0, rows, 256):
        lag, ahead, behind = frame_info(pos[0] + b, 256, table)
        zp, zm = shifted(ext[b : b + 256 + 2 * RIM, :], lag, ahead, behind)
        own = ext[b + RIM : b + RIM + 256, :]
        right[b : b + 256, :n] = own * (0.5 * (ahead + behind)).astype(BF16)
        right[b : b + 256, n : 2 * n] = zp
        right[b : b + 256, 2 * n :] = zm


def cov_kernel(pos, table, x, g0, g1, g2, g3, m0, t0, m1, t1, ext, right, sem):
    rows, n = x.shape[0], P_SIZE
    c, z, y, col = pos[1], pos[3], pos[4], pos[5]
    for wait in (False, True):
        for k, g in enumerate((g0, g1, g2, g3)):
            q = lax.rem(col - k + 4, 4)

            def bring(src, dst, i):
                copy = pltpu.make_async_copy(src, dst, sem.at[k, i])
                copy.wait() if wait else copy.start()

            @pl.when(q == 0)
            def _():
                bring(g.at[0:RIM, :], ext.at[0:RIM, :], 0)
                bring(g.at[RIM : 2 * RIM, :], ext.at[RIM + rows : 2 * RIM + rows, :], 1)
                bring(g.at[2 * RIM : CHUNK, :], ext.at[RIM : RIM + FIRST, :], 2)

            @pl.when(q != 0)
            def _():
                at = pl.multiple_of(RIM + STEP0 + CHUNK * (q - 1), 16)
                bring(g, ext.at[pl.ds(at, CHUNK), :], 0)

    fill_right(pos, table, ext, right, rows, n)
    scale = 1.0 / pair_count(table)
    for zz in range(4):
        left = x[:, 256 * zz : 256 * zz + 256]
        d0 = mm(left, right[:, :n]) * scale
        d1 = mm(left, right[:, n : 2 * n]) + mm(left, right[:, 2 * n :])
        d1 = d1 * (0.5 * scale)
        at = pl.multiple_of(lax.rem(zz - z + 4, 4) * 32, 32)
        for yy in range(4):
            ky = lax.rem(yy - y + 4, 4)
            for d, mine, theirs in ((d0, m0, t0), (d1, m1, t1)):
                a, b = d[64 * yy : 64 * yy + 32, :], d[64 * yy + 32 : 64 * yy + 64, :]
                mine[ky, pl.ds(at, 32), :] = jnp.where(c == 0, a, b)
                theirs[ky, pl.ds(at, 32), :] = jnp.where(c == 0, b, a)


def factor(s):
    n = NB
    groups = [s[8 * i : 8 * i + 8, :] for i in range(n // 8)]
    sub = lax.broadcasted_iota(jnp.int32, (8, n), 0)
    lane = lax.broadcasted_iota(jnp.int32, (8, n), 1)
    for j in range(n // 8):
        r0 = 8 * j
        look = j + 1 < n // 8
        block = (lane >= r0) & (lane < r0 + 8)
        rows = groups[j]
        cols = [jnp.broadcast_to(rows[:, r0 + r : r0 + r + 1], (8, n)) for r in range(8)]
        rows = jnp.where(block, jnp.where(lane - r0 == sub, 1.0, 0.0), rows)
        if look:
            more = groups[j + 1]
            below = [jnp.broadcast_to(more[:, r0 + r : r0 + r + 1], (8, n)) for r in range(8)]
            more = jnp.where(block, 0.0, more)
        for r in range(8):
            rs = lax.rsqrt(cols[r][r : r + 1, :])
            l = cols[r] * rs
            lm = jnp.where(sub > r, l, 0.0)
            row = rows[r : r + 1, :] * rs
            rows = jnp.where(sub == r, row, rows - lm * row)
            if look:
                lq = below[r] * rs
                more = more - lq * row
            for s_ in range(r + 1, 8):
                at = l[s_ : s_ + 1, :]
                cols[s_] = cols[s_] - lm * at
                if look:
                    below[s_] = below[s_] - lq * at
        groups[j] = rows
        if look:
            groups[j + 1] = more
        if j + 2 < n // 8:
            m = n - r0 - 16
            rest = jnp.concatenate(groups[j + 2 :], axis=0)
            lanes = lax.broadcasted_iota(jnp.int32, (m, n), 1)
            rest = jnp.where((lanes >= r0) & (lanes < r0 + 8), 0.0, rest)
            rest = rest - mm(rows, rows, HI)[r0 + 16 :, :]
            for i in range(j + 2, n // 8):
                groups[i] = rest[8 * (i - j - 2) : 8 * (i - j - 1), :]
    return lower_part(jnp.concatenate(groups, axis=0))


def lower_part(v):
    r = lax.broadcasted_iota(jnp.int32, v.shape, 0)
    c = lax.broadcasted_iota(jnp.int32, v.shape, 1)
    return jnp.where(r >= c, v, 0.0)


def unpack_kernel(pos, own, other, w, up):
    c = pos[1]
    r = lax.broadcasted_iota(jnp.int32, (P_SIZE // 2, P_SIZE), 0)
    l = lax.broadcasted_iota(jnp.int32, (P_SIZE // 2, P_SIZE), 1)
    for half in range(2):
        at = slice(256 * half, 256 * half + 256)
        v = jnp.where(c == half, own[:, :P_SIZE], other[:, :P_SIZE])
        d = jnp.where(c == half, own[:, P_SIZE : P_SIZE + 1], other[:, P_SIZE : P_SIZE + 1])
        w[at, :] = v
        up[at, :] = jnp.where(l > r + 256 * half, v, jnp.where(l == r + 256 * half, d, 0.0))
    r = lax.broadcasted_iota(jnp.int32, (NB, NB), 0)
    l = lax.broadcasted_iota(jnp.int32, (NB, NB), 1)
    for o in range(0, P_SIZE, NB):
        s = jnp.where(r >= l, w[o : o + NB, o : o + NB], 0.0)
        w[o : o + NB, o : o + NB] = s + jnp.where(r < l, s.T, 0.0)
    inverse_step(0, w)


def inverse_step(o, w):
    e = o + NB
    t = factor(w[o:e, o:e])
    w[o:e, o:e] = t
    if o:
        w[o:e, :o] = mn(t, w[o:e, :o])
    if e < P_SIZE:
        low = mt(w[e:, o:e], t)
        w[e:, o:e] = -mn(low, t)
        if o:
            w[e:, :o] = w[e:, :o] - mn(low, w[o:e, :o])
        w[e:, e:] = w[e:, e:] - mt(low, low)
    else:
        w[...] = lower_part(w[...])


def inverse_kernel(o, pos, v, w):
    w[...] = v[...]
    inverse_step(o, w)


def whiten_kernel(pos, inv, up, p0, p1, p2, p3, q0, q1, q2, q3, panel, cross, tau, left):
    m = inv[...]
    left[0:32, :] = (p0[...] + p1[...]) + (p2[...] + p3[...])
    left[32:64, :] = (q0[...] + q1[...]) + (q2[...] + q3[...])
    rows = inv[pl.ds(pl.multiple_of(pos[2], 16), 16), :]
    u = up[...]
    r = lax.broadcasted_iota(jnp.int32, u.shape, 0)
    l = lax.broadcasted_iota(jnp.int32, u.shape, 1)
    left[64:80, :] = mn(rows, u) + mt(rows, jnp.where(l > r, u, 0.0))
    res = mt(left[...], m)
    panel[0] = res[0:32, :]
    cross[0] = res[32:64, :]
    tau[...] = res[64:80, :]


def swap_core(v, only=None):
    return move(v, lambda z, y, c, w, x: (z, y, 1 - c, w, x) if only is None or (w, x) == only else None)


def exchange(v, axes):
    return lax.all_to_all(v, axes, 0, 0, tiled=True)


def spread(v, axes, n):
    return exchange(jnp.broadcast_to(v[None], (n, *v.shape)), axes)


def together(*values):
    return lax.optimization_barrier(values)


def diag_half(mine, theirs):
    half = (mine + swap_core(theirs, (0, 0))).reshape(4, 64, mine.shape[1])
    return jnp.sum(exchange(half, "y"), axis=0)


def diag_rows(quarter):
    return jnp.sum(exchange(quarter.reshape(4, 16, quarter.shape[1]), "z"), axis=0)


def diag_feat(own, w):
    over = move(own, lambda z, y, c, w, x: (z, y, c, 1, 0) if (w, x) == (0, 0) else None)
    return spread(jnp.where(w == 0, own, over), "x", 4)[0]


def diag_gather(own):
    half = spread(own, ("y", "z"), 16).reshape(256, own.shape[1])
    return half, swap_core(half)


def body(frames_data, starts, lags):
    tok, width = frames_data.shape
    z, y, c, w, x = (lax.axis_index(a) for a in AXES)
    slab = z * 8 + y * 2 + c
    total = tok * 32
    ends = jnp.concatenate([starts[1:], jnp.array([total], dtype=jnp.int32)])
    table = jnp.stack([starts, ends, lags])
    pos = jnp.stack([slab * tok, c, slab * 16, z, y, x]).astype(jnp.int32)
    panel = frames_data[:, :P_SIZE]

    def step(by):
        def target(z, y, c, w, x):
            i = z * 8 + y * 2 + c + by
            return (i // 8, i // 2 % 4, i % 2, 0, 0) if (w, x) == (0, 0) and 0 <= i < 32 else None
        return target

    behind = move(panel[:RIM], step(-1))
    before = move(panel[tok - RIM :], step(1))

    packed = jax.ShapeDtypeStruct((256, P_SIZE + NB), F32)
    dz = call(
        diag_kernel, [packed, packed], (pos, table, panel, before, behind), "diagonal",
        scratch=[pltpu.VMEM((tok + 2 * RIM, P_SIZE), BF16), pltpu.VMEM((tok, 3 * P_SIZE), BF16)],
        flops=3 * 10**9,
    )
    sent = [
        move(panel[STEP0 + CHUNK * (k - 1) : STEP0 + CHUNK * k],
             lambda z, y, c, w, x: (z, y, c, w, k) if (w, x) == (0, 0) else None)
        for k in (2, 1, 3)
    ]
    first = jnp.concatenate([before, behind, panel[:FIRST]], axis=0)
    hold = jnp.where(x == 0, first, sent[0] + sent[1] + sent[2])
    mine, theirs = dz
    theirs, hold = together(theirs, hold)
    over = move(hold, lambda z, y, c, w, x: (z, y, c, 1, x) if w == 0 else None)
    quarter, over = together(diag_half(mine, theirs), over)
    rows16 = diag_rows(quarter)
    hold = jnp.where(w == 0, hold, over)
    gathered = [hold] + [
        move(hold, lambda z, y, c, w, x: (z, y, c, w, (x + k) % 4)) for k in (1, 2, 3)
    ]
    rows16, later = together(diag_feat(rows16, w), pos)
    own, other = diag_gather(rows16)
    part = jax.ShapeDtypeStruct((4, 128, P_SIZE), F32)
    m0, t0, m1, t1 = call(
        cov_kernel, [part] * 4, (later, table, frames_data, *gathered), "covariance",
        scratch=[
            pltpu.VMEM((tok + 2 * RIM, P_SIZE), BF16),
            pltpu.VMEM((tok, 3 * P_SIZE), BF16),
            pltpu.SemaphoreType.DMA((4, 3)),
        ],
        flops=5 * 10**9, vmem=20, hbm=(3, 4, 5, 6),
    )
    rows = []
    for mine, theirs in ((m0, t0), (m1, t1)):
        got = swap_core(theirs)
        s = [mine[k] + got[k] for k in range(4)]
        ys = [move(s[k], lambda z, y, c, w, x: (z, (y + k) % 4, c, w, x)) for k in (2, 1, 3)]
        t = s[0] + ys[0] + ys[1] + ys[2]
        rows += [t[:32]] + [
            move(t[32 * k : 32 * k + 32], lambda z, y, c, w, x: ((z + k) % 4, y, c, w, x)) for k in (2, 1, 3)
        ]

    full = jax.ShapeDtypeStruct((P_SIZE, P_SIZE), F32)
    inv, up = call(unpack_kernel, [full, full], (pos, own, other), "factor0", flops=5 * 10**9, vmem=8)
    for o in range(NB, P_SIZE, NB):
        (inv,) = call(functools.partial(inverse_kernel, o), [full], (pos, inv), "factor%d" % o, flops=5 * 10**9, vmem=8)
    own = jax.ShapeDtypeStruct((1, 32, P_SIZE), F32)
    return tuple(
        call(
            whiten_kernel, [own, own, jax.ShapeDtypeStruct((16, P_SIZE), F32)],
            (pos, inv, up, *rows), "whiten", scratch=[pltpu.VMEM((80, P_SIZE), F32)], flops=2 * 10**9,
        )
    )


def solution(mesh):
    split = Mesh(mesh.devices.reshape(SIZES), AXES)
    frames, feat = ("z", "y", "c"), ("w", "x")
    return jax.shard_map(
        body,
        mesh=split,
        in_specs=(P(frames, feat), P(), P()),
        out_specs=(P(feat, frames, None), P(feat, frames, None), P(frames, None)),
        check_vma=False,
    )
```

```python
import functools

import jax
import jax.numpy as jnp
from jax import lax
from jax.experimental import pallas as pl
from jax.experimental.pallas import tpu as pltpu
from jax.sharding import Mesh
from jax.sharding import PartitionSpec as P

P_SIZE = 512
RIM = 16
NB = 128
HI = lax.Precision.HIGHEST
F32 = jnp.float32
BF16 = jnp.bfloat16
AXES = ("z", "y", "c", "w", "x")
SIZES = (4, 4, 2, 2, 4)
CHUNK = 272
FIRST = CHUNK - 2 * RIM
STEP0 = 1024 - 3 * CHUNK


def coords():
    for z in range(4):
        for y in range(4):
            for c in range(2):
                for w in range(2):
                    for x in range(4):
                        yield (z, y, c, w, x)


def flat(p):
    i = 0
    for v, n in zip(p, SIZES):
        i = i * n + v
    return i


def move(value, target):
    pairs = []
    for p in coords():
        q = target(*p)
        if q is not None:
            pairs.append((flat(p), flat(q)))
    return lax.ppermute(value, AXES, pairs)


def call(kernel, outs, args, name, scratch=(), flops=0, vmem=16, hbm=()):
    specs = [pl.BlockSpec(memory_space=pltpu.VMEM)] * len(args)
    specs[0] = pl.BlockSpec(memory_space=pltpu.SMEM)
    for i in hbm:
        specs[i] = pl.BlockSpec(memory_space=pltpu.HBM)
    return pl.pallas_call(
        kernel,
        out_shape=outs,
        in_specs=specs,
        out_specs=[pl.BlockSpec(memory_space=pltpu.VMEM)] * len(outs),
        scratch_shapes=list(scratch),
        compiler_params=pltpu.CompilerParams(vmem_limit_bytes=vmem * 2**20),
        cost_estimate=pl.CostEstimate(flops=flops, bytes_accessed=2**20, transcendentals=0),
        name=name,
    )(*args)


def mm(a, b, precision=None):
    return lax.dot_general(
        a, b, (((0,), (0,)), ((), ())), precision=precision, preferred_element_type=F32
    )


def mn(a, b):
    return lax.dot_general(
        a, b, (((1,), (0,)), ((), ())), precision=HI, preferred_element_type=F32
    )


def mt(a, b):
    return lax.dot_general(
        a, b, (((1,), (1,)), ((), ())), precision=HI, preferred_element_type=F32
    )


def frame_info(first, rows, table):
    starts, ends, lags = (table[i : i + 1, :].astype(F32) for i in range(3))
    t = (first + lax.broadcasted_iota(jnp.int32, (rows, 1), 0)).astype(F32)
    here = (starts <= t) & (t < ends)
    pick = lambda v: jnp.sum(jnp.where(here, v, 0.0), axis=1, keepdims=True)
    lag = pick(lags)
    ahead = jnp.where(t + lag < pick(ends), 1.0, 0.0)
    behind = jnp.where(t - lag >= pick(starts), 1.0, 0.0)
    return lag, ahead, behind


def pair_count(table):
    starts, ends, lags = (table[i : i + 1, :].astype(F32) for i in range(3))
    return jnp.sum(jnp.maximum(ends - starts - lags, 0.0), axis=1, keepdims=True)


def shifted(window, lag, ahead, behind):
    rows, width = lag.shape[0], window.shape[0]
    off = (
        lax.broadcasted_iota(jnp.int32, (rows, width), 1)
        - lax.broadcasted_iota(jnp.int32, (rows, width), 0)
        - RIM
    ).astype(F32)
    later = jnp.where((off == lag) & (ahead > 0.0), 1.0, 0.0).astype(BF16)
    earlier = jnp.where((off == -lag) & (behind > 0.0), 1.0, 0.0).astype(BF16)
    dims = (((1,), (0,)), ((), ()))
    zp = lax.dot_general(later, window, dims, preferred_element_type=F32)
    zm = lax.dot_general(earlier, window, dims, preferred_element_type=F32)
    return zp.astype(BF16), zm.astype(BF16)


def diag_kernel(pos, table, xp, before, after, mine, theirs, ext, right):
    rows = xp.shape[0]
    ext[0:RIM, :] = before[...]
    ext[RIM : RIM + rows, :] = xp[...]
    ext[RIM + rows :, :] = after[...]
    fill_right(pos, table, ext, right, rows, P_SIZE)
    scale = 1.0 / pair_count(table)
    c = pos[1]
    v = xp[...]
    for half in range(2):
        cols = slice(256 * half, 256 * half + 256)
        d0 = mm(v[:, cols], right[:, :P_SIZE]) * scale
        d1 = mm(v[:, cols], right[:, P_SIZE : 2 * P_SIZE]) + mm(v[:, cols], right[:, 2 * P_SIZE :])
        d1 = d1 * (0.5 * scale)
        r = lax.broadcasted_iota(jnp.int32, d0.shape, 0) + 256 * half
        l = lax.broadcasted_iota(jnp.int32, d0.shape, 1)
        packed = jnp.where(r >= l, d0, d1)
        diag = jnp.sum(jnp.where(r == l, d1, 0.0), axis=1, keepdims=True)
        diag = jnp.broadcast_to(diag, (256, NB))

        @pl.when(c == half)
        def _():
            mine[:, :P_SIZE] = packed
            mine[:, P_SIZE:] = diag

        @pl.when(c != half)
        def _():
            theirs[:, :P_SIZE] = packed
            theirs[:, P_SIZE:] = diag


def fill_right(pos, table, ext, right, rows, n):
    for b in range(0, rows, 256):
        lag, ahead, behind = frame_info(pos[0] + b, 256, table)
        zp, zm = shifted(ext[b : b + 256 + 2 * RIM, :], lag, ahead, behind)
        own = ext[b + RIM : b + RIM + 256, :]
        right[b : b + 256, :n] = own * (0.5 * (ahead + behind)).astype(BF16)
        right[b : b + 256, n : 2 * n] = zp
        right[b : b + 256, 2 * n :] = zm


def cov_kernel(pos, table, x, g0, g1, g2, g3, out, ext, right, sem):
    rows, n = x.shape[0], P_SIZE
    z, col = pos[3], pos[5]
    for wait in (False, True):
        for k, g in enumerate((g0, g1, g2, g3)):
            q = lax.rem(col - k + 4, 4)

            def bring(src, dst, i):
                copy = pltpu.make_async_copy(src, dst, sem.at[k, i])
                copy.wait() if wait else copy.start()

            @pl.when(q == 0)
            def _():
                bring(g.at[0:RIM, :], ext.at[0:RIM, :], 0)
                bring(g.at[RIM : 2 * RIM, :], ext.at[RIM + rows : 2 * RIM + rows, :], 1)
                bring(g.at[2 * RIM : CHUNK, :], ext.at[RIM : RIM + FIRST, :], 2)

            @pl.when(q != 0)
            def _():
                at = pl.multiple_of(RIM + STEP0 + CHUNK * (q - 1), 16)
                bring(g, ext.at[pl.ds(at, CHUNK), :], 0)

    fill_right(pos, table, ext, right, rows, n)
    scale = 1.0 / pair_count(table)
    for zz in range(4):
        left = x[:, 256 * zz : 256 * zz + 256]
        d0 = mm(left, right[:, :n]) * scale
        d1 = mm(left, right[:, n : 2 * n]) + mm(left, right[:, 2 * n :])
        d1 = d1 * (0.5 * scale)
        at = pl.multiple_of(lax.rem(zz - z + 4, 4) * 32, 32)
        for k in range(8):
            out[k, pl.ds(at, 32), :n] = d0[32 * k : 32 * k + 32, :]
            out[k, pl.ds(at, 32), n:] = d1[32 * k : 32 * k + 32, :]


def factor(s):
    n = NB
    groups = [s[8 * i : 8 * i + 8, :] for i in range(n // 8)]
    sub = lax.broadcasted_iota(jnp.int32, (8, n), 0)
    lane = lax.broadcasted_iota(jnp.int32, (8, n), 1)
    for j in range(n // 8):
        r0 = 8 * j
        look = j + 1 < n // 8
        block = (lane >= r0) & (lane < r0 + 8)
        rows = groups[j]
        cols = [jnp.broadcast_to(rows[:, r0 + r : r0 + r + 1], (8, n)) for r in range(8)]
        rows = jnp.where(block, jnp.where(lane - r0 == sub, 1.0, 0.0), rows)
        if look:
            more = groups[j + 1]
            below = [jnp.broadcast_to(more[:, r0 + r : r0 + r + 1], (8, n)) for r in range(8)]
            more = jnp.where(block, 0.0, more)
        for r in range(8):
            rs = lax.rsqrt(cols[r][r : r + 1, :])
            l = cols[r] * rs
            lm = jnp.where(sub > r, l, 0.0)
            row = rows[r : r + 1, :] * rs
            rows = jnp.where(sub == r, row, rows - lm * row)
            if look:
                lq = below[r] * rs
                more = more - lq * row
            for s_ in range(r + 1, 8):
                at = l[s_ : s_ + 1, :]
                cols[s_] = cols[s_] - lm * at
                if look:
                    below[s_] = below[s_] - lq * at
        groups[j] = rows
        if look:
            groups[j + 1] = more
        if j + 2 < n // 8:
            m = n - r0 - 16
            rest = jnp.concatenate(groups[j + 2 :], axis=0)
            lanes = lax.broadcasted_iota(jnp.int32, (m, n), 1)
            rest = jnp.where((lanes >= r0) & (lanes < r0 + 8), 0.0, rest)
            rest = rest - mm(rows, rows, HI)[r0 + 16 :, :]
            for i in range(j + 2, n // 8):
                groups[i] = rest[8 * (i - j - 2) : 8 * (i - j - 1), :]
    return lower_part(jnp.concatenate(groups, axis=0))


def lower_part(v):
    r = lax.broadcasted_iota(jnp.int32, v.shape, 0)
    c = lax.broadcasted_iota(jnp.int32, v.shape, 1)
    return jnp.where(r >= c, v, 0.0)


def unpack_kernel(pos, own, other, w, up):
    c = pos[1]
    r = lax.broadcasted_iota(jnp.int32, (P_SIZE // 2, P_SIZE), 0)
    l = lax.broadcasted_iota(jnp.int32, (P_SIZE // 2, P_SIZE), 1)
    for half in range(2):
        at = slice(256 * half, 256 * half + 256)
        v = jnp.where(c == half, own[:, :P_SIZE], other[:, :P_SIZE])
        d = jnp.where(c == half, own[:, P_SIZE : P_SIZE + 1], other[:, P_SIZE : P_SIZE + 1])
        w[at, :] = v
        up[at, :] = jnp.where(l > r + 256 * half, v, jnp.where(l == r + 256 * half, d, 0.0))
    r = lax.broadcasted_iota(jnp.int32, (NB, NB), 0)
    l = lax.broadcasted_iota(jnp.int32, (NB, NB), 1)
    for o in range(0, P_SIZE, NB):
        s = jnp.where(r >= l, w[o : o + NB, o : o + NB], 0.0)
        w[o : o + NB, o : o + NB] = s + jnp.where(r < l, s.T, 0.0)
    inverse_step(0, w)


def inverse_step(o, w):
    e = o + NB
    t = factor(w[o:e, o:e])
    w[o:e, o:e] = t
    if o:
        w[o:e, :o] = mn(t, w[o:e, :o])
    if e < P_SIZE:
        low = mt(w[e:, o:e], t)
        w[e:, o:e] = -mn(low, t)
        if o:
            w[e:, :o] = w[e:, :o] - mn(low, w[o:e, :o])
        w[e:, e:] = w[e:, e:] - mt(low, low)
    else:
        w[...] = lower_part(w[...])


def inverse_kernel(o, pos, v, w):
    w[...] = v[...]
    inverse_step(o, w)


def whiten_kernel(pos, inv, up, p0, p1, p2, p3, panel, cross, tau, left):
    m = inv[...]
    s = (p0[...] + p1[...]) + (p2[...] + p3[...])
    left[0:32, :] = s[:, :P_SIZE]
    left[32:64, :] = s[:, P_SIZE:]
    rows = inv[pl.ds(pl.multiple_of(pos[2], 16), 16), :]
    u = up[...]
    r = lax.broadcasted_iota(jnp.int32, u.shape, 0)
    l = lax.broadcasted_iota(jnp.int32, u.shape, 1)
    left[64:80, :] = mn(rows, u) + mt(rows, jnp.where(l > r, u, 0.0))
    res = mt(left[...], m)
    panel[0] = res[0:32, :]
    cross[0] = res[32:64, :]
    tau[...] = res[64:80, :]


def swap_core(v, only=None):
    return move(v, lambda z, y, c, w, x: (z, y, 1 - c, w, x) if only is None or (w, x) == only else None)


def exchange(v, axes):
    return lax.all_to_all(v, axes, 0, 0, tiled=True)


def spread(v, axes, n):
    return exchange(jnp.broadcast_to(v[None], (n, *v.shape)), axes)


def together(*values):
    return lax.optimization_barrier(values)


def diag_half(mine, theirs):
    half = (mine + swap_core(theirs, (0, 0))).reshape(4, 64, mine.shape[1])
    return jnp.sum(exchange(half, "y"), axis=0)


def diag_rows(quarter):
    return jnp.sum(exchange(quarter.reshape(4, 16, quarter.shape[1]), "z"), axis=0)


def diag_feat(own, w):
    over = move(own, lambda z, y, c, w, x: (z, y, c, 1, 0) if (w, x) == (0, 0) else None)
    return spread(jnp.where(w == 0, own, over), "x", 4)[0]


def diag_gather(own):
    half = spread(own, ("y", "z"), 16).reshape(256, own.shape[1])
    return half, swap_core(half)


def body(frames_data, starts, lags):
    tok, width = frames_data.shape
    z, y, c, w, x = (lax.axis_index(a) for a in AXES)
    slab = z * 8 + y * 2 + c
    total = tok * 32
    ends = jnp.concatenate([starts[1:], jnp.array([total], dtype=jnp.int32)])
    table = jnp.stack([starts, ends, lags])
    pos = jnp.stack([slab * tok, c, slab * 16, z, y, x]).astype(jnp.int32)
    panel = frames_data[:, :P_SIZE]

    def step(by):
        def target(z, y, c, w, x):
            i = z * 8 + y * 2 + c + by
            return (i // 8, i // 2 % 4, i % 2, 0, 0) if (w, x) == (0, 0) and 0 <= i < 32 else None
        return target

    behind = move(panel[:RIM], step(-1))
    before = move(panel[tok - RIM :], step(1))

    packed = jax.ShapeDtypeStruct((256, P_SIZE + NB), F32)
    dz = call(
        diag_kernel, [packed, packed], (pos, table, panel, before, behind), "diagonal",
        scratch=[pltpu.VMEM((tok + 2 * RIM, P_SIZE), BF16), pltpu.VMEM((tok, 3 * P_SIZE), BF16)],
        flops=3 * 10**9,
    )
    sent = [
        move(panel[STEP0 + CHUNK * (k - 1) : STEP0 + CHUNK * k],
             lambda z, y, c, w, x: (z, y, c, w, k) if (w, x) == (0, 0) else None)
        for k in (2, 1, 3)
    ]
    first = jnp.concatenate([before, behind, panel[:FIRST]], axis=0)
    hold = jnp.where(x == 0, first, sent[0] + sent[1] + sent[2])
    mine, theirs = dz
    theirs, hold = together(theirs, hold)
    over = move(hold, lambda z, y, c, w, x: (z, y, c, 1, x) if w == 0 else None)
    quarter, over = together(diag_half(mine, theirs), over)
    rows16 = diag_rows(quarter)
    hold = jnp.where(w == 0, hold, over)
    gathered = [hold] + [
        move(hold, lambda z, y, c, w, x: (z, y, c, w, (x + k) % 4)) for k in (1, 2, 3)
    ]
    rows16, *gathered = together(rows16, *gathered)
    own, other = diag_gather(diag_feat(rows16, w))
    (part,) = call(
        cov_kernel, [jax.ShapeDtypeStruct((8, 128, 2 * P_SIZE), F32)], (pos, table, frames_data, *gathered), "covariance",
        scratch=[
            pltpu.VMEM((tok + 2 * RIM, P_SIZE), BF16),
            pltpu.VMEM((tok, 3 * P_SIZE), BF16),
            pltpu.SemaphoreType.DMA((4, 3)),
        ],
        flops=5 * 10**9, vmem=20, hbm=(3, 4, 5, 6),
    )
    t = lax.psum_scatter(part.reshape(1024, 2 * P_SIZE), ("y", "c"), scatter_dimension=0, tiled=True)
    rows = [t[:32]] + [
        move(t[32 * k : 32 * k + 32], lambda z, y, c, w, x: ((z + k) % 4, y, c, w, x)) for k in (2, 1, 3)
    ]

    full = jax.ShapeDtypeStruct((P_SIZE, P_SIZE), F32)
    inv, up = call(unpack_kernel, [full, full], (pos, own, other), "factor0", flops=5 * 10**9, vmem=8)
    for o in range(NB, P_SIZE, NB):
        (inv,) = call(functools.partial(inverse_kernel, o), [full], (pos, inv), "factor%d" % o, flops=5 * 10**9, vmem=8)
    own = jax.ShapeDtypeStruct((1, 32, P_SIZE), F32)
    return tuple(
        call(
            whiten_kernel, [own, own, jax.ShapeDtypeStruct((16, P_SIZE), F32)],
            (pos, inv, up, *rows), "whiten", scratch=[pltpu.VMEM((80, P_SIZE), F32)], flops=2 * 10**9,
        )
    )


def solution(mesh):
    split = Mesh(mesh.devices.reshape(SIZES), AXES)
    frames, feat = ("z", "y", "c"), ("w", "x")
    return jax.shard_map(
        body,
        mesh=split,
        in_specs=(P(frames, feat), P(), P()),
        out_specs=(P(feat, frames, None), P(feat, frames, None), P(frames, None)),
        check_vma=False,
    )
```

```python
import functools

import jax
import jax.numpy as jnp
from jax import lax
from jax.experimental import pallas as pl
from jax.experimental.pallas import tpu as pltpu
from jax.sharding import Mesh
from jax.sharding import PartitionSpec as P

P_SIZE = 512
RIM = 16
NB = 128
HI = lax.Precision.HIGHEST
F32 = jnp.float32
BF16 = jnp.bfloat16
AXES = ("z", "y", "c", "w", "x")
SIZES = (4, 4, 2, 2, 4)
CHUNK = 272
FIRST = CHUNK - 2 * RIM
STEP0 = 1024 - 3 * CHUNK


def coords():
    for z in range(4):
        for y in range(4):
            for c in range(2):
                for w in range(2):
                    for x in range(4):
                        yield (z, y, c, w, x)


def flat(p):
    i = 0
    for v, n in zip(p, SIZES):
        i = i * n + v
    return i


def move(value, target):
    pairs = []
    for p in coords():
        q = target(*p)
        if q is not None:
            pairs.append((flat(p), flat(q)))
    return lax.ppermute(value, AXES, pairs)


def call(kernel, outs, args, name, scratch=(), flops=0, vmem=16, hbm=(), block=None):
    specs = [pl.BlockSpec(memory_space=pltpu.VMEM)] * len(args)
    specs[0] = pl.BlockSpec(memory_space=pltpu.SMEM)
    for i in hbm:
        specs[i] = pl.BlockSpec(memory_space=pltpu.HBM)
    for i, shape in (block or {}).items():
        specs[i] = pl.BlockSpec(shape, lambda i: (0, 0))
    return pl.pallas_call(
        kernel,
        grid=(1,),
        out_shape=outs,
        in_specs=specs,
        out_specs=[pl.BlockSpec(memory_space=pltpu.VMEM)] * len(outs),
        scratch_shapes=list(scratch),
        compiler_params=pltpu.CompilerParams(vmem_limit_bytes=vmem * 2**20),
        cost_estimate=pl.CostEstimate(flops=flops, bytes_accessed=2**20, transcendentals=0),
        name=name,
    )(*args)


def mm(a, b, precision=None):
    return lax.dot_general(
        a, b, (((0,), (0,)), ((), ())), precision=precision, preferred_element_type=F32
    )


def mn(a, b):
    return lax.dot_general(
        a, b, (((1,), (0,)), ((), ())), precision=HI, preferred_element_type=F32
    )


def mt(a, b):
    return lax.dot_general(
        a, b, (((1,), (1,)), ((), ())), precision=HI, preferred_element_type=F32
    )


def frame_info(first, rows, table):
    starts, ends, lags = (table[i : i + 1, :].astype(F32) for i in range(3))
    t = (first + lax.broadcasted_iota(jnp.int32, (rows, 1), 0)).astype(F32)
    here = (starts <= t) & (t < ends)
    pick = lambda v: jnp.sum(jnp.where(here, v, 0.0), axis=1, keepdims=True)
    lag = pick(lags)
    ahead = jnp.where(t + lag < pick(ends), 1.0, 0.0)
    behind = jnp.where(t - lag >= pick(starts), 1.0, 0.0)
    return lag, ahead, behind


def pair_count(table):
    starts, ends, lags = (table[i : i + 1, :].astype(F32) for i in range(3))
    return jnp.sum(jnp.maximum(ends - starts - lags, 0.0), axis=1, keepdims=True)


def shifted(window, lag, ahead, behind):
    rows, width = lag.shape[0], window.shape[0]
    off = (
        lax.broadcasted_iota(jnp.int32, (rows, width), 1)
        - lax.broadcasted_iota(jnp.int32, (rows, width), 0)
        - RIM
    ).astype(F32)
    later = jnp.where((off == lag) & (ahead > 0.0), 1.0, 0.0).astype(BF16)
    earlier = jnp.where((off == -lag) & (behind > 0.0), 1.0, 0.0).astype(BF16)
    dims = (((1,), (0,)), ((), ()))
    zp = lax.dot_general(later, window, dims, preferred_element_type=F32)
    zm = lax.dot_general(earlier, window, dims, preferred_element_type=F32)
    return zp.astype(BF16), zm.astype(BF16)


def diag_kernel(pos, table, xp, before, after, mine, theirs, ext, right):
    rows = xp.shape[0]
    ext[0:RIM, :] = before[...]
    ext[RIM : RIM + rows, :] = xp[...]
    ext[RIM + rows :, :] = after[...]
    fill_right(pos, table, ext, right, rows, P_SIZE)
    scale = 1.0 / pair_count(table)
    c = pos[1]
    v = xp[...]
    for half in range(2):
        cols = slice(256 * half, 256 * half + 256)
        d0 = mm(v[:, cols], right[:, :P_SIZE]) * scale
        d1 = mm(v[:, cols], right[:, P_SIZE : 2 * P_SIZE]) + mm(v[:, cols], right[:, 2 * P_SIZE :])
        d1 = d1 * (0.5 * scale)
        r = lax.broadcasted_iota(jnp.int32, d0.shape, 0) + 256 * half
        l = lax.broadcasted_iota(jnp.int32, d0.shape, 1)
        packed = jnp.where(r >= l, d0, d1)
        diag = jnp.sum(jnp.where(r == l, d1, 0.0), axis=1, keepdims=True)
        diag = jnp.broadcast_to(diag, (256, NB))

        @pl.when(c == half)
        def _():
            mine[:, :P_SIZE] = packed
            mine[:, P_SIZE:] = diag

        @pl.when(c != half)
        def _():
            theirs[:, :P_SIZE] = packed
            theirs[:, P_SIZE:] = diag


def fill_right(pos, table, ext, right, rows, n):
    for b in range(0, rows, 256):
        lag, ahead, behind = frame_info(pos[0] + b, 256, table)
        zp, zm = shifted(ext[b : b + 256 + 2 * RIM, :], lag, ahead, behind)
        own = ext[b + RIM : b + RIM + 256, :]
        right[b : b + 256, :n] = own * (0.5 * (ahead + behind)).astype(BF16)
        right[b : b + 256, n : 2 * n] = zp
        right[b : b + 256, 2 * n :] = zm


def cov_kernel(pos, table, x, g0, g1, g2, g3, out, ext, right, sem):
    rows, n = x.shape[0], P_SIZE
    z, col = pos[3], pos[5]
    for wait in (False, True):
        for k, g in enumerate((g0, g1, g2, g3)):
            q = lax.rem(col - k + 4, 4)

            def bring(src, dst, i):
                copy = pltpu.make_async_copy(src, dst, sem.at[k, i])
                copy.wait() if wait else copy.start()

            @pl.when(q == 0)
            def _():
                bring(g.at[0:RIM, :], ext.at[0:RIM, :], 0)
                bring(g.at[RIM : 2 * RIM, :], ext.at[RIM + rows : 2 * RIM + rows, :], 1)
                bring(g.at[2 * RIM : CHUNK, :], ext.at[RIM : RIM + FIRST, :], 2)

            @pl.when(q != 0)
            def _():
                at = pl.multiple_of(RIM + STEP0 + CHUNK * (q - 1), 16)
                bring(g, ext.at[pl.ds(at, CHUNK), :], 0)

    fill_right(pos, table, ext, right, rows, n)
    scale = 1.0 / pair_count(table)
    for zz in range(4):
        left = x[:, 256 * zz : 256 * zz + 256]
        d0 = mm(left, right[:, :n]) * scale
        d1 = mm(left, right[:, n : 2 * n]) + mm(left, right[:, 2 * n :])
        d1 = d1 * (0.5 * scale)
        at = pl.multiple_of(lax.rem(zz - z + 4, 4) * 32, 32)
        for k in range(8):
            out[k, pl.ds(at, 32), :n] = d0[32 * k : 32 * k + 32, :]
            out[k, pl.ds(at, 32), n:] = d1[32 * k : 32 * k + 32, :]


def factor(s):
    n = NB
    groups = [s[8 * i : 8 * i + 8, :] for i in range(n // 8)]
    sub = lax.broadcasted_iota(jnp.int32, (8, n), 0)
    lane = lax.broadcasted_iota(jnp.int32, (8, n), 1)
    for j in range(n // 8):
        r0 = 8 * j
        look = j + 1 < n // 8
        block = (lane >= r0) & (lane < r0 + 8)
        rows = groups[j]
        cols = [jnp.broadcast_to(rows[:, r0 + r : r0 + r + 1], (8, n)) for r in range(8)]
        rows = jnp.where(block, jnp.where(lane - r0 == sub, 1.0, 0.0), rows)
        if look:
            more = groups[j + 1]
            below = [jnp.broadcast_to(more[:, r0 + r : r0 + r + 1], (8, n)) for r in range(8)]
            more = jnp.where(block, 0.0, more)
        for r in range(8):
            rs = lax.rsqrt(cols[r][r : r + 1, :])
            l = cols[r] * rs
            lm = jnp.where(sub > r, l, 0.0)
            row = rows[r : r + 1, :] * rs
            rows = jnp.where(sub == r, row, rows - lm * row)
            if look:
                lq = below[r] * rs
                more = more - lq * row
            for s_ in range(r + 1, 8):
                at = l[s_ : s_ + 1, :]
                cols[s_] = cols[s_] - lm * at
                if look:
                    below[s_] = below[s_] - lq * at
        groups[j] = rows
        if look:
            groups[j + 1] = more
        if j + 2 < n // 8:
            m = n - r0 - 16
            rest = jnp.concatenate(groups[j + 2 :], axis=0)
            lanes = lax.broadcasted_iota(jnp.int32, (m, n), 1)
            rest = jnp.where((lanes >= r0) & (lanes < r0 + 8), 0.0, rest)
            rest = rest - mm(rows, rows, HI)[r0 + 16 :, :]
            for i in range(j + 2, n // 8):
                groups[i] = rest[8 * (i - j - 2) : 8 * (i - j - 1), :]
    return lower_part(jnp.concatenate(groups, axis=0))


def lower_part(v):
    r = lax.broadcasted_iota(jnp.int32, v.shape, 0)
    c = lax.broadcasted_iota(jnp.int32, v.shape, 1)
    return jnp.where(r >= c, v, 0.0)


def unpack_kernel(pos, own, other, w, up):
    c = pos[1]
    r = lax.broadcasted_iota(jnp.int32, (P_SIZE // 2, P_SIZE), 0)
    l = lax.broadcasted_iota(jnp.int32, (P_SIZE // 2, P_SIZE), 1)
    for half in range(2):
        at = slice(256 * half, 256 * half + 256)
        v = jnp.where(c == half, own[:, :P_SIZE], other[:, :P_SIZE])
        d = jnp.where(c == half, own[:, P_SIZE : P_SIZE + 1], other[:, P_SIZE : P_SIZE + 1])
        w[at, :] = v
        up[at, :] = jnp.where(l > r + 256 * half, v, jnp.where(l == r + 256 * half, d, 0.0))
    r = lax.broadcasted_iota(jnp.int32, (NB, NB), 0)
    l = lax.broadcasted_iota(jnp.int32, (NB, NB), 1)
    for o in range(0, P_SIZE, NB):
        s = jnp.where(r >= l, w[o : o + NB, o : o + NB], 0.0)
        w[o : o + NB, o : o + NB] = s + jnp.where(r < l, s.T, 0.0)
    inverse_step(0, w)


def inverse_step(o, w):
    e = o + NB
    t = factor(w[o:e, o:e])
    w[o:e, o:e] = t
    if o:
        w[o:e, :o] = mn(t, w[o:e, :o])
    if e < P_SIZE:
        low = mt(w[e:, o:e], t)
        w[e:, o:e] = -mn(low, t)
        if o:
            w[e:, :o] = w[e:, :o] - mn(low, w[o:e, :o])
        w[e:, e:] = w[e:, e:] - mt(low, low)
    else:
        w[...] = lower_part(w[...])


def inverse_kernel(o, pos, v, w):
    w[...] = v[...]
    inverse_step(o, w)


def whiten_kernel(pos, inv, up, p0, p1, p2, p3, panel, cross, tau, left):
    m = inv[...]
    s = (p0[...] + p1[...]) + (p2[...] + p3[...])
    left[0:32, :] = s[:, :P_SIZE]
    left[32:64, :] = s[:, P_SIZE:]
    rows = inv[pl.ds(pl.multiple_of(pos[2], 16), 16), :]
    u = up[...]
    r = lax.broadcasted_iota(jnp.int32, u.shape, 0)
    l = lax.broadcasted_iota(jnp.int32, u.shape, 1)
    left[64:80, :] = mn(rows, u) + mt(rows, jnp.where(l > r, u, 0.0))
    res = mt(left[...], m)
    panel[0] = res[0:32, :]
    cross[0] = res[32:64, :]
    tau[...] = res[64:80, :]


def swap_core(v, only=None):
    return move(v, lambda z, y, c, w, x: (z, y, 1 - c, w, x) if only is None or (w, x) == only else None)


def exchange(v, axes):
    return lax.all_to_all(v, axes, 0, 0, tiled=True)


def spread(v, axes, n):
    return exchange(jnp.broadcast_to(v[None], (n, *v.shape)), axes)


def together(*values):
    return lax.optimization_barrier(values)


def diag_half(mine, theirs):
    half = (mine + swap_core(theirs, (0, 0))).reshape(4, 64, mine.shape[1])
    return jnp.sum(exchange(half, "y"), axis=0)


def diag_rows(quarter):
    return jnp.sum(exchange(quarter.reshape(4, 16, quarter.shape[1]), "z"), axis=0)


def diag_gather(own):
    half = spread(own, ("y", "z"), 16).reshape(256, own.shape[1])
    return half, swap_core(half)


def body(frames_data, starts, lags):
    tok, width = frames_data.shape
    z, y, c, w, x = (lax.axis_index(a) for a in AXES)
    slab = z * 8 + y * 2 + c
    total = tok * 32
    ends = jnp.concatenate([starts[1:], jnp.array([total], dtype=jnp.int32)])
    table = jnp.stack([starts, ends, lags])
    pos = jnp.stack([slab * tok, c, slab * 16, z, y, x]).astype(jnp.int32)
    panel = frames_data[:, :P_SIZE]

    def step(by):
        def target(z, y, c, w, x):
            i = z * 8 + y * 2 + c + by
            return (i // 8, i // 2 % 4, i % 2, 0, 0) if (w, x) == (0, 0) and 0 <= i < 32 else None
        return target

    behind = move(panel[:RIM], step(-1))
    before = move(panel[tok - RIM :], step(1))

    packed = jax.ShapeDtypeStruct((256, P_SIZE + NB), F32)
    mine, theirs = call(
        diag_kernel, [packed, packed], (pos, table, frames_data, before, behind), "diagonal",
        scratch=[pltpu.VMEM((tok + 2 * RIM, P_SIZE), BF16), pltpu.VMEM((tok, 3 * P_SIZE), BF16)],
        flops=3 * 10**9, block={2: (tok, P_SIZE)},
    )
    theirs, *chunks = together(theirs, *(panel[STEP0 + CHUNK * (k - 1) : STEP0 + CHUNK * k] for k in (2, 1, 3)))
    sent = [
        move(v, lambda z, y, c, w, x: (z, y, c, w, k) if (w, x) == (0, 0) else None)
        for k, v in zip((2, 1, 3), chunks)
    ]
    first = jnp.concatenate([before, behind, panel[:FIRST]], axis=0)
    hold = jnp.where(x == 0, first, sent[0] + sent[1] + sent[2])
    over = move(hold, lambda z, y, c, w, x: (z, y, c, 1, x) if w == 0 else None)
    quarter, over = together(diag_half(mine, theirs), over)
    rows16 = diag_rows(quarter)
    hold = jnp.where(w == 0, hold, over)
    gathered = [hold] + [
        move(hold, lambda z, y, c, w, x: (z, y, c, w, (x + k) % 4)) for k in (1, 2, 3)
    ]
    over = move(rows16, lambda z, y, c, w, x: (z, y, c, 1, 0) if (w, x) == (0, 0) else None)
    over, *gathered = together(over, *gathered)
    own, other = diag_gather(spread(jnp.where(w == 0, rows16, over), "x", 4)[0])
    (part,) = call(
        cov_kernel, [jax.ShapeDtypeStruct((8, 128, 2 * P_SIZE), F32)], (pos, table, frames_data, *gathered), "covariance",
        scratch=[
            pltpu.VMEM((tok + 2 * RIM, P_SIZE), BF16),
            pltpu.VMEM((tok, 3 * P_SIZE), BF16),
            pltpu.SemaphoreType.DMA((4, 3)),
        ],
        flops=5 * 10**9, vmem=20, hbm=(3, 4, 5, 6),
    )
    t = lax.psum_scatter(part.reshape(1024, 2 * P_SIZE), ("y", "c"), scatter_dimension=0, tiled=True)
    rows = [t[:32]] + [
        move(t[32 * k : 32 * k + 32], lambda z, y, c, w, x: ((z + k) % 4, y, c, w, x)) for k in (2, 1, 3)
    ]

    full = jax.ShapeDtypeStruct((P_SIZE, P_SIZE), F32)
    inv, up = call(unpack_kernel, [full, full], (pos, own, other), "factor0", flops=5 * 10**9, vmem=8)
    for o in range(NB, P_SIZE, NB):
        (inv,) = call(functools.partial(inverse_kernel, o), [full], (pos, inv), "factor%d" % o, flops=5 * 10**9, vmem=8)
    own = jax.ShapeDtypeStruct((1, 32, P_SIZE), F32)
    return tuple(
        call(
            whiten_kernel, [own, own, jax.ShapeDtypeStruct((16, P_SIZE), F32)],
            (pos, inv, up, *rows), "whiten", scratch=[pltpu.VMEM((80, P_SIZE), F32)], flops=2 * 10**9,
        )
    )


def solution(mesh):
    split = Mesh(mesh.devices.reshape(SIZES), AXES)
    frames, feat = ("z", "y", "c"), ("w", "x")
    return jax.shard_map(
        body,
        mesh=split,
        in_specs=(P(frames, feat), P(), P()),
        out_specs=(P(feat, frames, None), P(feat, frames, None), P(frames, None)),
        check_vma=False,
    )
```

```python
import functools

import jax
import jax.numpy as jnp
from jax import lax
from jax.experimental import pallas as pl
from jax.experimental.pallas import tpu as pltpu
from jax.sharding import Mesh
from jax.sharding import PartitionSpec as P

P_SIZE = 512
RIM = 16
NB = 128
AHEAD = 3
HI = lax.Precision.HIGHEST
F32 = jnp.float32
BF16 = jnp.bfloat16
AXES = ("z", "y", "c", "w", "x")
SIZES = (4, 4, 2, 2, 4)
CHUNK = 272
FIRST = CHUNK - 2 * RIM
STEP0 = 1024 - 3 * CHUNK


def coords():
    for z in range(4):
        for y in range(4):
            for c in range(2):
                for w in range(2):
                    for x in range(4):
                        yield (z, y, c, w, x)


def flat(p):
    i = 0
    for v, n in zip(p, SIZES):
        i = i * n + v
    return i


def move(value, target):
    pairs = []
    for p in coords():
        q = target(*p)
        if q is not None:
            pairs.append((flat(p), flat(q)))
    return lax.ppermute(value, AXES, pairs)


def call(kernel, outs, args, name, scratch=(), flops=0, vmem=16, hbm=(), block=None, out=pltpu.VMEM):
    specs = [pl.BlockSpec(memory_space=pltpu.VMEM)] * len(args)
    specs[0] = pl.BlockSpec(memory_space=pltpu.SMEM)
    for i in hbm:
        specs[i] = pl.BlockSpec(memory_space=pltpu.HBM)
    for i, shape in (block or {}).items():
        specs[i] = pl.BlockSpec(shape, lambda i: (0, 0))
    return pl.pallas_call(
        kernel,
        grid=(1,),
        out_shape=outs,
        in_specs=specs,
        out_specs=[pl.BlockSpec(memory_space=out)] * len(outs),
        scratch_shapes=list(scratch),
        compiler_params=pltpu.CompilerParams(vmem_limit_bytes=vmem * 2**20),
        cost_estimate=pl.CostEstimate(flops=flops, bytes_accessed=2**20, transcendentals=0),
        name=name,
    )(*args)


def mm(a, b, precision=None):
    return lax.dot_general(
        a, b, (((0,), (0,)), ((), ())), precision=precision, preferred_element_type=F32
    )


def mn(a, b):
    return lax.dot_general(
        a, b, (((1,), (0,)), ((), ())), precision=HI, preferred_element_type=F32
    )


def mt(a, b):
    return lax.dot_general(
        a, b, (((1,), (1,)), ((), ())), precision=HI, preferred_element_type=F32
    )


def frame_info(first, rows, table):
    starts, ends, lags = (table[i : i + 1, :].astype(F32) for i in range(3))
    t = (first + lax.broadcasted_iota(jnp.int32, (rows, 1), 0)).astype(F32)
    here = (starts <= t) & (t < ends)
    pick = lambda v: jnp.sum(jnp.where(here, v, 0.0), axis=1, keepdims=True)
    lag = pick(lags)
    ahead = jnp.where(t + lag < pick(ends), 1.0, 0.0)
    behind = jnp.where(t - lag >= pick(starts), 1.0, 0.0)
    return lag, ahead, behind


def pair_count(table):
    starts, ends, lags = (table[i : i + 1, :].astype(F32) for i in range(3))
    return jnp.sum(jnp.maximum(ends - starts - lags, 0.0), axis=1, keepdims=True)


def shifted(window, lag, ahead, behind):
    rows, width = lag.shape[0], window.shape[0]
    off = (
        lax.broadcasted_iota(jnp.int32, (rows, width), 1)
        - lax.broadcasted_iota(jnp.int32, (rows, width), 0)
        - RIM
    ).astype(F32)
    later = jnp.where((off == lag) & (ahead > 0.0), 1.0, 0.0).astype(BF16)
    earlier = jnp.where((off == -lag) & (behind > 0.0), 1.0, 0.0).astype(BF16)
    dims = (((1,), (0,)), ((), ()))
    zp = lax.dot_general(later, window, dims, preferred_element_type=F32)
    zm = lax.dot_general(earlier, window, dims, preferred_element_type=F32)
    return zp.astype(BF16), zm.astype(BF16)


def diag_kernel(pos, table, xp, before, after, mine, theirs, ext, right):
    rows = xp.shape[0]
    ext[0:RIM, :] = before[...]
    ext[RIM : RIM + rows, :] = xp[...]
    ext[RIM + rows :, :] = after[...]
    fill_right(pos, table, ext, right, rows, P_SIZE)
    scale = 1.0 / pair_count(table)
    c = pos[1]
    v = xp[...]
    for half in range(2):
        cols = slice(256 * half, 256 * half + 256)
        d0 = mm(v[:, cols], right[:, :P_SIZE]) * scale
        d1 = mm(v[:, cols], right[:, P_SIZE : 2 * P_SIZE]) + mm(v[:, cols], right[:, 2 * P_SIZE :])
        d1 = d1 * (0.5 * scale)
        r = lax.broadcasted_iota(jnp.int32, d0.shape, 0) + 256 * half
        l = lax.broadcasted_iota(jnp.int32, d0.shape, 1)
        packed = jnp.where(r >= l, d0, d1)
        diag = jnp.sum(jnp.where(r == l, d1, 0.0), axis=1, keepdims=True)
        diag = jnp.broadcast_to(diag, (256, NB))

        @pl.when(c == half)
        def _():
            mine[:, :P_SIZE] = packed
            mine[:, P_SIZE:] = diag

        @pl.when(c != half)
        def _():
            theirs[:, :P_SIZE] = packed
            theirs[:, P_SIZE:] = diag


def fill_right(pos, table, ext, right, rows, n):
    for b in range(0, rows, 256):
        lag, ahead, behind = frame_info(pos[0] + b, 256, table)
        zp, zm = shifted(ext[b : b + 256 + 2 * RIM, :], lag, ahead, behind)
        own = ext[b + RIM : b + RIM + 256, :]
        right[b : b + 256, :n] = own * (0.5 * (ahead + behind)).astype(BF16)
        right[b : b + 256, n : 2 * n] = zp
        right[b : b + 256, 2 * n :] = zm


def select_kernel(pos, table, g0, g1, g2, g3, right, ext, sem):
    rows, n = right.shape[0], P_SIZE
    col = pos[5]
    for wait in (False, True):
        for k, g in enumerate((g0, g1, g2, g3)):
            q = lax.rem(col - k + 4, 4)

            def bring(src, dst, i):
                copy = pltpu.make_async_copy(src, dst, sem.at[k, i])
                copy.wait() if wait else copy.start()

            @pl.when(q == 0)
            def _():
                bring(g.at[0:RIM, :], ext.at[0:RIM, :], 0)
                bring(g.at[RIM : 2 * RIM, :], ext.at[RIM + rows : 2 * RIM + rows, :], 1)
                bring(g.at[2 * RIM : CHUNK, :], ext.at[RIM : RIM + FIRST, :], 2)

            @pl.when(q != 0)
            def _():
                at = pl.multiple_of(RIM + STEP0 + CHUNK * (q - 1), 16)
                bring(g, ext.at[pl.ds(at, CHUNK), :], 0)

    fill_right(pos, table, ext, right, rows, n)


def cov_kernel(pos, table, x, right, out, done, sent):
    n = P_SIZE
    z = pos[3]
    scale = 1.0 / pair_count(table)
    leave = []
    for zz in range(4):
        left = x[:, 256 * zz : 256 * zz + 256]
        d0 = mm(left, right[:, :n]) * scale
        d1 = mm(left, right[:, n : 2 * n]) + mm(left, right[:, 2 * n :])
        d1 = d1 * (0.5 * scale)
        at = pl.multiple_of(lax.rem(zz - z + 4, 4) * 32, 32)
        if zz >= 2:
            leave[zz - 2].wait()
        for k in range(8):
            done[zz % 2, k, :, :n] = d0[32 * k : 32 * k + 32, :]
            done[zz % 2, k, :, n:] = d1[32 * k : 32 * k + 32, :]
        leave.append(pltpu.make_async_copy(done.at[zz % 2], out.at[:, pl.ds(at, 32), :], sent.at[zz % 2]))
        leave[zz].start()
    leave[2].wait()
    leave[3].wait()


def parts(v):
    hi = v.astype(BF16)
    rest = v - hi.astype(F32)
    mid = rest.astype(BF16)
    return hi, mid, (rest - mid.astype(F32)).astype(BF16)


def factor(s):
    n = NB
    groups = [s[8 * i : 8 * i + 8, :] for i in range(n // 8)]
    sub = lax.broadcasted_iota(jnp.int32, (8, n), 0)
    lane = lax.broadcasted_iota(jnp.int32, (8, n), 1)
    for j in range(n // 8):
        r0 = 8 * j
        block = (lane >= r0) & (lane < r0 + 8)
        columns = lambda v: [jnp.broadcast_to(v[:, r0 + r : r0 + r + 1], (8, n)) for r in range(8)]
        rows = groups[j]
        cols = columns(rows)
        rows = jnp.where(block, jnp.where(lane - r0 == sub, 1.0, 0.0), rows)
        far = min(j + 1 + AHEAD, n // 8)
        near = range(j + 1, far)
        below = {k: columns(groups[k]) for k in near}
        more = {k: jnp.where(block, 0.0, groups[k]) for k in near}
        for r in range(8):
            rs = lax.rsqrt(cols[r][r : r + 1, :])
            l = cols[r] * rs
            lm = jnp.where(sub > r, l, 0.0)
            row = rows[r : r + 1, :] * rs
            rows = jnp.where(sub == r, row, rows - lm * row)
            lq = {k: below[k][r] * rs for k in near}
            for k in near:
                more[k] = more[k] - lq[k] * row
            for t in range(r + 1, 8):
                at = l[t : t + 1, :]
                cols[t] = cols[t] - lm * at
                for k in near:
                    below[k][t] = below[k][t] - lq[k] * at
        groups[j] = rows
        for k in near:
            groups[k] = more[k]
        if far < n // 8:
            rest = jnp.concatenate(groups[far:], axis=0)
            lanes = lax.broadcasted_iota(jnp.int32, rest.shape, 1)
            rest = jnp.where((lanes >= r0) & (lanes < r0 + 8), 0.0, rest)
            hi, mid, lo = parts(rows)
            left = jnp.concatenate([hi, hi, mid, hi, mid, lo], axis=0)
            right = jnp.concatenate([hi, mid, hi, lo, mid, hi], axis=0)
            rest = rest - mm(left, right)[8 * far :, :]
            for k in range(far, n // 8):
                groups[k] = rest[8 * (k - far) : 8 * (k - far) + 8, :]
    return lower_part(jnp.concatenate(groups, axis=0))


def lower_part(v):
    r = lax.broadcasted_iota(jnp.int32, v.shape, 0)
    c = lax.broadcasted_iota(jnp.int32, v.shape, 1)
    return jnp.where(r >= c, v, 0.0)


def unpack_kernel(pos, own, other, w, up):
    c = pos[1]
    r = lax.broadcasted_iota(jnp.int32, (P_SIZE // 2, P_SIZE), 0)
    l = lax.broadcasted_iota(jnp.int32, (P_SIZE // 2, P_SIZE), 1)
    for half in range(2):
        at = slice(256 * half, 256 * half + 256)
        v = jnp.where(c == half, own[:, :P_SIZE], other[:, :P_SIZE])
        d = jnp.where(c == half, own[:, P_SIZE : P_SIZE + 1], other[:, P_SIZE : P_SIZE + 1])
        w[at, :] = v
        up[at, :] = jnp.where(l > r + 256 * half, v, jnp.where(l == r + 256 * half, d, 0.0))
    r = lax.broadcasted_iota(jnp.int32, (NB, NB), 0)
    l = lax.broadcasted_iota(jnp.int32, (NB, NB), 1)
    for o in range(0, P_SIZE, NB):
        s = jnp.where(r >= l, w[o : o + NB, o : o + NB], 0.0)
        w[o : o + NB, o : o + NB] = s + jnp.where(r < l, s.T, 0.0)
    inverse_step(0, w)


def inverse_step(o, w):
    e = o + NB
    t = factor(w[o:e, o:e])
    w[o:e, o:e] = t
    if o:
        w[o:e, :o] = mn(t, w[o:e, :o])
    if e < P_SIZE:
        low = mt(w[e:, o:e], t)
        w[e:, o:e] = -mn(low, t)
        if o:
            w[e:, :o] = w[e:, :o] - mn(low, w[o:e, :o])
        w[e:, e:] = w[e:, e:] - mt(low, low)
    else:
        w[...] = lower_part(w[...])


def inverse_kernel(o, pos, v, w):
    w[...] = v[...]
    inverse_step(o, w)


def whiten_kernel(pos, inv, up, p0, p1, p2, p3, panel, cross, tau, left):
    m = inv[...]
    s = (p0[...] + p1[...]) + (p2[...] + p3[...])
    left[0:32, :] = s[:, :P_SIZE]
    left[32:64, :] = s[:, P_SIZE:]
    rows = inv[pl.ds(pl.multiple_of(pos[2], 16), 16), :]
    u = up[...]
    r = lax.broadcasted_iota(jnp.int32, u.shape, 0)
    l = lax.broadcasted_iota(jnp.int32, u.shape, 1)
    left[64:80, :] = mn(rows, u) + mt(rows, jnp.where(l > r, u, 0.0))
    res = mt(left[...], m)
    panel[0] = res[0:32, :]
    cross[0] = res[32:64, :]
    tau[...] = res[64:80, :]


def swap_core(v, only=None):
    return move(v, lambda z, y, c, w, x: (z, y, 1 - c, w, x) if only is None or (w, x) == only else None)


def exchange(v, axes):
    return lax.all_to_all(v, axes, 0, 0, tiled=True)


def spread(v, axes, n):
    return exchange(jnp.broadcast_to(v[None], (n, *v.shape)), axes)


def together(*values):
    return lax.optimization_barrier(values)


def diag_half(mine, theirs):
    half = (mine + swap_core(theirs, (0, 0))).reshape(4, 64, mine.shape[1])
    return jnp.sum(exchange(half, "y"), axis=0)


def diag_rows(quarter):
    return jnp.sum(exchange(quarter.reshape(4, 16, quarter.shape[1]), "z"), axis=0)


def diag_gather(own):
    half = spread(own, ("y", "z"), 16).reshape(256, own.shape[1])
    return half, swap_core(half)


def body(frames_data, starts, lags):
    tok, width = frames_data.shape
    z, y, c, w, x = (lax.axis_index(a) for a in AXES)
    slab = z * 8 + y * 2 + c
    total = tok * 32
    ends = jnp.concatenate([starts[1:], jnp.array([total], dtype=jnp.int32)])
    table = jnp.stack([starts, ends, lags])
    pos = jnp.stack([slab * tok, c, slab * 16, z, y, x]).astype(jnp.int32)
    panel = frames_data[:, :P_SIZE]

    def step(by):
        def target(z, y, c, w, x):
            i = z * 8 + y * 2 + c + by
            return (i // 8, i // 2 % 4, i % 2, 0, 0) if (w, x) == (0, 0) and 0 <= i < 32 else None
        return target

    behind = move(panel[:RIM], step(-1))
    before = move(panel[tok - RIM :], step(1))

    packed = jax.ShapeDtypeStruct((256, P_SIZE + NB), F32)
    mine, theirs = call(
        diag_kernel, [packed, packed], (pos, table, frames_data, before, behind), "diagonal",
        scratch=[pltpu.VMEM((tok + 2 * RIM, P_SIZE), BF16), pltpu.VMEM((tok, 3 * P_SIZE), BF16)],
        flops=3 * 10**9, block={2: (tok, P_SIZE)},
    )
    theirs, *chunks = together(theirs, *(panel[STEP0 + CHUNK * (k - 1) : STEP0 + CHUNK * k] for k in (2, 1, 3)))
    sent = [
        move(v, lambda z, y, c, w, x: (z, y, c, w, k) if (w, x) == (0, 0) else None)
        for k, v in zip((2, 1, 3), chunks)
    ]
    first = jnp.concatenate([before, behind, panel[:FIRST]], axis=0)
    hold = jnp.where(x == 0, first, sent[0] + sent[1] + sent[2])
    over = move(hold, lambda z, y, c, w, x: (z, y, c, 1, x) if w == 0 else None)
    quarter, over = together(diag_half(mine, theirs), over)
    rows16 = diag_rows(quarter)
    hold = jnp.where(w == 0, hold, over)
    gathered = [hold] + [
        move(hold, lambda z, y, c, w, x: (z, y, c, w, (x + k) % 4)) for k in (1, 2, 3)
    ]
    rows16, *gathered = together(rows16, *gathered)
    (right,) = call(
        select_kernel, [jax.ShapeDtypeStruct((tok, 3 * P_SIZE), BF16)], (pos, table, *gathered), "select",
        scratch=[pltpu.VMEM((tok + 2 * RIM, P_SIZE), BF16), pltpu.SemaphoreType.DMA((4, 3))],
        flops=2 * 10**9, hbm=(2, 3, 4, 5),
    )
    rows16, right = together(spread(rows16, ("w", "x"), 8)[0], right)
    own, other = diag_gather(rows16)
    (part,) = call(
        cov_kernel, [jax.ShapeDtypeStruct((8, 128, 2 * P_SIZE), F32)], (pos, table, frames_data, right), "covariance",
        scratch=[pltpu.VMEM((2, 8, 32, 2 * P_SIZE), F32), pltpu.SemaphoreType.DMA((2,))],
        flops=4 * 10**9, vmem=56, out=pltpu.HBM,
    )
    t = lax.psum_scatter(part.reshape(1024, 2 * P_SIZE), ("y", "c"), scatter_dimension=0, tiled=True)
    rows = [t[:32]] + [
        move(t[32 * k : 32 * k + 32], lambda z, y, c, w, x: ((z + k) % 4, y, c, w, x)) for k in (2, 1, 3)
    ]

    full = jax.ShapeDtypeStruct((P_SIZE, P_SIZE), F32)
    inv, up = call(unpack_kernel, [full, full], (pos, own, other), "factor0", flops=5 * 10**9, vmem=8)
    for o in range(NB, P_SIZE, NB):
        (inv,) = call(functools.partial(inverse_kernel, o), [full], (pos, inv), "factor%d" % o, flops=5 * 10**9, vmem=8)
    own = jax.ShapeDtypeStruct((1, 32, P_SIZE), F32)
    return tuple(
        call(
            whiten_kernel, [own, own, jax.ShapeDtypeStruct((16, P_SIZE), F32)],
            (pos, inv, up, *rows), "whiten", scratch=[pltpu.VMEM((80, P_SIZE), F32)], flops=2 * 10**9,
        )
    )


def solution(mesh):
    split = Mesh(mesh.devices.reshape(SIZES), AXES)
    frames, feat = ("z", "y", "c"), ("w", "x")
    return jax.shard_map(
        body,
        mesh=split,
        in_specs=(P(frames, feat), P(), P()),
        out_specs=(P(feat, frames, None), P(feat, frames, None), P(frames, None)),
        check_vma=False,
    )
```

```python
import functools

import jax
import jax.numpy as jnp
from jax import lax
from jax.experimental import pallas as pl
from jax.experimental.pallas import tpu as pltpu
from jax.sharding import Mesh
from jax.sharding import PartitionSpec as P

P_SIZE = 512
RIM = 16
NB = 128
AHEAD = 3
HI = lax.Precision.HIGHEST
F32 = jnp.float32
BF16 = jnp.bfloat16
AXES = ("z", "y", "c", "w", "x")
SIZES = (4, 4, 2, 2, 4)
CHUNK = 272
FIRST = CHUNK - 2 * RIM
STEP0 = 1024 - 3 * CHUNK


def coords():
    for z in range(4):
        for y in range(4):
            for c in range(2):
                for w in range(2):
                    for x in range(4):
                        yield (z, y, c, w, x)


def flat(p):
    i = 0
    for v, n in zip(p, SIZES):
        i = i * n + v
    return i


def move(value, target):
    pairs = []
    for p in coords():
        q = target(*p)
        if q is not None:
            pairs.append((flat(p), flat(q)))
    return lax.ppermute(value, AXES, pairs)


def call(kernel, outs, args, name, scratch=(), flops=0, vmem=16, hbm=(), block=None):
    specs = [pl.BlockSpec(memory_space=pltpu.VMEM)] * len(args)
    specs[0] = pl.BlockSpec(memory_space=pltpu.SMEM)
    for i in hbm:
        specs[i] = pl.BlockSpec(memory_space=pltpu.HBM)
    for i, shape in (block or {}).items():
        specs[i] = pl.BlockSpec(shape, lambda i: (0, 0))
    return pl.pallas_call(
        kernel,
        grid=(1,),
        out_shape=outs,
        in_specs=specs,
        out_specs=[pl.BlockSpec(memory_space=pltpu.VMEM)] * len(outs),
        scratch_shapes=list(scratch),
        compiler_params=pltpu.CompilerParams(vmem_limit_bytes=vmem * 2**20),
        cost_estimate=pl.CostEstimate(flops=flops, bytes_accessed=2**20, transcendentals=0),
        name=name,
    )(*args)


def mm(a, b, precision=None):
    return lax.dot_general(
        a, b, (((0,), (0,)), ((), ())), precision=precision, preferred_element_type=F32
    )


def mn(a, b):
    return lax.dot_general(
        a, b, (((1,), (0,)), ((), ())), precision=HI, preferred_element_type=F32
    )


def mt(a, b):
    return lax.dot_general(
        a, b, (((1,), (1,)), ((), ())), precision=HI, preferred_element_type=F32
    )


def frame_info(first, rows, table):
    starts, ends, lags = (table[i : i + 1, :].astype(F32) for i in range(3))
    t = (first + lax.broadcasted_iota(jnp.int32, (rows, 1), 0)).astype(F32)
    here = (starts <= t) & (t < ends)
    pick = lambda v: jnp.sum(jnp.where(here, v, 0.0), axis=1, keepdims=True)
    lag = pick(lags)
    ahead = jnp.where(t + lag < pick(ends), 1.0, 0.0)
    behind = jnp.where(t - lag >= pick(starts), 1.0, 0.0)
    return lag, ahead, behind


def pair_count(table):
    starts, ends, lags = (table[i : i + 1, :].astype(F32) for i in range(3))
    return jnp.sum(jnp.maximum(ends - starts - lags, 0.0), axis=1, keepdims=True)


def shifted(window, lag, ahead, behind):
    rows, width = lag.shape[0], window.shape[0]
    off = (
        lax.broadcasted_iota(jnp.int32, (rows, width), 1)
        - lax.broadcasted_iota(jnp.int32, (rows, width), 0)
        - RIM
    ).astype(F32)
    later = jnp.where((off == lag) & (ahead > 0.0), 1.0, 0.0).astype(BF16)
    earlier = jnp.where((off == -lag) & (behind > 0.0), 1.0, 0.0).astype(BF16)
    dims = (((1,), (0,)), ((), ()))
    zp = lax.dot_general(later, window, dims, preferred_element_type=F32)
    zm = lax.dot_general(earlier, window, dims, preferred_element_type=F32)
    return zp.astype(BF16), zm.astype(BF16)


def diag_kernel(pos, table, xp, before, after, mine, theirs, ext, right):
    rows = xp.shape[0]
    ext[0:RIM, :] = before[...]
    ext[RIM : RIM + rows, :] = xp[...]
    ext[RIM + rows :, :] = after[...]
    fill_right(pos, table, ext, right, rows, P_SIZE)
    scale = 1.0 / pair_count(table)
    c = pos[1]
    v = xp[...]
    for half in range(2):
        cols = slice(256 * half, 256 * half + 256)
        d0 = mm(v[:, cols], right[:, :P_SIZE]) * scale
        d1 = mm(v[:, cols], right[:, P_SIZE : 2 * P_SIZE]) + mm(v[:, cols], right[:, 2 * P_SIZE :])
        d1 = d1 * (0.5 * scale)
        r = lax.broadcasted_iota(jnp.int32, d0.shape, 0) + 256 * half
        l = lax.broadcasted_iota(jnp.int32, d0.shape, 1)
        packed = jnp.where(r >= l, d0, d1)
        diag = jnp.sum(jnp.where(r == l, d1, 0.0), axis=1, keepdims=True)
        diag = jnp.broadcast_to(diag, (256, NB))

        @pl.when(c == half)
        def _():
            mine[:, :P_SIZE] = packed
            mine[:, P_SIZE:] = diag

        @pl.when(c != half)
        def _():
            theirs[:, :P_SIZE] = packed
            theirs[:, P_SIZE:] = diag


def fill_right(pos, table, ext, right, rows, n):
    for b in range(0, rows, 256):
        lag, ahead, behind = frame_info(pos[0] + b, 256, table)
        zp, zm = shifted(ext[b : b + 256 + 2 * RIM, :], lag, ahead, behind)
        own = ext[b + RIM : b + RIM + 256, :]
        right[b : b + 256, :n] = own * (0.5 * (ahead + behind)).astype(BF16)
        right[b : b + 256, n : 2 * n] = zp
        right[b : b + 256, 2 * n :] = zm


def cov_kernel(pos, table, x, g0, g1, g2, g3, out, ext, right, sem):
    rows, n = x.shape[0], P_SIZE
    z, col = pos[3], pos[5]
    for wait in (False, True):
        for k, g in enumerate((g0, g1, g2, g3)):
            q = lax.rem(col - k + 4, 4)

            def bring(src, dst, i):
                copy = pltpu.make_async_copy(src, dst, sem.at[k, i])
                copy.wait() if wait else copy.start()

            @pl.when(q == 0)
            def _():
                bring(g.at[0:RIM, :], ext.at[0:RIM, :], 0)
                bring(g.at[RIM : 2 * RIM, :], ext.at[RIM + rows : 2 * RIM + rows, :], 1)
                bring(g.at[2 * RIM : CHUNK, :], ext.at[RIM : RIM + FIRST, :], 2)

            @pl.when(q != 0)
            def _():
                at = pl.multiple_of(RIM + STEP0 + CHUNK * (q - 1), 16)
                bring(g, ext.at[pl.ds(at, CHUNK), :], 0)

    fill_right(pos, table, ext, right, rows, n)
    scale = 1.0 / pair_count(table)
    for zz in range(4):
        left = x[:, 256 * zz : 256 * zz + 256]
        d0 = mm(left, right[:, :n]) * scale
        d1 = mm(left, right[:, n : 2 * n]) + mm(left, right[:, 2 * n :])
        d1 = d1 * (0.5 * scale)
        at = pl.multiple_of(lax.rem(zz - z + 4, 4) * 32, 32)
        for k in range(8):
            out[k, pl.ds(at, 32), :n] = d0[32 * k : 32 * k + 32, :]
            out[k, pl.ds(at, 32), n:] = d1[32 * k : 32 * k + 32, :]


def parts(v):
    hi = v.astype(BF16)
    rest = v - hi.astype(F32)
    mid = rest.astype(BF16)
    return hi, mid, (rest - mid.astype(F32)).astype(BF16)


def factor(s):
    n = NB
    groups = [s[8 * i : 8 * i + 8, :] for i in range(n // 8)]
    sub = lax.broadcasted_iota(jnp.int32, (8, n), 0)
    lane = lax.broadcasted_iota(jnp.int32, (8, n), 1)
    for j in range(n // 8):
        r0 = 8 * j
        block = (lane >= r0) & (lane < r0 + 8)
        columns = lambda v: [jnp.broadcast_to(v[:, r0 + r : r0 + r + 1], (8, n)) for r in range(8)]
        rows = groups[j]
        cols = columns(rows)
        rows = jnp.where(block, jnp.where(lane - r0 == sub, 1.0, 0.0), rows)
        far = min(j + 1 + AHEAD, n // 8)
        near = range(j + 1, far)
        below = {k: columns(groups[k]) for k in near}
        more = {k: jnp.where(block, 0.0, groups[k]) for k in near}
        for r in range(8):
            rs = lax.rsqrt(cols[r][r : r + 1, :])
            l = cols[r] * rs
            lm = jnp.where(sub > r, l, 0.0)
            row = rows[r : r + 1, :] * rs
            rows = jnp.where(sub == r, row, rows - lm * row)
            lq = {k: below[k][r] * rs for k in near}
            for k in near:
                more[k] = more[k] - lq[k] * row
            for t in range(r + 1, 8):
                at = l[t : t + 1, :]
                cols[t] = cols[t] - lm * at
                for k in near:
                    below[k][t] = below[k][t] - lq[k] * at
        groups[j] = rows
        for k in near:
            groups[k] = more[k]
        if far < n // 8:
            rest = jnp.concatenate(groups[far:], axis=0)
            lanes = lax.broadcasted_iota(jnp.int32, rest.shape, 1)
            rest = jnp.where((lanes >= r0) & (lanes < r0 + 8), 0.0, rest)
            hi, mid, lo = parts(rows)
            left = jnp.concatenate([hi, hi, mid, hi, mid, lo], axis=0)
            right = jnp.concatenate([hi, mid, hi, lo, mid, hi], axis=0)
            rest = rest - mm(left, right)[8 * far :, :]
            for k in range(far, n // 8):
                groups[k] = rest[8 * (k - far) : 8 * (k - far) + 8, :]
    return lower_part(jnp.concatenate(groups, axis=0))


def lower_part(v):
    r = lax.broadcasted_iota(jnp.int32, v.shape, 0)
    c = lax.broadcasted_iota(jnp.int32, v.shape, 1)
    return jnp.where(r >= c, v, 0.0)


def unpack_kernel(pos, own, other, w, up):
    c = pos[1]
    r = lax.broadcasted_iota(jnp.int32, (P_SIZE // 2, P_SIZE), 0)
    l = lax.broadcasted_iota(jnp.int32, (P_SIZE // 2, P_SIZE), 1)
    for half in range(2):
        at = slice(256 * half, 256 * half + 256)
        v = jnp.where(c == half, own[:, :P_SIZE], other[:, :P_SIZE])
        d = jnp.where(c == half, own[:, P_SIZE : P_SIZE + 1], other[:, P_SIZE : P_SIZE + 1])
        w[at, :] = v
        up[at, :] = jnp.where(l > r + 256 * half, v, jnp.where(l == r + 256 * half, d, 0.0))
    r = lax.broadcasted_iota(jnp.int32, (NB, NB), 0)
    l = lax.broadcasted_iota(jnp.int32, (NB, NB), 1)
    for o in range(0, P_SIZE, NB):
        s = jnp.where(r >= l, w[o : o + NB, o : o + NB], 0.0)
        w[o : o + NB, o : o + NB] = s + jnp.where(r < l, s.T, 0.0)
    inverse_step(0, w)


def inverse_step(o, w):
    e = o + NB
    t = factor(w[o:e, o:e])
    w[o:e, o:e] = t
    if o:
        w[o:e, :o] = mn(t, w[o:e, :o])
    if e < P_SIZE:
        low = mt(w[e:, o:e], t)
        w[e:, o:e] = -mn(low, t)
        if o:
            w[e:, :o] = w[e:, :o] - mn(low, w[o:e, :o])
        w[e:, e:] = w[e:, e:] - mt(low, low)
    else:
        w[...] = lower_part(w[...])


def inverse_kernel(o, pos, v, w):
    w[...] = v[...]
    inverse_step(o, w)


def whiten_kernel(pos, inv, up, p0, p1, p2, p3, panel, cross, tau, left):
    m = inv[...]
    s = (p0[...] + p1[...]) + (p2[...] + p3[...])
    left[0:32, :] = s[:, :P_SIZE]
    left[32:64, :] = s[:, P_SIZE:]
    rows = inv[pl.ds(pl.multiple_of(pos[2], 16), 16), :]
    u = up[...]
    r = lax.broadcasted_iota(jnp.int32, u.shape, 0)
    l = lax.broadcasted_iota(jnp.int32, u.shape, 1)
    left[64:80, :] = mn(rows, u) + mt(rows, jnp.where(l > r, u, 0.0))
    res = mt(left[...], m)
    panel[0] = res[0:32, :]
    cross[0] = res[32:64, :]
    tau[...] = res[64:80, :]


def swap_core(v, only=None):
    return move(v, lambda z, y, c, w, x: (z, y, 1 - c, w, x) if only is None or (w, x) == only else None)


def exchange(v, axes):
    return lax.all_to_all(v, axes, 0, 0, tiled=True)


def spread(v, axes, n):
    return exchange(jnp.broadcast_to(v[None], (n, *v.shape)), axes)


def together(*values):
    return lax.optimization_barrier(values)


def diag_half(mine, theirs):
    half = (mine + swap_core(theirs, (0, 0))).reshape(4, 64, mine.shape[1])
    return jnp.sum(exchange(half, "y"), axis=0)


def diag_rows(quarter):
    return jnp.sum(exchange(quarter.reshape(4, 16, quarter.shape[1]), "z"), axis=0)


def diag_gather(own):
    half = spread(own, ("y", "z"), 16).reshape(256, own.shape[1])
    return half, swap_core(half)


def body(frames_data, starts, lags):
    tok, width = frames_data.shape
    z, y, c, w, x = (lax.axis_index(a) for a in AXES)
    slab = z * 8 + y * 2 + c
    total = tok * 32
    ends = jnp.concatenate([starts[1:], jnp.array([total], dtype=jnp.int32)])
    table = jnp.stack([starts, ends, lags])
    pos = jnp.stack([slab * tok, c, slab * 16, z, y, x]).astype(jnp.int32)
    panel = frames_data[:, :P_SIZE]

    def step(by):
        def target(z, y, c, w, x):
            i = z * 8 + y * 2 + c + by
            return (i // 8, i // 2 % 4, i % 2, 0, 0) if (w, x) == (0, 0) and 0 <= i < 32 else None
        return target

    behind = move(panel[:RIM], step(-1))
    before = move(panel[tok - RIM :], step(1))

    packed = jax.ShapeDtypeStruct((256, P_SIZE + NB), F32)
    mine, theirs = call(
        diag_kernel, [packed, packed], (pos, table, frames_data, before, behind), "diagonal",
        scratch=[pltpu.VMEM((tok + 2 * RIM, P_SIZE), BF16), pltpu.VMEM((tok, 3 * P_SIZE), BF16)],
        flops=3 * 10**9, block={2: (tok, P_SIZE)},
    )
    theirs, *chunks = together(theirs, *(panel[STEP0 + CHUNK * (k - 1) : STEP0 + CHUNK * k] for k in (2, 1, 3)))
    sent = [
        move(v, lambda z, y, c, w, x: (z, y, c, w, k) if (w, x) == (0, 0) else None)
        for k, v in zip((2, 1, 3), chunks)
    ]
    first = jnp.concatenate([before, behind, panel[:FIRST]], axis=0)
    hold = jnp.where(x == 0, first, sent[0] + sent[1] + sent[2])
    over = move(hold, lambda z, y, c, w, x: (z, y, c, 1, x) if w == 0 else None)
    rows16 = diag_rows(diag_half(mine, theirs))
    hold = jnp.where(w == 0, hold, over)
    gathered = [hold] + [
        move(hold, lambda z, y, c, w, x: (z, y, c, w, (x + k) % 4)) for k in (1, 2, 3)
    ]
    over = move(rows16, lambda z, y, c, w, x: (z, y, c, 1, 0) if (w, x) == (0, 0) else None)
    over, *gathered = together(over, *gathered)
    rows16 = jnp.where(w == 0, rows16, over)
    copies = [
        move(rows16, lambda z, y, c, w, x: (z, y, c, w, k) if x == 0 else None) for k in (2, 1, 3)
    ]
    rows16 = jnp.where(x == 0, rows16, copies[0] + copies[1] + copies[2])
    own, other = diag_gather(rows16)
    (part,) = call(
        cov_kernel, [jax.ShapeDtypeStruct((8, 128, 2 * P_SIZE), F32)], (pos, table, frames_data, *gathered), "covariance",
        scratch=[
            pltpu.VMEM((tok + 2 * RIM, P_SIZE), BF16),
            pltpu.VMEM((tok, 3 * P_SIZE), BF16),
            pltpu.SemaphoreType.DMA((4, 3)),
        ],
        flops=5 * 10**9, vmem=20, hbm=(3, 4, 5, 6),
    )
    t = lax.psum_scatter(part.reshape(1024, 2 * P_SIZE), ("y", "c"), scatter_dimension=0, tiled=True)
    rows = [t[:32]] + [
        move(t[32 * k : 32 * k + 32], lambda z, y, c, w, x: ((z + k) % 4, y, c, w, x)) for k in (2, 1, 3)
    ]

    full = jax.ShapeDtypeStruct((P_SIZE, P_SIZE), F32)
    inv, up = call(unpack_kernel, [full, full], (pos, own, other), "factor0", flops=5 * 10**9, vmem=8)
    for o in range(NB, P_SIZE, NB):
        (inv,) = call(functools.partial(inverse_kernel, o), [full], (pos, inv), "factor%d" % o, flops=5 * 10**9, vmem=8)
    own = jax.ShapeDtypeStruct((1, 32, P_SIZE), F32)
    return tuple(
        call(
            whiten_kernel, [own, own, jax.ShapeDtypeStruct((16, P_SIZE), F32)],
            (pos, inv, up, *rows), "whiten", scratch=[pltpu.VMEM((80, P_SIZE), F32)], flops=2 * 10**9,
        )
    )


def solution(mesh):
    split = Mesh(mesh.devices.reshape(SIZES), AXES)
    frames, feat = ("z", "y", "c"), ("w", "x")
    return jax.shard_map(
        body,
        mesh=split,
        in_specs=(P(frames, feat), P(), P()),
        out_specs=(P(feat, frames, None), P(feat, frames, None), P(frames, None)),
        check_vma=False,
    )
```

```python
import functools

import jax
import jax.numpy as jnp
from jax import lax
from jax.experimental import pallas as pl
from jax.experimental.pallas import tpu as pltpu
from jax.sharding import Mesh
from jax.sharding import PartitionSpec as P

P_SIZE = 512
RIM = 16
NB = 128
AHEAD = 3
HI = lax.Precision.HIGHEST
F32 = jnp.float32
BF16 = jnp.bfloat16
AXES = ("z", "y", "c", "w", "x")
SIZES = (4, 4, 2, 2, 4)
CHUNK = 272
FIRST = CHUNK - 2 * RIM
STEP0 = 1024 - 3 * CHUNK


def coords():
    for z in range(4):
        for y in range(4):
            for c in range(2):
                for w in range(2):
                    for x in range(4):
                        yield (z, y, c, w, x)


def flat(p):
    i = 0
    for v, n in zip(p, SIZES):
        i = i * n + v
    return i


def move(value, target):
    pairs = []
    for p in coords():
        q = target(*p)
        if q is not None:
            pairs.append((flat(p), flat(q)))
    return lax.ppermute(value, AXES, pairs)


def call(kernel, outs, args, name, scratch=(), flops=0, vmem=16, hbm=(), block=None):
    specs = [pl.BlockSpec(memory_space=pltpu.VMEM)] * len(args)
    specs[0] = pl.BlockSpec(memory_space=pltpu.SMEM)
    for i in hbm:
        specs[i] = pl.BlockSpec(memory_space=pltpu.HBM)
    for i, shape in (block or {}).items():
        specs[i] = pl.BlockSpec(shape, lambda i: (0, 0))
    return pl.pallas_call(
        kernel,
        grid=(1,),
        out_shape=outs,
        in_specs=specs,
        out_specs=[pl.BlockSpec(memory_space=pltpu.VMEM)] * len(outs),
        scratch_shapes=list(scratch),
        compiler_params=pltpu.CompilerParams(vmem_limit_bytes=vmem * 2**20),
        cost_estimate=pl.CostEstimate(flops=flops, bytes_accessed=2**20, transcendentals=0),
        name=name,
    )(*args)


def mm(a, b, precision=None):
    return lax.dot_general(
        a, b, (((0,), (0,)), ((), ())), precision=precision, preferred_element_type=F32
    )


def mn(a, b):
    return lax.dot_general(
        a, b, (((1,), (0,)), ((), ())), precision=HI, preferred_element_type=F32
    )


def mt(a, b):
    return lax.dot_general(
        a, b, (((1,), (1,)), ((), ())), precision=HI, preferred_element_type=F32
    )


def frame_info(first, rows, table):
    starts, ends, lags = (table[i : i + 1, :].astype(F32) for i in range(3))
    t = (first + lax.broadcasted_iota(jnp.int32, (rows, 1), 0)).astype(F32)
    here = (starts <= t) & (t < ends)
    pick = lambda v: jnp.sum(jnp.where(here, v, 0.0), axis=1, keepdims=True)
    lag = pick(lags)
    ahead = jnp.where(t + lag < pick(ends), 1.0, 0.0)
    behind = jnp.where(t - lag >= pick(starts), 1.0, 0.0)
    return lag, ahead, behind


def pair_count(table):
    starts, ends, lags = (table[i : i + 1, :].astype(F32) for i in range(3))
    return jnp.sum(jnp.maximum(ends - starts - lags, 0.0), axis=1, keepdims=True)


def shifted(window, lag, ahead, behind):
    rows, width = lag.shape[0], window.shape[0]
    off = (
        lax.broadcasted_iota(jnp.int32, (rows, width), 1)
        - lax.broadcasted_iota(jnp.int32, (rows, width), 0)
        - RIM
    ).astype(F32)
    later = jnp.where((off == lag) & (ahead > 0.0), 1.0, 0.0).astype(BF16)
    earlier = jnp.where((off == -lag) & (behind > 0.0), 1.0, 0.0).astype(BF16)
    dims = (((1,), (0,)), ((), ()))
    zp = lax.dot_general(later, window, dims, preferred_element_type=F32)
    zm = lax.dot_general(earlier, window, dims, preferred_element_type=F32)
    return zp.astype(BF16), zm.astype(BF16)


def diag_kernel(pos, table, xp, before, after, mine, theirs, ext, right):
    rows = xp.shape[0]
    ext[0:RIM, :] = before[...]
    ext[RIM : RIM + rows, :] = xp[...]
    ext[RIM + rows :, :] = after[...]
    fill_right(pos, table, ext, right, rows, P_SIZE)
    scale = 1.0 / pair_count(table)
    c = pos[1]
    v = xp[...]
    for half in range(2):
        cols = slice(256 * half, 256 * half + 256)
        d0 = mm(v[:, cols], right[:, :P_SIZE]) * scale
        d1 = mm(v[:, cols], right[:, P_SIZE : 2 * P_SIZE]) + mm(v[:, cols], right[:, 2 * P_SIZE :])
        d1 = d1 * (0.5 * scale)
        r = lax.broadcasted_iota(jnp.int32, d0.shape, 0) + 256 * half
        l = lax.broadcasted_iota(jnp.int32, d0.shape, 1)
        packed = jnp.where(r >= l, d0, d1)
        diag = jnp.sum(jnp.where(r == l, d1, 0.0), axis=1, keepdims=True)
        diag = jnp.broadcast_to(diag, (256, NB))

        @pl.when(c == half)
        def _():
            mine[:, :P_SIZE] = packed
            mine[:, P_SIZE:] = diag

        @pl.when(c != half)
        def _():
            theirs[:, :P_SIZE] = packed
            theirs[:, P_SIZE:] = diag


def fill_right(pos, table, ext, right, rows, n):
    for b in range(0, rows, 256):
        lag, ahead, behind = frame_info(pos[0] + b, 256, table)
        zp, zm = shifted(ext[b : b + 256 + 2 * RIM, :], lag, ahead, behind)
        own = ext[b + RIM : b + RIM + 256, :]
        right[b : b + 256, :n] = own * (0.5 * (ahead + behind)).astype(BF16)
        right[b : b + 256, n : 2 * n] = zp
        right[b : b + 256, 2 * n :] = zm


def cov_kernel(pos, table, x, g0, g1, g2, g3, out, ext, right, sem):
    rows, n = x.shape[0], P_SIZE
    z, col = pos[3], pos[5]
    for wait in (False, True):
        for k, g in enumerate((g0, g1, g2, g3)):
            q = lax.rem(col - k + 4, 4)

            def bring(src, dst, i):
                copy = pltpu.make_async_copy(src, dst, sem.at[k, i])
                copy.wait() if wait else copy.start()

            @pl.when(q == 0)
            def _():
                bring(g.at[0:RIM, :], ext.at[0:RIM, :], 0)
                bring(g.at[RIM : 2 * RIM, :], ext.at[RIM + rows : 2 * RIM + rows, :], 1)
                bring(g.at[2 * RIM : CHUNK, :], ext.at[RIM : RIM + FIRST, :], 2)

            @pl.when(q != 0)
            def _():
                at = pl.multiple_of(RIM + STEP0 + CHUNK * (q - 1), 16)
                bring(g, ext.at[pl.ds(at, CHUNK), :], 0)

    fill_right(pos, table, ext, right, rows, n)
    scale = 1.0 / pair_count(table)
    for zz in range(4):
        left = x[:, 256 * zz : 256 * zz + 256]
        d0 = mm(left, right[:, :n]) * scale
        d1 = mm(left, right[:, n : 2 * n]) + mm(left, right[:, 2 * n :])
        d1 = d1 * (0.5 * scale)
        at = pl.multiple_of(lax.rem(zz - z + 4, 4) * 32, 32)
        for k in range(8):
            out[k, pl.ds(at, 32), :n] = d0[32 * k : 32 * k + 32, :]
            out[k, pl.ds(at, 32), n:] = d1[32 * k : 32 * k + 32, :]


def parts(v):
    hi = v.astype(BF16)
    rest = v - hi.astype(F32)
    mid = rest.astype(BF16)
    return hi, mid, (rest - mid.astype(F32)).astype(BF16)


def factor(s):
    n = NB
    groups = [s[8 * i : 8 * i + 8, :] for i in range(n // 8)]
    sub = lax.broadcasted_iota(jnp.int32, (8, n), 0)
    lane = lax.broadcasted_iota(jnp.int32, (8, n), 1)
    for j in range(n // 8):
        r0 = 8 * j
        block = (lane >= r0) & (lane < r0 + 8)
        columns = lambda v: [jnp.broadcast_to(v[:, r0 + r : r0 + r + 1], (8, n)) for r in range(8)]
        rows = groups[j]
        cols = columns(rows)
        rows = jnp.where(block, jnp.where(lane - r0 == sub, 1.0, 0.0), rows)
        far = min(j + 1 + AHEAD, n // 8)
        near = range(j + 1, far)
        below = {k: columns(groups[k]) for k in near}
        more = {k: jnp.where(block, 0.0, groups[k]) for k in near}
        for r in range(8):
            rs = lax.rsqrt(cols[r][r : r + 1, :])
            l = cols[r] * rs
            lm = jnp.where(sub > r, l, 0.0)
            row = rows[r : r + 1, :] * rs
            rows = jnp.where(sub == r, row, rows - lm * row)
            lq = {k: below[k][r] * rs for k in near}
            for k in near:
                more[k] = more[k] - lq[k] * row
            for t in range(r + 1, 8):
                at = l[t : t + 1, :]
                cols[t] = cols[t] - lm * at
                for k in near:
                    below[k][t] = below[k][t] - lq[k] * at
        groups[j] = rows
        for k in near:
            groups[k] = more[k]
        if far < n // 8:
            rest = jnp.concatenate(groups[far:], axis=0)
            lanes = lax.broadcasted_iota(jnp.int32, rest.shape, 1)
            rest = jnp.where((lanes >= r0) & (lanes < r0 + 8), 0.0, rest)
            hi, mid, lo = parts(rows)
            left = jnp.concatenate([hi, hi, mid, hi, mid, lo], axis=0)
            right = jnp.concatenate([hi, mid, hi, lo, mid, hi], axis=0)
            rest = rest - mm(left, right)[8 * far :, :]
            for k in range(far, n // 8):
                groups[k] = rest[8 * (k - far) : 8 * (k - far) + 8, :]
    return lower_part(jnp.concatenate(groups, axis=0))


def lower_part(v):
    r = lax.broadcasted_iota(jnp.int32, v.shape, 0)
    c = lax.broadcasted_iota(jnp.int32, v.shape, 1)
    return jnp.where(r >= c, v, 0.0)


def unpack_kernel(pos, own, other, w, up):
    c = pos[1]
    r = lax.broadcasted_iota(jnp.int32, (P_SIZE // 2, P_SIZE), 0)
    l = lax.broadcasted_iota(jnp.int32, (P_SIZE // 2, P_SIZE), 1)
    for half in range(2):
        at = slice(256 * half, 256 * half + 256)
        v = jnp.where(c == half, own[:, :P_SIZE], other[:, :P_SIZE])
        d = jnp.where(c == half, own[:, P_SIZE : P_SIZE + 1], other[:, P_SIZE : P_SIZE + 1])
        w[at, :] = v
        up[at, :] = jnp.where(l > r + 256 * half, v, jnp.where(l == r + 256 * half, d, 0.0))
    r = lax.broadcasted_iota(jnp.int32, (NB, NB), 0)
    l = lax.broadcasted_iota(jnp.int32, (NB, NB), 1)
    for o in range(0, P_SIZE, NB):
        s = jnp.where(r >= l, w[o : o + NB, o : o + NB], 0.0)
        w[o : o + NB, o : o + NB] = s + jnp.where(r < l, s.T, 0.0)
    inverse_step(0, w)


def inverse_step(o, w):
    e = o + NB
    t = factor(w[o:e, o:e])
    w[o:e, o:e] = t
    if o:
        w[o:e, :o] = mn(t, w[o:e, :o])
    if e < P_SIZE:
        low = mt(w[e:, o:e], t)
        w[e:, o:e] = -mn(low, t)
        if o:
            w[e:, :o] = w[e:, :o] - mn(low, w[o:e, :o])
        w[e:, e:] = w[e:, e:] - mt(low, low)
    else:
        w[...] = lower_part(w[...])


def inverse_kernel(o, pos, v, w):
    w[...] = v[...]
    inverse_step(o, w)


def mt_parts(a, b):
    n = a.shape[0]
    a0, a1, a2 = parts(a)
    dims = (((1,), (1,)), ((), ()))
    by = [
        lax.dot_general(jnp.concatenate(rows, axis=0), p, dims, preferred_element_type=F32)
        for rows, p in zip(((a0, a1, a2), (a0, a1), (a0,)), parts(b))
    ]
    low = by[0][2 * n :] + by[1][n:] + by[2]
    return by[0][:n] + ((by[0][n : 2 * n] + by[1][:n]) + low)


def tau_kernel(pos, inv, up, tau):
    rows = inv[pl.ds(pl.multiple_of(pos[2], 16), 16), :]
    u = up[...]
    r = lax.broadcasted_iota(jnp.int32, u.shape, 0)
    l = lax.broadcasted_iota(jnp.int32, u.shape, 1)
    tau[...] = mt(mn(rows, u) + mt(rows, jnp.where(l > r, u, 0.0)), inv[...])


def whiten_kernel(pos, inv, p0, p1, p2, p3, panel, cross, left):
    s = (p0[...] + p1[...]) + (p2[...] + p3[...])
    left[0:32, :] = s[:, :P_SIZE]
    left[32:64, :] = s[:, P_SIZE:]
    res = mt_parts(left[...], inv[...])
    panel[0] = res[0:32, :]
    cross[0] = res[32:64, :]


def swap_core(v, only=None):
    return move(v, lambda z, y, c, w, x: (z, y, 1 - c, w, x) if only is None or (w, x) == only else None)


def exchange(v, axes):
    return lax.all_to_all(v, axes, 0, 0, tiled=True)


def spread(v, axes, n):
    return exchange(jnp.broadcast_to(v[None], (n, *v.shape)), axes)


def together(*values):
    return lax.optimization_barrier(values)


def diag_half(mine, theirs):
    half = (mine + swap_core(theirs, (0, 0))).reshape(4, 64, mine.shape[1])
    return jnp.sum(exchange(half, "y"), axis=0)


def diag_rows(quarter):
    return jnp.sum(exchange(quarter.reshape(4, 16, quarter.shape[1]), "z"), axis=0)


def diag_gather(own):
    half = spread(own, ("y", "z"), 16).reshape(256, own.shape[1])
    return half, swap_core(half)


def body(frames_data, starts, lags):
    tok, width = frames_data.shape
    z, y, c, w, x = (lax.axis_index(a) for a in AXES)
    slab = z * 8 + y * 2 + c
    total = tok * 32
    ends = jnp.concatenate([starts[1:], jnp.array([total], dtype=jnp.int32)])
    table = jnp.stack([starts, ends, lags])
    pos = jnp.stack([slab * tok, c, slab * 16, z, y, x]).astype(jnp.int32)
    panel = frames_data[:, :P_SIZE]

    def step(by):
        def target(z, y, c, w, x):
            i = z * 8 + y * 2 + c + by
            return (i // 8, i // 2 % 4, i % 2, 0, 0) if (w, x) == (0, 0) and 0 <= i < 32 else None
        return target

    behind = move(panel[:RIM], step(-1))
    before = move(panel[tok - RIM :], step(1))

    packed = jax.ShapeDtypeStruct((256, P_SIZE + NB), F32)
    mine, theirs = call(
        diag_kernel, [packed, packed], (pos, table, frames_data, before, behind), "diagonal",
        scratch=[pltpu.VMEM((tok + 2 * RIM, P_SIZE), BF16), pltpu.VMEM((tok, 3 * P_SIZE), BF16)],
        flops=3 * 10**9, block={2: (tok, P_SIZE)},
    )
    theirs, *chunks = together(theirs, *(panel[STEP0 + CHUNK * (k - 1) : STEP0 + CHUNK * k] for k in (2, 1, 3)))
    sent = [
        move(v, lambda z, y, c, w, x: (z, y, c, w, k) if (w, x) == (0, 0) else None)
        for k, v in zip((2, 1, 3), chunks)
    ]
    first = jnp.concatenate([before, behind, panel[:FIRST]], axis=0)
    hold = jnp.where(x == 0, first, sent[0] + sent[1] + sent[2])
    over = move(hold, lambda z, y, c, w, x: (z, y, c, 1, x) if w == 0 else None)
    rows16 = diag_rows(diag_half(mine, theirs))
    hold = jnp.where(w == 0, hold, over)
    gathered = [hold] + [
        move(hold, lambda z, y, c, w, x: (z, y, c, w, (x + k) % 4)) for k in (1, 2, 3)
    ]
    over = move(rows16, lambda z, y, c, w, x: (z, y, c, 1, 0) if (w, x) == (0, 0) else None)
    over, *gathered = together(over, *gathered)
    rows16 = jnp.where(w == 0, rows16, over)
    copies = [
        move(rows16, lambda z, y, c, w, x: (z, y, c, w, k) if x == 0 else None) for k in (2, 1, 3)
    ]
    rows16 = jnp.where(x == 0, rows16, copies[0] + copies[1] + copies[2])
    own, other = diag_gather(rows16)
    (part,) = call(
        cov_kernel, [jax.ShapeDtypeStruct((8, 128, 2 * P_SIZE), F32)], (pos, table, frames_data, *gathered), "covariance",
        scratch=[
            pltpu.VMEM((tok + 2 * RIM, P_SIZE), BF16),
            pltpu.VMEM((tok, 3 * P_SIZE), BF16),
            pltpu.SemaphoreType.DMA((4, 3)),
        ],
        flops=5 * 10**9, vmem=20, hbm=(3, 4, 5, 6),
    )
    t = lax.psum_scatter(part.reshape(1024, 2 * P_SIZE), ("y", "c"), scatter_dimension=0, tiled=True)
    rows = [t[:32]] + [
        move(t[32 * k : 32 * k + 32], lambda z, y, c, w, x: ((z + k) % 4, y, c, w, x)) for k in (2, 1, 3)
    ]

    full = jax.ShapeDtypeStruct((P_SIZE, P_SIZE), F32)
    inv, up = call(unpack_kernel, [full, full], (pos, own, other), "factor0", flops=5 * 10**9, vmem=8)
    for o in range(NB, P_SIZE, NB):
        (inv,) = call(functools.partial(inverse_kernel, o), [full], (pos, inv), "factor%d" % o, flops=5 * 10**9, vmem=8)
    (tau,) = call(
        tau_kernel, [jax.ShapeDtypeStruct((16, P_SIZE), F32)], (pos, inv, up), "tau", flops=10**9, vmem=8
    )
    own = jax.ShapeDtypeStruct((1, 32, P_SIZE), F32)
    panel, cross = call(
        whiten_kernel, [own, own], (pos, inv, *rows), "whiten",
        scratch=[pltpu.VMEM((64, P_SIZE), F32)], flops=10**9, vmem=8,
    )
    return panel, cross, tau


def solution(mesh):
    split = Mesh(mesh.devices.reshape(SIZES), AXES)
    frames, feat = ("z", "y", "c"), ("w", "x")
    return jax.shard_map(
        body,
        mesh=split,
        in_specs=(P(frames, feat), P(), P()),
        out_specs=(P(feat, frames, None), P(feat, frames, None), P(frames, None)),
        check_vma=False,
    )
```

```python
import functools

import jax
import jax.numpy as jnp
from jax import lax
from jax.experimental import pallas as pl
from jax.experimental.pallas import tpu as pltpu
from jax.sharding import Mesh
from jax.sharding import PartitionSpec as P

P_SIZE = 512
RIM = 16
NB = 128
AHEAD = 3
HI = lax.Precision.HIGHEST
F32 = jnp.float32
BF16 = jnp.bfloat16
AXES = ("z", "y", "c", "w", "x")
SIZES = (4, 4, 2, 2, 4)
CHUNK = 272
FIRST = CHUNK - 2 * RIM
STEP0 = 1024 - 3 * CHUNK


def coords():
    for z in range(4):
        for y in range(4):
            for c in range(2):
                for w in range(2):
                    for x in range(4):
                        yield (z, y, c, w, x)


def flat(p):
    i = 0
    for v, n in zip(p, SIZES):
        i = i * n + v
    return i


def move(value, target):
    pairs = []
    for p in coords():
        q = target(*p)
        if q is not None:
            pairs.append((flat(p), flat(q)))
    return lax.ppermute(value, AXES, pairs)


def call(kernel, outs, args, name, scratch=(), flops=0, vmem=16, hbm=(), block=None):
    specs = [pl.BlockSpec(memory_space=pltpu.VMEM)] * len(args)
    specs[0] = pl.BlockSpec(memory_space=pltpu.SMEM)
    for i in hbm:
        specs[i] = pl.BlockSpec(memory_space=pltpu.HBM)
    for i, shape in (block or {}).items():
        specs[i] = pl.BlockSpec(shape, lambda i: (0, 0))
    return pl.pallas_call(
        kernel,
        grid=(1,),
        out_shape=outs,
        in_specs=specs,
        out_specs=[pl.BlockSpec(memory_space=pltpu.VMEM)] * len(outs),
        scratch_shapes=list(scratch),
        compiler_params=pltpu.CompilerParams(vmem_limit_bytes=vmem * 2**20),
        cost_estimate=pl.CostEstimate(flops=flops, bytes_accessed=2**20, transcendentals=0),
        name=name,
    )(*args)


def mm(a, b, precision=None):
    return lax.dot_general(
        a, b, (((0,), (0,)), ((), ())), precision=precision, preferred_element_type=F32
    )


def mn(a, b):
    return lax.dot_general(
        a, b, (((1,), (0,)), ((), ())), precision=HI, preferred_element_type=F32
    )


def mt(a, b):
    return lax.dot_general(
        a, b, (((1,), (1,)), ((), ())), precision=HI, preferred_element_type=F32
    )


def frame_info(first, rows, table):
    starts, ends, lags = (table[i : i + 1, :].astype(F32) for i in range(3))
    t = (first + lax.broadcasted_iota(jnp.int32, (rows, 1), 0)).astype(F32)
    here = (starts <= t) & (t < ends)
    pick = lambda v: jnp.sum(jnp.where(here, v, 0.0), axis=1, keepdims=True)
    lag = pick(lags)
    ahead = jnp.where(t + lag < pick(ends), 1.0, 0.0)
    behind = jnp.where(t - lag >= pick(starts), 1.0, 0.0)
    return lag, ahead, behind


def pair_count(table):
    starts, ends, lags = (table[i : i + 1, :].astype(F32) for i in range(3))
    return jnp.sum(jnp.maximum(ends - starts - lags, 0.0), axis=1, keepdims=True)


def shifted(window, lag, ahead, behind):
    rows, width = lag.shape[0], window.shape[0]
    off = (
        lax.broadcasted_iota(jnp.int32, (rows, width), 1)
        - lax.broadcasted_iota(jnp.int32, (rows, width), 0)
        - RIM
    ).astype(F32)
    later = jnp.where((off == lag) & (ahead > 0.0), 1.0, 0.0).astype(BF16)
    earlier = jnp.where((off == -lag) & (behind > 0.0), 1.0, 0.0).astype(BF16)
    dims = (((1,), (0,)), ((), ()))
    zp = lax.dot_general(later, window, dims, preferred_element_type=F32)
    zm = lax.dot_general(earlier, window, dims, preferred_element_type=F32)
    return zp.astype(BF16), zm.astype(BF16)


def diag_kernel(pos, table, xp, before, after, mine, theirs, ext, right):
    rows = xp.shape[0]
    ext[0:RIM, :] = before[...]
    ext[RIM : RIM + rows, :] = xp[...]
    ext[RIM + rows :, :] = after[...]
    fill_right(pos, table, ext, right, rows, P_SIZE)
    scale = 1.0 / pair_count(table)
    c = pos[1]
    v = xp[...]
    for half in range(2):
        cols = slice(256 * half, 256 * half + 256)
        d0 = mm(v[:, cols], right[:, :P_SIZE]) * scale
        d1 = mm(v[:, cols], right[:, P_SIZE : 2 * P_SIZE]) + mm(v[:, cols], right[:, 2 * P_SIZE :])
        d1 = d1 * (0.5 * scale)
        r = lax.broadcasted_iota(jnp.int32, d0.shape, 0) + 256 * half
        l = lax.broadcasted_iota(jnp.int32, d0.shape, 1)
        packed = jnp.where(r >= l, d0, d1)
        diag = jnp.sum(jnp.where(r == l, d1, 0.0), axis=1, keepdims=True)
        diag = jnp.broadcast_to(diag, (256, NB))

        @pl.when(c == half)
        def _():
            mine[:, :P_SIZE] = packed
            mine[:, P_SIZE:] = diag

        @pl.when(c != half)
        def _():
            theirs[:, :P_SIZE] = packed
            theirs[:, P_SIZE:] = diag


def fill_right(pos, table, ext, right, rows, n):
    for b in range(0, rows, 256):
        lag, ahead, behind = frame_info(pos[0] + b, 256, table)
        zp, zm = shifted(ext[b : b + 256 + 2 * RIM, :], lag, ahead, behind)
        own = ext[b + RIM : b + RIM + 256, :]
        right[b : b + 256, :n] = own * (0.5 * (ahead + behind)).astype(BF16)
        right[b : b + 256, n : 2 * n] = zp
        right[b : b + 256, 2 * n :] = zm


def cov_kernel(pos, table, x, g0, g1, g2, g3, out, ext, right, sem):
    rows, n = x.shape[0], P_SIZE
    z, col = pos[3], pos[5]
    for wait in (False, True):
        for k, g in enumerate((g0, g1, g2, g3)):
            q = lax.rem(col - k + 4, 4)

            def bring(src, dst, i):
                copy = pltpu.make_async_copy(src, dst, sem.at[k, i])
                copy.wait() if wait else copy.start()

            @pl.when(q == 0)
            def _():
                bring(g.at[0:RIM, :], ext.at[0:RIM, :], 0)
                bring(g.at[RIM : 2 * RIM, :], ext.at[RIM + rows : 2 * RIM + rows, :], 1)
                bring(g.at[2 * RIM : CHUNK, :], ext.at[RIM : RIM + FIRST, :], 2)

            @pl.when(q != 0)
            def _():
                at = pl.multiple_of(RIM + STEP0 + CHUNK * (q - 1), 16)
                bring(g, ext.at[pl.ds(at, CHUNK), :], 0)

    fill_right(pos, table, ext, right, rows, n)
    scale = 1.0 / pair_count(table)
    for zz in range(4):
        left = x[:, 256 * zz : 256 * zz + 256]
        d0 = mm(left, right[:, :n]) * scale
        d1 = mm(left, right[:, n : 2 * n]) + mm(left, right[:, 2 * n :])
        d1 = d1 * (0.5 * scale)
        at = pl.multiple_of(lax.rem(zz - z + 4, 4) * 32, 32)
        for k in range(8):
            out[k, pl.ds(at, 32), :n] = d0[32 * k : 32 * k + 32, :]
            out[k, pl.ds(at, 32), n:] = d1[32 * k : 32 * k + 32, :]


def parts(v):
    hi = v.astype(BF16)
    rest = v - hi.astype(F32)
    mid = rest.astype(BF16)
    return hi, mid, (rest - mid.astype(F32)).astype(BF16)


def factor(s):
    n = NB
    groups = [s[8 * i : 8 * i + 8, :] for i in range(n // 8)]
    sub = lax.broadcasted_iota(jnp.int32, (8, n), 0)
    lane = lax.broadcasted_iota(jnp.int32, (8, n), 1)
    for j in range(n // 8):
        r0 = 8 * j
        block = (lane >= r0) & (lane < r0 + 8)
        columns = lambda v: [jnp.broadcast_to(v[:, r0 + r : r0 + r + 1], (8, n)) for r in range(8)]
        rows = groups[j]
        cols = columns(rows)
        rows = jnp.where(block, jnp.where(lane - r0 == sub, 1.0, 0.0), rows)
        far = min(j + 1 + AHEAD, n // 8)
        near = range(j + 1, far)
        below = {k: columns(groups[k]) for k in near}
        more = {k: jnp.where(block, 0.0, groups[k]) for k in near}
        for r in range(8):
            rs = lax.rsqrt(cols[r][r : r + 1, :])
            l = cols[r] * rs
            lm = jnp.where(sub > r, l, 0.0)
            row = rows[r : r + 1, :] * rs
            rows = jnp.where(sub == r, row, rows - lm * row)
            lq = {k: below[k][r] * rs for k in near}
            for k in near:
                more[k] = more[k] - lq[k] * row
            for t in range(r + 1, 8):
                at = l[t : t + 1, :]
                cols[t] = cols[t] - lm * at
                for k in near:
                    below[k][t] = below[k][t] - lq[k] * at
        groups[j] = rows
        for k in near:
            groups[k] = more[k]
        if far < n // 8:
            rest = jnp.concatenate(groups[far:], axis=0)
            lanes = lax.broadcasted_iota(jnp.int32, rest.shape, 1)
            rest = jnp.where((lanes >= r0) & (lanes < r0 + 8), 0.0, rest)
            hi, mid, lo = parts(rows)
            left = jnp.concatenate([hi, hi, mid, hi, mid, lo], axis=0)
            right = jnp.concatenate([hi, mid, hi, lo, mid, hi], axis=0)
            rest = rest - mm(left, right)[8 * far :, :]
            for k in range(far, n // 8):
                groups[k] = rest[8 * (k - far) : 8 * (k - far) + 8, :]
    return lower_part(jnp.concatenate(groups, axis=0))


def lower_part(v):
    r = lax.broadcasted_iota(jnp.int32, v.shape, 0)
    c = lax.broadcasted_iota(jnp.int32, v.shape, 1)
    return jnp.where(r >= c, v, 0.0)


def unpack_kernel(pos, own, other, w, up, buf):
    c = pos[1]
    r = lax.broadcasted_iota(jnp.int32, (P_SIZE // 2, P_SIZE), 0)
    l = lax.broadcasted_iota(jnp.int32, (P_SIZE // 2, P_SIZE), 1)
    for half in range(2):
        for k in range(16):
            for q in range(4):
                at = 16 * k + 4 * q
                buf[at : at + 4, :] = jnp.where(c == half, own[q, k], other[q, k])
        at = slice(256 * half, 256 * half + 256)
        v = buf[:, :P_SIZE]
        w[at, :] = v
        diag = buf[:, P_SIZE : P_SIZE + 1]
        up[at, :] = jnp.where(l > r + 256 * half, v, jnp.where(l == r + 256 * half, diag, 0.0))
    r = lax.broadcasted_iota(jnp.int32, (NB, NB), 0)
    l = lax.broadcasted_iota(jnp.int32, (NB, NB), 1)
    for o in range(0, P_SIZE, NB):
        s = jnp.where(r >= l, w[o : o + NB, o : o + NB], 0.0)
        w[o : o + NB, o : o + NB] = s + jnp.where(r < l, s.T, 0.0)
    inverse_step(0, w)


def inverse_step(o, w):
    e = o + NB
    t = factor(w[o:e, o:e])
    w[o:e, o:e] = t
    if o:
        w[o:e, :o] = mn(t, w[o:e, :o])
    if e < P_SIZE:
        low = mt(w[e:, o:e], t)
        w[e:, o:e] = -mn(low, t)
        if o:
            w[e:, :o] = w[e:, :o] - mn(low, w[o:e, :o])
        w[e:, e:] = w[e:, e:] - mt(low, low)
    else:
        w[...] = lower_part(w[...])


def inverse_kernel(o, pos, v, w):
    w[...] = v[...]
    inverse_step(o, w)


def mt_parts(a, b):
    n = a.shape[0]
    a0, a1, a2 = parts(a)
    dims = (((1,), (1,)), ((), ()))
    by = [
        lax.dot_general(jnp.concatenate(rows, axis=0), p, dims, preferred_element_type=F32)
        for rows, p in zip(((a0, a1, a2), (a0, a1), (a0,)), parts(b))
    ]
    low = by[0][2 * n :] + by[1][n:] + by[2]
    return by[0][:n] + ((by[0][n : 2 * n] + by[1][:n]) + low)


def tau_kernel(pos, inv, up, tau):
    rows = inv[pl.ds(pl.multiple_of(pos[2], 16), 16), :]
    u = up[...]
    r = lax.broadcasted_iota(jnp.int32, u.shape, 0)
    l = lax.broadcasted_iota(jnp.int32, u.shape, 1)
    tau[...] = mt(mn(rows, u) + mt(rows, jnp.where(l > r, u, 0.0)), inv[...])


def whiten_kernel(pos, inv, p0, p1, p2, p3, panel, cross, left):
    s = (p0[...] + p1[...]) + (p2[...] + p3[...])
    left[0:32, :] = s[:, :P_SIZE]
    left[32:64, :] = s[:, P_SIZE:]
    res = mt_parts(left[...], inv[...])
    panel[0] = res[0:32, :]
    cross[0] = res[32:64, :]


def swap_core(v, only=None):
    return move(v, lambda z, y, c, w, x: (z, y, 1 - c, w, x) if only is None or (w, x) == only else None)


def exchange(v, axes):
    return lax.all_to_all(v, axes, 0, 0, tiled=True)


def spread(v, axes, n):
    return exchange(jnp.broadcast_to(v[None], (n, *v.shape)), axes)


def together(*values):
    return lax.optimization_barrier(values)


def diag_half(mine, theirs):
    half = (mine + swap_core(theirs, (0, 0))).reshape(4, 64, mine.shape[1])
    return jnp.sum(exchange(half, "y"), axis=0)


def diag_rows(quarter):
    return jnp.sum(exchange(quarter.reshape(4, 16, quarter.shape[1]), "z"), axis=0)


def diag_gather(own):
    half = spread(spread(own, ("y", "z"), 16), "x", 4)
    return half, swap_core(half)


def body(frames_data, starts, lags):
    tok, width = frames_data.shape
    z, y, c, w, x = (lax.axis_index(a) for a in AXES)
    slab = z * 8 + y * 2 + c
    total = tok * 32
    ends = jnp.concatenate([starts[1:], jnp.array([total], dtype=jnp.int32)])
    table = jnp.stack([starts, ends, lags])
    pos = jnp.stack([slab * tok, c, slab * 16, z, y, x]).astype(jnp.int32)
    panel = frames_data[:, :P_SIZE]

    def step(by):
        def target(z, y, c, w, x):
            i = z * 8 + y * 2 + c + by
            return (i // 8, i // 2 % 4, i % 2, 0, 0) if (w, x) == (0, 0) and 0 <= i < 32 else None
        return target

    behind = move(panel[:RIM], step(-1))
    before = move(panel[tok - RIM :], step(1))

    packed = jax.ShapeDtypeStruct((256, P_SIZE + NB), F32)
    mine, theirs = call(
        diag_kernel, [packed, packed], (pos, table, frames_data, before, behind), "diagonal",
        scratch=[pltpu.VMEM((tok + 2 * RIM, P_SIZE), BF16), pltpu.VMEM((tok, 3 * P_SIZE), BF16)],
        flops=3 * 10**9, block={2: (tok, P_SIZE)},
    )
    theirs, *chunks = together(theirs, *(panel[STEP0 + CHUNK * (k - 1) : STEP0 + CHUNK * k] for k in (2, 1, 3)))
    sent = [
        move(v, lambda z, y, c, w, x: (z, y, c, w, k) if (w, x) == (0, 0) else None)
        for k, v in zip((2, 1, 3), chunks)
    ]
    first = jnp.concatenate([before, behind, panel[:FIRST]], axis=0)
    hold = jnp.where(x == 0, first, sent[0] + sent[1] + sent[2])
    over = move(hold, lambda z, y, c, w, x: (z, y, c, 1, x) if w == 0 else None)
    rows16 = diag_rows(diag_half(mine, theirs))
    hold = jnp.where(w == 0, hold, over)
    gathered = [hold] + [
        move(hold, lambda z, y, c, w, x: (z, y, c, w, (x + k) % 4)) for k in (1, 2, 3)
    ]
    over = move(rows16, lambda z, y, c, w, x: (z, y, c, 1, 0) if (w, x) == (0, 0) else None)
    over, *gathered = together(over, *gathered)
    rows16 = jnp.where(w == 0, rows16, over)
    copies = [
        move(rows16[4 * k : 4 * k + 4], lambda z, y, c, w, x: (z, y, c, w, k) if x == 0 else None) for k in (2, 1, 3)
    ]
    own, other = diag_gather(jnp.where(x == 0, rows16[:4], copies[0] + copies[1] + copies[2]))
    (part,) = call(
        cov_kernel, [jax.ShapeDtypeStruct((8, 128, 2 * P_SIZE), F32)], (pos, table, frames_data, *gathered), "covariance",
        scratch=[
            pltpu.VMEM((tok + 2 * RIM, P_SIZE), BF16),
            pltpu.VMEM((tok, 3 * P_SIZE), BF16),
            pltpu.SemaphoreType.DMA((4, 3)),
        ],
        flops=5 * 10**9, vmem=20, hbm=(3, 4, 5, 6),
    )
    t = lax.psum_scatter(part.reshape(1024, 2 * P_SIZE), ("y", "c"), scatter_dimension=0, tiled=True)
    rows = [t[:32]] + [
        move(t[32 * k : 32 * k + 32], lambda z, y, c, w, x: ((z + k) % 4, y, c, w, x)) for k in (2, 1, 3)
    ]

    full = jax.ShapeDtypeStruct((P_SIZE, P_SIZE), F32)
    inv, up = call(
        unpack_kernel, [full, full], (pos, own, other), "factor0",
        scratch=[pltpu.VMEM((P_SIZE // 2, P_SIZE + NB), F32)], flops=5 * 10**9, vmem=8,
    )
    for o in range(NB, P_SIZE, NB):
        (inv,) = call(functools.partial(inverse_kernel, o), [full], (pos, inv), "factor%d" % o, flops=5 * 10**9, vmem=8)
    (tau,) = call(
        tau_kernel, [jax.ShapeDtypeStruct((16, P_SIZE), F32)], (pos, inv, up), "tau", flops=10**9, vmem=8
    )
    own = jax.ShapeDtypeStruct((1, 32, P_SIZE), F32)
    panel, cross = call(
        whiten_kernel, [own, own], (pos, inv, *rows), "whiten",
        scratch=[pltpu.VMEM((64, P_SIZE), F32)], flops=10**9, vmem=8,
    )
    return panel, cross, tau


def solution(mesh):
    split = Mesh(mesh.devices.reshape(SIZES), AXES)
    frames, feat = ("z", "y", "c"), ("w", "x")
    return jax.shard_map(
        body,
        mesh=split,
        in_specs=(P(frames, feat), P(), P()),
        out_specs=(P(feat, frames, None), P(feat, frames, None), P(frames, None)),
        check_vma=False,
    )
```

```python
import functools

import jax
import jax.numpy as jnp
from jax import lax
from jax.experimental import pallas as pl
from jax.experimental.pallas import tpu as pltpu
from jax.sharding import Mesh
from jax.sharding import PartitionSpec as P

P_SIZE = 512
RIM = 16
NB = 128
AHEAD = 3
HI = lax.Precision.HIGHEST
F32 = jnp.float32
BF16 = jnp.bfloat16
AXES = ("z", "y", "c", "w", "x")
SIZES = (4, 4, 2, 2, 4)
CHUNK = 272
FIRST = CHUNK - 2 * RIM
STEP0 = 1024 - 3 * CHUNK


def coords():
    for z in range(4):
        for y in range(4):
            for c in range(2):
                for w in range(2):
                    for x in range(4):
                        yield (z, y, c, w, x)


def flat(p):
    i = 0
    for v, n in zip(p, SIZES):
        i = i * n + v
    return i


def move(value, target):
    pairs = []
    for p in coords():
        q = target(*p)
        if q is not None:
            pairs.append((flat(p), flat(q)))
    return lax.ppermute(value, AXES, pairs)


def call(kernel, outs, args, name, scratch=(), flops=0, vmem=16, hbm=(), block=None):
    specs = [pl.BlockSpec(memory_space=pltpu.VMEM)] * len(args)
    specs[0] = pl.BlockSpec(memory_space=pltpu.SMEM)
    for i in hbm:
        specs[i] = pl.BlockSpec(memory_space=pltpu.HBM)
    for i, shape in (block or {}).items():
        specs[i] = pl.BlockSpec(shape, lambda i: (0, 0))
    return pl.pallas_call(
        kernel,
        grid=(1,),
        out_shape=outs,
        in_specs=specs,
        out_specs=[pl.BlockSpec(memory_space=pltpu.VMEM)] * len(outs),
        scratch_shapes=list(scratch),
        compiler_params=pltpu.CompilerParams(vmem_limit_bytes=vmem * 2**20),
        cost_estimate=pl.CostEstimate(flops=flops, bytes_accessed=2**20, transcendentals=0),
        name=name,
    )(*args)


def mm(a, b, precision=None):
    return lax.dot_general(
        a, b, (((0,), (0,)), ((), ())), precision=precision, preferred_element_type=F32
    )


def mn(a, b):
    return lax.dot_general(
        a, b, (((1,), (0,)), ((), ())), precision=HI, preferred_element_type=F32
    )


def mt(a, b):
    return lax.dot_general(
        a, b, (((1,), (1,)), ((), ())), precision=HI, preferred_element_type=F32
    )


def frame_info(first, rows, table):
    starts, ends, lags = (table[i : i + 1, :].astype(F32) for i in range(3))
    t = (first + lax.broadcasted_iota(jnp.int32, (rows, 1), 0)).astype(F32)
    here = (starts <= t) & (t < ends)
    pick = lambda v: jnp.sum(jnp.where(here, v, 0.0), axis=1, keepdims=True)
    lag = pick(lags)
    ahead = jnp.where(t + lag < pick(ends), 1.0, 0.0)
    behind = jnp.where(t - lag >= pick(starts), 1.0, 0.0)
    return lag, ahead, behind


def pair_count(table):
    starts, ends, lags = (table[i : i + 1, :].astype(F32) for i in range(3))
    return jnp.sum(jnp.maximum(ends - starts - lags, 0.0), axis=1, keepdims=True)


def shifted(window, lag, ahead, behind):
    rows, width = lag.shape[0], window.shape[0]
    off = (
        lax.broadcasted_iota(jnp.int32, (rows, width), 1)
        - lax.broadcasted_iota(jnp.int32, (rows, width), 0)
        - RIM
    ).astype(F32)
    later = jnp.where((off == lag) & (ahead > 0.0), 1.0, 0.0).astype(BF16)
    earlier = jnp.where((off == -lag) & (behind > 0.0), 1.0, 0.0).astype(BF16)
    dims = (((1,), (0,)), ((), ()))
    zp = lax.dot_general(later, window, dims, preferred_element_type=F32)
    zm = lax.dot_general(earlier, window, dims, preferred_element_type=F32)
    return zp.astype(BF16), zm.astype(BF16)


def diag_kernel(pos, table, xp, before, after, mine, theirs, ext, right):
    rows = xp.shape[0]
    ext[0:RIM, :] = before[...]
    ext[RIM : RIM + rows, :] = xp[...]
    ext[RIM + rows :, :] = after[...]
    fill_right(pos, table, ext, right, rows, P_SIZE)
    scale = 1.0 / pair_count(table)
    c = pos[1]
    v = xp[...]
    for half in range(2):
        cols = slice(256 * half, 256 * half + 256)
        d0 = mm(v[:, cols], right[:, :P_SIZE]) * scale
        d1 = mm(v[:, cols], right[:, P_SIZE : 2 * P_SIZE]) + mm(v[:, cols], right[:, 2 * P_SIZE :])
        d1 = d1 * (0.5 * scale)
        r = lax.broadcasted_iota(jnp.int32, d0.shape, 0) + 256 * half
        l = lax.broadcasted_iota(jnp.int32, d0.shape, 1)
        packed = jnp.where(r >= l, d0, d1)
        diag = jnp.sum(jnp.where(r == l, d1, 0.0), axis=1, keepdims=True)
        diag = jnp.broadcast_to(diag, (256, NB))

        @pl.when(c == half)
        def _():
            mine[:, :P_SIZE] = packed
            mine[:, P_SIZE:] = diag

        @pl.when(c != half)
        def _():
            theirs[:, :P_SIZE] = packed
            theirs[:, P_SIZE:] = diag


def fill_right(pos, table, ext, right, rows, n):
    for b in range(0, rows, 256):
        lag, ahead, behind = frame_info(pos[0] + b, 256, table)
        zp, zm = shifted(ext[b : b + 256 + 2 * RIM, :], lag, ahead, behind)
        own = ext[b + RIM : b + RIM + 256, :]
        right[b : b + 256, :n] = own * (0.5 * (ahead + behind)).astype(BF16)
        right[b : b + 256, n : 2 * n] = zp
        right[b : b + 256, 2 * n :] = zm


def cov_kernel(pos, table, x, g0, g1, g2, g3, out, ext, right, sem):
    rows, n = x.shape[0], P_SIZE
    z, col = pos[3], pos[5]
    for wait in (False, True):
        for k, g in enumerate((g0, g1, g2, g3)):
            q = lax.rem(col - k + 4, 4)

            def bring(src, dst, i):
                copy = pltpu.make_async_copy(src, dst, sem.at[k, i])
                copy.wait() if wait else copy.start()

            @pl.when(q == 0)
            def _():
                bring(g.at[0:RIM, :], ext.at[0:RIM, :], 0)
                bring(g.at[RIM : 2 * RIM, :], ext.at[RIM + rows : 2 * RIM + rows, :], 1)
                bring(g.at[2 * RIM : CHUNK, :], ext.at[RIM : RIM + FIRST, :], 2)

            @pl.when(q != 0)
            def _():
                at = pl.multiple_of(RIM + STEP0 + CHUNK * (q - 1), 16)
                bring(g, ext.at[pl.ds(at, CHUNK), :], 0)

    fill_right(pos, table, ext, right, rows, n)
    scale = 1.0 / pair_count(table)
    for zz in range(4):
        left = x[:, 256 * zz : 256 * zz + 256]
        d0 = mm(left, right[:, :n]) * scale
        d1 = mm(left, right[:, n : 2 * n]) + mm(left, right[:, 2 * n :])
        d1 = d1 * (0.5 * scale)
        at = pl.multiple_of(lax.rem(zz - z + 4, 4) * 32, 32)
        for k in range(8):
            out[k, pl.ds(at, 32), :n] = d0[32 * k : 32 * k + 32, :]
            out[k, pl.ds(at, 32), n:] = d1[32 * k : 32 * k + 32, :]


def parts(v):
    hi = v.astype(BF16)
    rest = v - hi.astype(F32)
    mid = rest.astype(BF16)
    return hi, mid, (rest - mid.astype(F32)).astype(BF16)


def factor(s):
    n = NB
    groups = [s[8 * i : 8 * i + 8, :] for i in range(n // 8)]
    sub = lax.broadcasted_iota(jnp.int32, (8, n), 0)
    lane = lax.broadcasted_iota(jnp.int32, (8, n), 1)
    for j in range(n // 8):
        r0 = 8 * j
        block = (lane >= r0) & (lane < r0 + 8)
        columns = lambda v: [jnp.broadcast_to(v[:, r0 + r : r0 + r + 1], (8, n)) for r in range(8)]
        rows = groups[j]
        cols = columns(rows)
        rows = jnp.where(block, jnp.where(lane - r0 == sub, 1.0, 0.0), rows)
        far = min(j + 1 + AHEAD, n // 8)
        near = range(j + 1, far)
        below = {k: columns(groups[k]) for k in near}
        more = {k: jnp.where(block, 0.0, groups[k]) for k in near}
        for r in range(8):
            rs = lax.rsqrt(cols[r][r : r + 1, :])
            l = cols[r] * rs
            lm = jnp.where(sub > r, l, 0.0)
            row = rows[r : r + 1, :] * rs
            rows = jnp.where(sub == r, row, rows - lm * row)
            lq = {k: below[k][r] * rs for k in near}
            for k in near:
                more[k] = more[k] - lq[k] * row
            for t in range(r + 1, 8):
                at = l[t : t + 1, :]
                cols[t] = cols[t] - lm * at
                for k in near:
                    below[k][t] = below[k][t] - lq[k] * at
        groups[j] = rows
        for k in near:
            groups[k] = more[k]
        if far < n // 8:
            rest = jnp.concatenate(groups[far:], axis=0)
            lanes = lax.broadcasted_iota(jnp.int32, rest.shape, 1)
            rest = jnp.where((lanes >= r0) & (lanes < r0 + 8), 0.0, rest)
            hi, mid, lo = parts(rows)
            left = jnp.concatenate([hi, hi, mid, hi, mid, lo], axis=0)
            right = jnp.concatenate([hi, mid, hi, lo, mid, hi], axis=0)
            rest = rest - mm(left, right)[8 * far :, :]
            for k in range(far, n // 8):
                groups[k] = rest[8 * (k - far) : 8 * (k - far) + 8, :]
    return lower_part(jnp.concatenate(groups, axis=0))


def lower_part(v):
    r = lax.broadcasted_iota(jnp.int32, v.shape, 0)
    c = lax.broadcasted_iota(jnp.int32, v.shape, 1)
    return jnp.where(r >= c, v, 0.0)


def unpack_kernel(pos, own, other, w, up):
    c = pos[1]
    r = lax.broadcasted_iota(jnp.int32, (P_SIZE // 2, P_SIZE), 0)
    l = lax.broadcasted_iota(jnp.int32, (P_SIZE // 2, P_SIZE), 1)
    for half in range(2):
        at = slice(256 * half, 256 * half + 256)
        v = jnp.where(c == half, own[:, :P_SIZE], other[:, :P_SIZE])
        d = jnp.where(c == half, own[:, P_SIZE : P_SIZE + 1], other[:, P_SIZE : P_SIZE + 1])
        w[at, :] = v
        up[at, :] = jnp.where(l > r + 256 * half, v, jnp.where(l == r + 256 * half, d, 0.0))
    r = lax.broadcasted_iota(jnp.int32, (NB, NB), 0)
    l = lax.broadcasted_iota(jnp.int32, (NB, NB), 1)
    for o in range(0, P_SIZE, NB):
        s = jnp.where(r >= l, w[o : o + NB, o : o + NB], 0.0)
        w[o : o + NB, o : o + NB] = s + jnp.where(r < l, s.T, 0.0)
    inverse_step(0, w)


def inverse_step(o, w):
    e = o + NB
    t = factor(w[o:e, o:e])
    w[o:e, o:e] = t
    if o:
        w[o:e, :o] = mn(t, w[o:e, :o])
    if e < P_SIZE:
        low = mt(w[e:, o:e], t)
        w[e:, o:e] = -mn(low, t)
        if o:
            w[e:, :o] = w[e:, :o] - mn(low, w[o:e, :o])
        w[e:, e:] = w[e:, e:] - mt(low, low)
    else:
        w[...] = lower_part(w[...])


def inverse_kernel(o, pos, v, w):
    w[...] = v[...]
    inverse_step(o, w)


def mt_parts(a, b):
    n = a.shape[0]
    a0, a1, a2 = parts(a)
    dims = (((1,), (1,)), ((), ()))
    by = [
        lax.dot_general(jnp.concatenate(rows, axis=0), p, dims, preferred_element_type=F32)
        for rows, p in zip(((a0, a1, a2), (a0, a1), (a0,)), parts(b))
    ]
    low = by[0][2 * n :] + by[1][n:] + by[2]
    return by[0][:n] + ((by[0][n : 2 * n] + by[1][:n]) + low)


def whiten_kernel(pos, inv, up, p0, p1, p2, p3, panel, cross, tau, left):
    s = (p0[...] + p1[...]) + (p2[...] + p3[...])
    left[0:32, :] = s[:, :P_SIZE]
    left[32:64, :] = s[:, P_SIZE:]
    rows = inv[pl.ds(pl.multiple_of(pos[2], 16), 16), :]
    u = up[...]
    r = lax.broadcasted_iota(jnp.int32, u.shape, 0)
    l = lax.broadcasted_iota(jnp.int32, u.shape, 1)
    left[64:80, :] = mn(rows, u) + mt(rows, jnp.where(l > r, u, 0.0))
    res = mt_parts(left[...], inv[...])
    panel[0] = res[0:32, :]
    cross[0] = res[32:64, :]
    tau[...] = res[64:80, :]


def swap_core(v, only=None):
    return move(v, lambda z, y, c, w, x: (z, y, 1 - c, w, x) if only is None or (w, x) == only else None)


def exchange(v, axes):
    return lax.all_to_all(v, axes, 0, 0, tiled=True)


def spread(v, axes, n):
    return exchange(jnp.broadcast_to(v[None], (n, *v.shape)), axes)


def together(*values):
    return lax.optimization_barrier(values)


def diag_half(mine, theirs, first):
    half = (mine + swap_core(theirs, (0, 0))).reshape(4, 64, mine.shape[1])
    half, first = together(half, first)
    return jnp.sum(exchange(half, "y"), axis=0), first


def diag_rows(quarter):
    return jnp.sum(exchange(quarter.reshape(4, 16, quarter.shape[1]), "z"), axis=0)


def diag_gather(own):
    half = spread(own, ("y", "z"), 16).reshape(256, own.shape[1])
    return half, swap_core(half)


def body(frames_data, starts, lags):
    tok, width = frames_data.shape
    z, y, c, w, x = (lax.axis_index(a) for a in AXES)
    slab = z * 8 + y * 2 + c
    total = tok * 32
    ends = jnp.concatenate([starts[1:], jnp.array([total], dtype=jnp.int32)])
    table = jnp.stack([starts, ends, lags])
    pos = jnp.stack([slab * tok, c, slab * 16, z, y, x]).astype(jnp.int32)
    panel = frames_data[:, :P_SIZE]

    def step(by):
        def target(z, y, c, w, x):
            i = z * 8 + y * 2 + c + by
            return (i // 8, i // 2 % 4, i % 2, 0, 0) if (w, x) == (0, 0) and 0 <= i < 32 else None
        return target

    behind = move(panel[:RIM], step(-1))
    before = move(panel[tok - RIM :], step(1))

    packed = jax.ShapeDtypeStruct((256, P_SIZE + NB), F32)
    mine, theirs = call(
        diag_kernel, [packed, packed], (pos, table, frames_data, before, behind), "diagonal",
        scratch=[pltpu.VMEM((tok + 2 * RIM, P_SIZE), BF16), pltpu.VMEM((tok, 3 * P_SIZE), BF16)],
        flops=3 * 10**9, block={2: (tok, P_SIZE)},
    )
    chunks = [panel[STEP0 + CHUNK * (k - 1) : STEP0 + CHUNK * k] for k in (2, 1, 3)]
    sent = [
        move(v, lambda z, y, c, w, x: (z, y, c, w, k) if (w, x) == (0, 0) else None)
        for k, v in zip((2, 1, 3), chunks)
    ]
    first = jnp.concatenate([before, behind, panel[:FIRST]], axis=0)
    hold = jnp.where(x == 0, first, sent[0] + sent[1] + sent[2])
    theirs, hold = together(theirs, hold)
    over = move(hold, lambda z, y, c, w, x: (z, y, c, 1, x) if w == 0 else None)
    quarter, over = diag_half(mine, theirs, over)
    hold = jnp.where(w == 0, hold, over)
    gathered = [hold] + [
        move(hold, lambda z, y, c, w, x: (z, y, c, w, (x + k) % 4)) for k in (1, 2, 3)
    ]
    quarter, gathered[1] = together(quarter, gathered[1])
    rows16 = diag_rows(quarter)
    over = move(rows16, lambda z, y, c, w, x: (z, y, c, 1, 0) if (w, x) == (0, 0) else None)
    rows16 = jnp.where(w == 0, rows16, over)
    copies = [
        move(rows16, lambda z, y, c, w, x: (z, y, c, w, k) if x == 0 else None) for k in (2, 1, 3)
    ]
    rows16 = jnp.where(x == 0, rows16, copies[0] + copies[1] + copies[2])
    own, other = diag_gather(rows16)
    (part,) = call(
        cov_kernel, [jax.ShapeDtypeStruct((8, 128, 2 * P_SIZE), F32)], (pos, table, frames_data, *gathered), "covariance",
        scratch=[
            pltpu.VMEM((tok + 2 * RIM, P_SIZE), BF16),
            pltpu.VMEM((tok, 3 * P_SIZE), BF16),
            pltpu.SemaphoreType.DMA((4, 3)),
        ],
        flops=5 * 10**9, vmem=20, hbm=(3, 4, 5, 6),
    )
    t = lax.psum_scatter(part.reshape(1024, 2 * P_SIZE), ("y", "c"), scatter_dimension=0, tiled=True)
    full = jax.ShapeDtypeStruct((P_SIZE, P_SIZE), F32)
    inv, up = call(unpack_kernel, [full, full], (pos, own, other), "factor0", flops=5 * 10**9, vmem=8)
    inv, t = together(inv, t)
    rows = [t[:32]] + [
        move(t[32 * k : 32 * k + 32], lambda z, y, c, w, x: ((z + k) % 4, y, c, w, x)) for k in (2, 1, 3)
    ]
    for o in range(NB, P_SIZE, NB):
        (inv,) = call(functools.partial(inverse_kernel, o), [full], (pos, inv), "factor%d" % o, flops=5 * 10**9, vmem=8)
    own = jax.ShapeDtypeStruct((1, 32, P_SIZE), F32)
    return tuple(
        call(
            whiten_kernel, [own, own, jax.ShapeDtypeStruct((16, P_SIZE), F32)],
            (pos, inv, up, *rows), "whiten", scratch=[pltpu.VMEM((80, P_SIZE), F32)], flops=2 * 10**9, vmem=8,
        )
    )


def solution(mesh):
    split = Mesh(mesh.devices.reshape(SIZES), AXES)
    frames, feat = ("z", "y", "c"), ("w", "x")
    return jax.shard_map(
        body,
        mesh=split,
        in_specs=(P(frames, feat), P(), P()),
        out_specs=(P(feat, frames, None), P(feat, frames, None), P(frames, None)),
        check_vma=False,
    )
```

```python
import functools

import jax
import jax.numpy as jnp
from jax import lax
from jax.experimental import pallas as pl
from jax.experimental.pallas import tpu as pltpu
from jax.sharding import Mesh
from jax.sharding import PartitionSpec as P

P_SIZE = 512
RIM = 16
NB = 128
AHEAD = 3
HI = lax.Precision.HIGHEST
F32 = jnp.float32
BF16 = jnp.bfloat16
AXES = ("z", "y", "c", "w", "x")
SIZES = (4, 4, 2, 2, 4)
CHUNK = 272
FIRST = CHUNK - 2 * RIM
STEP0 = 1024 - 3 * CHUNK


def coords():
    for z in range(4):
        for y in range(4):
            for c in range(2):
                for w in range(2):
                    for x in range(4):
                        yield (z, y, c, w, x)


def flat(p):
    i = 0
    for v, n in zip(p, SIZES):
        i = i * n + v
    return i


def move(value, target):
    pairs = []
    for p in coords():
        q = target(*p)
        if q is not None:
            pairs.append((flat(p), flat(q)))
    return lax.ppermute(value, AXES, pairs)


def call(kernel, outs, args, name, scratch=(), flops=0, vmem=16, hbm=(), block=None):
    specs = [pl.BlockSpec(memory_space=pltpu.VMEM)] * len(args)
    specs[0] = pl.BlockSpec(memory_space=pltpu.SMEM)
    for i in hbm:
        specs[i] = pl.BlockSpec(memory_space=pltpu.HBM)
    for i, shape in (block or {}).items():
        specs[i] = pl.BlockSpec(shape, lambda i: (0, 0))
    return pl.pallas_call(
        kernel,
        grid=(1,),
        out_shape=outs,
        in_specs=specs,
        out_specs=[pl.BlockSpec(memory_space=pltpu.VMEM)] * len(outs),
        scratch_shapes=list(scratch),
        compiler_params=pltpu.CompilerParams(vmem_limit_bytes=vmem * 2**20),
        cost_estimate=pl.CostEstimate(flops=flops, bytes_accessed=2**20, transcendentals=0),
        name=name,
    )(*args)


def mm(a, b, precision=None):
    return lax.dot_general(
        a, b, (((0,), (0,)), ((), ())), precision=precision, preferred_element_type=F32
    )


def mn(a, b):
    return lax.dot_general(
        a, b, (((1,), (0,)), ((), ())), precision=HI, preferred_element_type=F32
    )


def mt(a, b):
    return lax.dot_general(
        a, b, (((1,), (1,)), ((), ())), precision=HI, preferred_element_type=F32
    )


def frame_info(first, rows, table):
    starts, ends, lags = (table[i : i + 1, :].astype(F32) for i in range(3))
    t = (first + lax.broadcasted_iota(jnp.int32, (rows, 1), 0)).astype(F32)
    here = (starts <= t) & (t < ends)
    pick = lambda v: jnp.sum(jnp.where(here, v, 0.0), axis=1, keepdims=True)
    lag = pick(lags)
    ahead = jnp.where(t + lag < pick(ends), 1.0, 0.0)
    behind = jnp.where(t - lag >= pick(starts), 1.0, 0.0)
    return lag, ahead, behind


def pair_count(table):
    starts, ends, lags = (table[i : i + 1, :].astype(F32) for i in range(3))
    return jnp.sum(jnp.maximum(ends - starts - lags, 0.0), axis=1, keepdims=True)


def shifted(window, lag, ahead, behind):
    rows, width = lag.shape[0], window.shape[0]
    off = (
        lax.broadcasted_iota(jnp.int32, (rows, width), 1)
        - lax.broadcasted_iota(jnp.int32, (rows, width), 0)
        - RIM
    ).astype(F32)
    later = jnp.where((off == lag) & (ahead > 0.0), 1.0, 0.0).astype(BF16)
    earlier = jnp.where((off == -lag) & (behind > 0.0), 1.0, 0.0).astype(BF16)
    dims = (((1,), (0,)), ((), ()))
    zp = lax.dot_general(later, window, dims, preferred_element_type=F32)
    zm = lax.dot_general(earlier, window, dims, preferred_element_type=F32)
    return zp.astype(BF16), zm.astype(BF16)


def diag_kernel(pos, table, xp, before, after, mine, theirs, ext, right):
    rows = xp.shape[0]
    ext[0:RIM, :] = before[...]
    ext[RIM : RIM + rows, :] = xp[...]
    ext[RIM + rows :, :] = after[...]
    fill_right(pos, table, ext, right, rows, P_SIZE)
    scale = 1.0 / pair_count(table)
    c = pos[1]
    v = xp[...]
    for half in range(2):
        cols = slice(256 * half, 256 * half + 256)
        d0 = mm(v[:, cols], right[:, :P_SIZE]) * scale
        d1 = mm(v[:, cols], right[:, P_SIZE : 2 * P_SIZE]) + mm(v[:, cols], right[:, 2 * P_SIZE :])
        d1 = d1 * (0.5 * scale)
        r = lax.broadcasted_iota(jnp.int32, d0.shape, 0) + 256 * half
        l = lax.broadcasted_iota(jnp.int32, d0.shape, 1)
        packed = jnp.where(r >= l, d0, d1)
        diag = jnp.sum(jnp.where(r == l, d1, 0.0), axis=1, keepdims=True)
        diag = jnp.broadcast_to(diag, (256, NB))

        @pl.when(c == half)
        def _():
            mine[:, :P_SIZE] = packed
            mine[:, P_SIZE:] = diag

        @pl.when(c != half)
        def _():
            theirs[:, :P_SIZE] = packed
            theirs[:, P_SIZE:] = diag


def fill_right(pos, table, ext, right, rows, n):
    for b in range(0, rows, 256):
        lag, ahead, behind = frame_info(pos[0] + b, 256, table)
        zp, zm = shifted(ext[b : b + 256 + 2 * RIM, :], lag, ahead, behind)
        own = ext[b + RIM : b + RIM + 256, :]
        right[b : b + 256, :n] = own * (0.5 * (ahead + behind)).astype(BF16)
        right[b : b + 256, n : 2 * n] = zp
        right[b : b + 256, 2 * n :] = zm


def cov_kernel(pos, table, x, g0, g1, g2, g3, out, ext, right, sem):
    rows, n = x.shape[0], P_SIZE
    z, col = pos[3], pos[5]
    for wait in (False, True):
        for k, g in enumerate((g0, g1, g2, g3)):
            q = lax.rem(col - k + 4, 4)

            def bring(src, dst, i):
                copy = pltpu.make_async_copy(src, dst, sem.at[k, i])
                copy.wait() if wait else copy.start()

            @pl.when(q == 0)
            def _():
                bring(g.at[0:RIM, :], ext.at[0:RIM, :], 0)
                bring(g.at[RIM : 2 * RIM, :], ext.at[RIM + rows : 2 * RIM + rows, :], 1)
                bring(g.at[2 * RIM : CHUNK, :], ext.at[RIM : RIM + FIRST, :], 2)

            @pl.when(q != 0)
            def _():
                at = pl.multiple_of(RIM + STEP0 + CHUNK * (q - 1), 16)
                bring(g, ext.at[pl.ds(at, CHUNK), :], 0)

    fill_right(pos, table, ext, right, rows, n)
    scale = 1.0 / pair_count(table)
    for zz in range(4):
        left = x[:, 256 * zz : 256 * zz + 256]
        d0 = mm(left, right[:, :n]) * scale
        d1 = mm(left, right[:, n : 2 * n]) + mm(left, right[:, 2 * n :])
        d1 = d1 * (0.5 * scale)
        at = pl.multiple_of(lax.rem(zz - z + 4, 4) * 32, 32)
        for k in range(8):
            out[k, pl.ds(at, 32), :n] = d0[32 * k : 32 * k + 32, :]
            out[k, pl.ds(at, 32), n:] = d1[32 * k : 32 * k + 32, :]


def parts(v):
    hi = v.astype(BF16)
    rest = v - hi.astype(F32)
    mid = rest.astype(BF16)
    return hi, mid, (rest - mid.astype(F32)).astype(BF16)


def factor(s):
    n = NB
    groups = [s[8 * i : 8 * i + 8, :] for i in range(n // 8)]
    sub = lax.broadcasted_iota(jnp.int32, (8, n), 0)
    lane = lax.broadcasted_iota(jnp.int32, (8, n), 1)
    for j in range(n // 8):
        r0 = 8 * j
        block = (lane >= r0) & (lane < r0 + 8)
        columns = lambda v: [jnp.broadcast_to(v[:, r0 + r : r0 + r + 1], (8, n)) for r in range(8)]
        rows = groups[j]
        cols = columns(rows)
        rows = jnp.where(block, jnp.where(lane - r0 == sub, 1.0, 0.0), rows)
        far = min(j + 1 + AHEAD, n // 8)
        near = range(j + 1, far)
        below = {k: columns(groups[k]) for k in near}
        more = {k: jnp.where(block, 0.0, groups[k]) for k in near}
        for r in range(8):
            rs = lax.rsqrt(cols[r][r : r + 1, :])
            l = cols[r] * rs
            lm = jnp.where(sub > r, l, 0.0)
            row = rows[r : r + 1, :] * rs
            rows = jnp.where(sub == r, row, rows - lm * row)
            lq = {k: below[k][r] * rs for k in near}
            for k in near:
                more[k] = more[k] - lq[k] * row
            for t in range(r + 1, 8):
                at = l[t : t + 1, :]
                cols[t] = cols[t] - lm * at
                for k in near:
                    below[k][t] = below[k][t] - lq[k] * at
        groups[j] = rows
        for k in near:
            groups[k] = more[k]
        if far < n // 8:
            rest = jnp.concatenate(groups[far:], axis=0)
            lanes = lax.broadcasted_iota(jnp.int32, rest.shape, 1)
            rest = jnp.where((lanes >= r0) & (lanes < r0 + 8), 0.0, rest)
            hi, mid, lo = parts(rows)
            left = jnp.concatenate([hi, hi, mid, hi, mid, lo], axis=0)
            right = jnp.concatenate([hi, mid, hi, lo, mid, hi], axis=0)
            rest = rest - mm(left, right)[8 * far :, :]
            for k in range(far, n // 8):
                groups[k] = rest[8 * (k - far) : 8 * (k - far) + 8, :]
    return lower_part(jnp.concatenate(groups, axis=0))


def lower_part(v):
    r = lax.broadcasted_iota(jnp.int32, v.shape, 0)
    c = lax.broadcasted_iota(jnp.int32, v.shape, 1)
    return jnp.where(r >= c, v, 0.0)


def unpack_kernel(pos, own, other, w, up):
    c = pos[1]
    r = lax.broadcasted_iota(jnp.int32, (P_SIZE // 2, P_SIZE), 0)
    l = lax.broadcasted_iota(jnp.int32, (P_SIZE // 2, P_SIZE), 1)
    for half in range(2):
        at = slice(256 * half, 256 * half + 256)
        v = jnp.where(c == half, own[:, :P_SIZE], other[:, :P_SIZE])
        d = jnp.where(c == half, own[:, P_SIZE : P_SIZE + 1], other[:, P_SIZE : P_SIZE + 1])
        w[at, :] = v
        up[at, :] = jnp.where(l > r + 256 * half, v, jnp.where(l == r + 256 * half, d, 0.0))
    r = lax.broadcasted_iota(jnp.int32, (NB, NB), 0)
    l = lax.broadcasted_iota(jnp.int32, (NB, NB), 1)
    for o in range(0, P_SIZE, NB):
        s = jnp.where(r >= l, w[o : o + NB, o : o + NB], 0.0)
        w[o : o + NB, o : o + NB] = s + jnp.where(r < l, s.T, 0.0)
    inverse_step(0, w)


def inverse_step(o, w):
    e = o + NB
    t = factor(w[o:e, o:e])
    w[o:e, o:e] = t
    if o:
        w[o:e, :o] = mn(t, w[o:e, :o])
    if e < P_SIZE:
        low = mt(w[e:, o:e], t)
        w[e:, o:e] = -mn(low, t)
        if o:
            w[e:, :o] = w[e:, :o] - mn(low, w[o:e, :o])
        w[e:, e:] = w[e:, e:] - mt(low, low)
    else:
        w[...] = lower_part(w[...])


def inverse_kernel(o, pos, v, w):
    w[...] = v[...]
    inverse_step(o, w)


def mt_parts(a, b):
    n = a.shape[0]
    a0, a1, a2 = parts(a)
    dims = (((1,), (1,)), ((), ()))
    by = [
        lax.dot_general(jnp.concatenate(rows, axis=0), p, dims, preferred_element_type=F32)
        for rows, p in zip(((a0, a1, a2), (a0, a1), (a0,)), parts(b))
    ]
    low = by[0][2 * n :] + by[1][n:] + by[2]
    return by[0][:n] + ((by[0][n : 2 * n] + by[1][:n]) + low)


def tau_kernel(pos, inv, up, tau):
    rows = inv[pl.ds(pl.multiple_of(pos[2], 16), 16), :]
    u = up[...]
    r = lax.broadcasted_iota(jnp.int32, u.shape, 0)
    l = lax.broadcasted_iota(jnp.int32, u.shape, 1)
    tau[...] = mt(mn(rows, u) + mt(rows, jnp.where(l > r, u, 0.0)), inv[...])


def whiten_kernel(pos, inv, p0, p1, p2, p3, panel, cross, left):
    s = (p0[...] + p1[...]) + (p2[...] + p3[...])
    left[0:32, :] = s[:, :P_SIZE]
    left[32:64, :] = s[:, P_SIZE:]
    res = mt_parts(left[...], inv[...])
    panel[0] = res[0:32, :]
    cross[0] = res[32:64, :]


def swap_core(v, only=None):
    return move(v, lambda z, y, c, w, x: (z, y, 1 - c, w, x) if only is None or (w, x) == only else None)


def exchange(v, axes):
    return lax.all_to_all(v, axes, 0, 0, tiled=True)


def spread(v, axes, n):
    return exchange(jnp.broadcast_to(v[None], (n, *v.shape)), axes)


def together(*values):
    return lax.optimization_barrier(values)


def diag_half(mine, theirs):
    half = (mine + swap_core(theirs, (0, 0))).reshape(4, 64, mine.shape[1])
    return jnp.sum(exchange(half, "y"), axis=0)


def diag_rows(quarter):
    return jnp.sum(exchange(quarter.reshape(4, 16, quarter.shape[1]), "z"), axis=0)


def diag_gather(own):
    column = spread(own, "z", 4).reshape(64, own.shape[1])
    half = spread(column, "y", 4).reshape(256, own.shape[1])
    return half, swap_core(half)


def body(frames_data, starts, lags):
    tok, width = frames_data.shape
    z, y, c, w, x = (lax.axis_index(a) for a in AXES)
    slab = z * 8 + y * 2 + c
    total = tok * 32
    ends = jnp.concatenate([starts[1:], jnp.array([total], dtype=jnp.int32)])
    table = jnp.stack([starts, ends, lags])
    pos = jnp.stack([slab * tok, c, slab * 16, z, y, x]).astype(jnp.int32)
    panel = frames_data[:, :P_SIZE]

    def step(by):
        def target(z, y, c, w, x):
            i = z * 8 + y * 2 + c + by
            return (i // 8, i // 2 % 4, i % 2, 0, 0) if (w, x) == (0, 0) and 0 <= i < 32 else None
        return target

    behind = move(panel[:RIM], step(-1))
    before = move(panel[tok - RIM :], step(1))

    packed = jax.ShapeDtypeStruct((256, P_SIZE + NB), F32)
    mine, theirs = call(
        diag_kernel, [packed, packed], (pos, table, frames_data, before, behind), "diagonal",
        scratch=[pltpu.VMEM((tok + 2 * RIM, P_SIZE), BF16), pltpu.VMEM((tok, 3 * P_SIZE), BF16)],
        flops=3 * 10**9, block={2: (tok, P_SIZE)},
    )
    theirs, *chunks = together(theirs, *(panel[STEP0 + CHUNK * (k - 1) : STEP0 + CHUNK * k] for k in (2, 1, 3)))
    sent = [
        move(v, lambda z, y, c, w, x: (z, y, c, w, k) if (w, x) == (0, 0) else None)
        for k, v in zip((2, 1, 3), chunks)
    ]
    first = jnp.concatenate([before, behind, panel[:FIRST]], axis=0)
    hold = jnp.where(x == 0, first, sent[0] + sent[1] + sent[2])
    over = move(hold, lambda z, y, c, w, x: (z, y, c, 1, x) if w == 0 else None)
    rows16 = diag_rows(diag_half(mine, theirs))
    hold = jnp.where(w == 0, hold, over)
    gathered = [hold] + [
        move(hold, lambda z, y, c, w, x: (z, y, c, w, (x + k) % 4)) for k in (1, 2, 3)
    ]
    over = move(rows16, lambda z, y, c, w, x: (z, y, c, 1, 0) if (w, x) == (0, 0) else None)
    over, *gathered = together(over, *gathered)
    rows16 = jnp.where(w == 0, rows16, over)
    copies = [
        move(rows16, lambda z, y, c, w, x: (z, y, c, w, k) if x == 0 else None) for k in (2, 1, 3)
    ]
    rows16 = jnp.where(x == 0, rows16, copies[0] + copies[1] + copies[2])
    own, other = diag_gather(rows16)
    (part,) = call(
        cov_kernel, [jax.ShapeDtypeStruct((8, 128, 2 * P_SIZE), F32)], (pos, table, frames_data, *gathered), "covariance",
        scratch=[
            pltpu.VMEM((tok + 2 * RIM, P_SIZE), BF16),
            pltpu.VMEM((tok, 3 * P_SIZE), BF16),
            pltpu.SemaphoreType.DMA((4, 3)),
        ],
        flops=5 * 10**9, vmem=20, hbm=(3, 4, 5, 6),
    )
    t = lax.psum_scatter(part.reshape(1024, 2 * P_SIZE), ("y", "c"), scatter_dimension=0, tiled=True)
    rows = [t[:32]] + [
        move(t[32 * k : 32 * k + 32], lambda z, y, c, w, x: ((z + k) % 4, y, c, w, x)) for k in (2, 1, 3)
    ]

    full = jax.ShapeDtypeStruct((P_SIZE, P_SIZE), F32)
    inv, up = call(unpack_kernel, [full, full], (pos, own, other), "factor0", flops=5 * 10**9, vmem=8)
    for o in range(NB, P_SIZE, NB):
        (inv,) = call(functools.partial(inverse_kernel, o), [full], (pos, inv), "factor%d" % o, flops=5 * 10**9, vmem=8)
    (tau,) = call(
        tau_kernel, [jax.ShapeDtypeStruct((16, P_SIZE), F32)], (pos, inv, up), "tau", flops=10**9, vmem=8
    )
    own = jax.ShapeDtypeStruct((1, 32, P_SIZE), F32)
    panel, cross = call(
        whiten_kernel, [own, own], (pos, inv, *rows), "whiten",
        scratch=[pltpu.VMEM((64, P_SIZE), F32)], flops=10**9, vmem=8,
    )
    return panel, cross, tau


def solution(mesh):
    split = Mesh(mesh.devices.reshape(SIZES), AXES)
    frames, feat = ("z", "y", "c"), ("w", "x")
    return jax.shard_map(
        body,
        mesh=split,
        in_specs=(P(frames, feat), P(), P()),
        out_specs=(P(feat, frames, None), P(feat, frames, None), P(frames, None)),
        check_vma=False,
    )
```
